32 devices in a mesh: pool: 8 (over z, core), tensor: 4 (over y, x).
Axes of the slice: x: 2, y: 2, z: 4, core: 2. Of those that a mesh axis runs over, the one named last changes fastest.
Arguments:
- hidden: bfloat16 [4096, 14336], P('pool', 'tensor'), may hold values from -6 to 6
- down_weight: bfloat16 [14336, 8192], P('tensor', 'pool'), may hold values from -0.046875 to 0.046875
- adapter_shrink: bfloat16 [16, 14336, 64], P('pool', 'tensor'), may hold values from -0.046875 to 0.046875
- adapter_expand: bfloat16 [16, 8192, 64], P('pool', 'tensor'), may hold values from -0.75 to 0.75
- block_adapter: int32 [32], P('pool'), may hold values from 0 to 15, as said below
- block_rows: int32 [32], P('pool'), may hold values from 1 to 128, 3072 in all
Outputs:
- projected: bfloat16 [4096, 8192], P(('pool', 'tensor'))
The draws below stay inside these ranges and needn't reach their ends.
Inputs may be any that keep to these rules, and one draw needn't show every extreme that they name: `block_adapter`: within each aligned run of 4 blocks (the rows of one pool index) no two blocks name adapters with the same a // 2. `block_rows`: some block is full.
All inputs are finite; a program needn't handle non-finite values.
Results may differ from the reference program's by a relative error of at most 0.02.
Values may be sent and summed in bfloat16 or wider, within the bound.
No kernel may reach another device: no remote copies, remote signals or barrier semaphores. Data moves between devices by JAX's collectives and lax.ppermute only.
A program may use at most 128 MiB of HBM per device.

```python
import math
import jax
import jax.numpy as jnp
import numpy as np
from jax import lax

D = 8192
FF = 14336
RANK = 64
ADP_DEV = 2
BLOCK = 128
ROWS = 512
ADAPTERS = 16
TOKENS = 4096
BLOCKS = 32
N_TENSOR = 4


def draw_block_adapter(key, part):
    groups = TOKENS // ROWS
    per_group = ROWS // BLOCK
    holders = ADAPTERS // ADP_DEV
    key_heat, key_noise, key_local = jax.random.split(jax.random.fold_in(key, 7), 3)
    heat = jax.random.randint(key_heat, (holders,), 0, 4)
    noise = jax.random.randint(key_noise, (groups, holders), 0, 1024)
    scores = (noise + heat[None, :] * 512) * holders + jnp.arange(holders, dtype=jnp.int32)[None, :]
    picked = lax.top_k(scores, per_group)[1].astype(jnp.int32)
    local = jax.random.randint(key_local, (groups, per_group), 0, ADP_DEV)
    return (picked * ADP_DEV + local).reshape(-1).astype(jnp.int32)


def block_scale(key, shape, shards, least, largest):
    def one(dim, shards_of):
        steps = jax.random.uniform(jax.random.fold_in(jax.random.fold_in(key, 6), dim), (shards_of,), jnp.float32, least / len(shards), largest / len(shards))
        return jnp.repeat(jnp.exp(steps), shape[dim] // shards_of).reshape((-1,) + (1,) * (len(shape) - dim - 1))

    gain = one(*shards[0])
    for cut in shards[1:]:
        gain = gain * one(*cut)
    return gain


def split_up(number_of, total, most, lean):
    portions = [(1 << 20) // math.isqrt(standing ** lean) + 1 for standing in range(2, number_of + 1)]
    surplus, holding = total - most - (number_of - 1), [1] * (number_of - 1)
    while surplus > 0:
        candidates = [i for i in range(number_of - 1) if holding[i] < most]
        pool, remaining = sum([portions[i] for i in candidates]), surplus
        for i in candidates:
            extra = min(most - holding[i], max(1, remaining * portions[i] // pool), surplus)
            holding[i] = holding[i] + extra
            surplus = surplus - extra
    return np.array([most] + holding)


def ragged_sizes(rng, count, total, bound, lean):
    if count == 2:
        one = jax.random.randint(rng, (), max(1, total - bound), min(bound, total - 1) + 1)
        return jnp.stack([one, total - one])
    tallies = jnp.asarray(split_up(count, total, bound, lean), jnp.int32)
    couples = (count - 1) // 2
    giver, sink = tallies[1:1 + 2 * couples:2], tallies[2:2 + 2 * couples:2]
    room = jnp.minimum(giver - 1, bound - sink)
    moved = jax.random.randint(jax.random.fold_in(rng, 1), (couples,), 0, 1 << 20) % (room + 1)
    tallies = tallies.at[1:1 + 2 * couples:2].set(giver - moved).at[2:2 + 2 * couples:2].set(sink + moved)
    return tallies[jax.random.permutation(jax.random.fold_in(rng, 2), count)]


def scatter_about(own_key, extent, scale, most, cuts=(), kind=jnp.bfloat16):
    drawn = scale * jax.random.normal(own_key, extent, jnp.float32)
    if cuts:
        drawn = drawn * block_scale(own_key, extent, cuts, -0.22, 0.18)
    return jnp.clip(drawn, -most, most).astype(kind)


def setup_inputs(seed: int = 0) -> dict:
    splits = jax.random.split(jax.random.key(seed), 7)
    return {
        "hidden": scatter_about(splits[0], (TOKENS, FF), 1.0, 6.0, ((0, 8), (1, 4))),
        "down_weight": scatter_about(splits[1], (FF, D), FF ** -0.5, 0.046875, ((0, 4), (1, 8))),
        "adapter_shrink": scatter_about(splits[2], (ADAPTERS, FF, RANK), FF ** -0.5, 0.046875, ((0, 8), (1, 4))),
        "adapter_expand": scatter_about(splits[3], (ADAPTERS, D, RANK), RANK ** -0.5, 0.75, ((0, 8), (1, 4))),
        "block_adapter": draw_block_adapter(jax.random.fold_in(splits[6], 71), 0),
        "block_rows": ragged_sizes(splits[5], BLOCKS, BLOCKS * BLOCK * 3 // 4, BLOCK, 1).astype(jnp.int32),
    }


adapter_scale_factor = 0.5


def reference(hidden, down_weight, adapter_shrink, adapter_expand, block_adapter, block_rows):
    def one_block(item):
        block_vals, ident = item
        ident = ident.astype(jnp.int32)
        shrink_w = lax.dynamic_index_in_dim(adapter_shrink, ident, 0, keepdims=False)
        expand_w = lax.dynamic_index_in_dim(adapter_expand, ident, 0, keepdims=False)
        shrink = jnp.dot(block_vals, shrink_w, preferred_element_type=jnp.float32).astype(jnp.bfloat16)
        enlarged_rows = jnp.dot(shrink, expand_w.T, preferred_element_type=jnp.float32)
        return (adapter_scale_factor * enlarged_rows).astype(jnp.bfloat16)

    delta = lax.map(one_block, (hidden.reshape(BLOCKS, BLOCK, FF), block_adapter)).reshape(TOKENS, D)
    width = FF // N_TENSOR

    def add_term(step, total):
        start = (step * width).astype(jnp.int32)
        columns = lax.dynamic_slice_in_dim(hidden, start, width, 1)
        weight_rows = lax.dynamic_slice_in_dim(down_weight, start, width, 0)
        term = jnp.dot(columns, weight_rows, preferred_element_type=jnp.float32)
        rounded_length = lax.optimization_barrier(term.astype(jnp.bfloat16))
        return total + rounded_length.astype(jnp.float32)

    total = lax.fori_loop(0, N_TENSOR, add_term, jnp.zeros((TOKENS, D), jnp.float32))
    total = total + delta.astype(jnp.float32)
    valid = (jnp.arange(TOKENS, dtype=jnp.int32) % BLOCK) < jnp.repeat(block_rows, BLOCK)
    return (total * valid[:, None].astype(jnp.float32)).astype(jnp.bfloat16)
```

```python
import jax
import jax.numpy as jnp
from jax import lax
from jax.sharding import PartitionSpec as P

BLOCK = 128
SCALE = 0.5


def general(hidden, down_weight, adapter_shrink, adapter_expand, block_adapter, block_rows):
    input_rows, feat = hidden.shape
    block_count = block_adapter.shape[0]
    column_span = adapter_expand.shape[1]
    tensor_pos = lax.axis_index("tensor")
    tensor_count = lax.axis_size("tensor")
    own_rows = input_rows // tensor_count
    blocks = hidden.reshape(block_count, BLOCK, feat)
    partial_value = jnp.dot(
        hidden,
        lax.all_gather(down_weight, "pool", axis=1, tiled=True),
        preferred_element_type=jnp.float32,
    )
    total = lax.psum_scatter(
        partial_value.astype(jnp.bfloat16), "tensor", scatter_dimension=0, tiled=True
    ).astype(jnp.float32)
    shrink_piece = lax.all_gather(adapter_shrink, "pool", axis=0, tiled=True)
    expand_piece = lax.all_gather(adapter_expand, "pool", axis=0, tiled=True)
    idents = jnp.arange(shrink_piece.shape[0], dtype=jnp.int32)
    pick = (block_adapter[:, None] == idents[None, :]).astype(jnp.bfloat16)
    first = jnp.einsum("bk,kfr->bfr", pick, shrink_piece, preferred_element_type=jnp.float32)
    second = jnp.einsum("bk,kcr->bcr", pick, expand_piece, preferred_element_type=jnp.float32)
    shrink = jnp.einsum(
        "bnf,bfr->bnr", blocks, first.astype(jnp.bfloat16), preferred_element_type=jnp.float32
    )
    summed_shrink = lax.psum(shrink.astype(jnp.bfloat16), "tensor")
    enlarged_rows = jnp.einsum(
        "bnr,bcr->bnc",
        summed_shrink,
        second.astype(jnp.bfloat16),
        preferred_element_type=jnp.float32,
    )
    adapter_delta_columns = (
        (SCALE * enlarged_rows).astype(jnp.bfloat16).reshape(input_rows, column_span)
    )
    delta_mine = lax.all_to_all(
        adapter_delta_columns, "tensor", split_axis=0, concat_axis=1, tiled=True
    )
    total = total + delta_mine.astype(jnp.float32)
    row_ids = tensor_pos * own_rows + jnp.arange(own_rows, dtype=jnp.int32)
    owning = (row_ids // BLOCK)[:, None] == jnp.arange(block_count, dtype=jnp.int32)[None, :]
    lengths = jnp.sum(jnp.where(owning, block_rows[None, :], 0), axis=1)
    valid = (row_ids % BLOCK < lengths).astype(jnp.float32)
    return (total * valid[:, None]).astype(jnp.bfloat16)


def dot(a, b):
    return jnp.dot(a, b, preferred_element_type=jnp.float32)


def on_line(pairs):
    return [(2 * a + c, 2 * b + c) for a, b in pairs for c in range(2)]


XOR = {s: on_line([(z, z ^ s) for z in range(4)]) for s in (1, 2, 3)}
MIDDLE = on_line([(1, 2), (2, 1)])
OUTWARD = on_line([(1, 0), (2, 3)])
SIBLING = [(p, p ^ 1) for p in range(8)]


def send(x, pairs):
    return lax.ppermute(x, "pool", pairs)


def line_of_four(hidden, down_weight, adapter_shrink, adapter_expand, block_adapter, block_rows):
    rows, feat = hidden.shape
    span = down_weight.shape[1]
    wide = 2 * span
    adp, _, rank = adapter_shrink.shape
    p = lax.axis_index("pool")
    t = lax.axis_index("tensor")
    tensor_count = lax.axis_size("tensor")
    z, c = p // 2, p % 2
    outer = (z == 0) | (z == 3)

    h1 = send(hidden, XOR[1])
    mid1 = send(hidden, MIDDLE)
    out2 = send(mid1, OUTWARD)
    mid2 = send(h1, MIDDLE)
    out3 = send(mid2, OUTWARD)
    slots = [hidden, h1, jnp.where(outer, out2, mid2), jnp.where(outer, out3, mid1)]

    w_other = send(down_weight, SIBLING)
    weight = jnp.concatenate(
        [jnp.where(c == 0, down_weight, w_other), jnp.where(c == 0, w_other, down_weight)], axis=1
    )
    a_other = send(adapter_shrink, SIBLING)
    shrink_w = jnp.concatenate(
        [jnp.where(c == 0, adapter_shrink, a_other), jnp.where(c == 0, a_other, adapter_shrink)], axis=0
    )
    held = 2 * adp
    shrink_w = shrink_w.transpose(1, 0, 2).reshape(feat, held * rank)
    names = lax.all_gather(block_adapter, "pool", axis=0)

    whole = lax.all_gather(adapter_expand, "tensor", axis=1, tiled=True)
    share = wide // tensor_count

    def part(s):
        return lax.dynamic_slice_in_dim(whole, (z ^ s) * wide + t * share, share, 1)

    parts = jnp.stack([part(0)] + [send(part(s), XOR[s]) for s in (1, 2, 3)])
    gathered = lax.all_gather(parts, "tensor", axis=2, tiled=True)
    g_other = send(gathered, SIBLING)

    partial = []
    for s, block in enumerate(slots):
        cols = dot(block, weight)
        low = dot(block, shrink_w).reshape(-1, BLOCK, held, rank)
        wants = lax.dynamic_index_in_dim(names, 2 * (z ^ s) + c, 0, keepdims=False)
        pick = wants[:, None] == z * held + jnp.arange(held, dtype=jnp.int32)[None, :]
        low = jnp.sum(jnp.where(pick[:, None, :, None], low, 0.0), axis=2).reshape(rows, rank)
        both = jnp.concatenate(
            [cols.astype(jnp.bfloat16), low.astype(jnp.bfloat16), jnp.zeros((rows, 128 - rank), jnp.bfloat16)], axis=1
        )
        partial.append(lax.psum_scatter(both, "tensor", scatter_dimension=0, tiled=True))

    own = [x[:, wide : wide + rank] for x in partial]
    summed = jnp.stack(own).astype(jnp.float32)
    for d in (1, 2, 3):
        summed = summed + send(jnp.stack([own[s ^ d] for s in range(4)]), XOR[d]).astype(jnp.float32)
    summed = summed.astype(jnp.bfloat16)

    final = []
    for s in range(4):
        want = lax.dynamic_index_in_dim(
            lax.dynamic_index_in_dim(names, 2 * (z ^ s) + c, 0, keepdims=False), t, 0, keepdims=False
        )
        source = (want // held) ^ z
        core = (want // adp) % 2
        local = want % adp
        mine = gathered[source, local]
        theirs = g_other[source, local]
        expand = jnp.where(core == c, mine, theirs)
        delta = SCALE * lax.dot_general(
            summed[s], expand, (((1,), (1,)), ((), ())), preferred_element_type=jnp.float32
        )
        total = (partial[s][:, :wide].astype(jnp.float32) + delta).astype(jnp.bfloat16)
        final.append(total if s == 0 else send(total, XOR[s]))
    final = jnp.stack(final)
    count = lax.dynamic_index_in_dim(block_rows, t, 0, keepdims=False)
    valid = jnp.arange(BLOCK, dtype=jnp.int32) < count
    columns = [lax.dynamic_index_in_dim(final, z ^ j, 0, keepdims=False) for j in range(4)]
    return jnp.where(valid[:, None], jnp.concatenate(columns, axis=1), jnp.zeros((), jnp.bfloat16))


def solution(mesh):
    in_specs = (
        P("pool", "tensor"),
        P("tensor", "pool"),
        P("pool", "tensor", None),
        P("pool", "tensor", None),
        P("pool"),
        P("pool"),
    )
    out_specs = P(("pool", "tensor"), None)
    body = line_of_four if dict(mesh.shape) == {"pool": 8, "tensor": 4} else general
    return jax.shard_map(body, mesh=mesh, in_specs=in_specs, out_specs=out_specs, check_vma=False)
```

```python
import functools

import jax
import jax.numpy as jnp
from jax import lax
from jax.experimental import pallas as pl
from jax.experimental.pallas import tpu as pltpu
from jax.sharding import PartitionSpec as P

BLOCK = 128
SCALE = 0.5


def general(hidden, down_weight, adapter_shrink, adapter_expand, block_adapter, block_rows):
    input_rows, feat = hidden.shape
    block_count = block_adapter.shape[0]
    column_span = adapter_expand.shape[1]
    tensor_pos = lax.axis_index("tensor")
    tensor_count = lax.axis_size("tensor")
    own_rows = input_rows // tensor_count
    blocks = hidden.reshape(block_count, BLOCK, feat)
    partial_value = jnp.dot(
        hidden,
        lax.all_gather(down_weight, "pool", axis=1, tiled=True),
        preferred_element_type=jnp.float32,
    )
    total = lax.psum_scatter(
        partial_value.astype(jnp.bfloat16), "tensor", scatter_dimension=0, tiled=True
    ).astype(jnp.float32)
    shrink_piece = lax.all_gather(adapter_shrink, "pool", axis=0, tiled=True)
    expand_piece = lax.all_gather(adapter_expand, "pool", axis=0, tiled=True)
    idents = jnp.arange(shrink_piece.shape[0], dtype=jnp.int32)
    pick = (block_adapter[:, None] == idents[None, :]).astype(jnp.bfloat16)
    first = jnp.einsum("bk,kfr->bfr", pick, shrink_piece, preferred_element_type=jnp.float32)
    second = jnp.einsum("bk,kcr->bcr", pick, expand_piece, preferred_element_type=jnp.float32)
    shrink = jnp.einsum(
        "bnf,bfr->bnr", blocks, first.astype(jnp.bfloat16), preferred_element_type=jnp.float32
    )
    summed_shrink = lax.psum(shrink.astype(jnp.bfloat16), "tensor")
    enlarged_rows = jnp.einsum(
        "bnr,bcr->bnc",
        summed_shrink,
        second.astype(jnp.bfloat16),
        preferred_element_type=jnp.float32,
    )
    adapter_delta_columns = (
        (SCALE * enlarged_rows).astype(jnp.bfloat16).reshape(input_rows, column_span)
    )
    delta_mine = lax.all_to_all(
        adapter_delta_columns, "tensor", split_axis=0, concat_axis=1, tiled=True
    )
    total = total + delta_mine.astype(jnp.float32)
    row_ids = tensor_pos * own_rows + jnp.arange(own_rows, dtype=jnp.int32)
    owning = (row_ids // BLOCK)[:, None] == jnp.arange(block_count, dtype=jnp.int32)[None, :]
    lengths = jnp.sum(jnp.where(owning, block_rows[None, :], 0), axis=1)
    valid = (row_ids % BLOCK < lengths).astype(jnp.float32)
    return (total * valid[:, None]).astype(jnp.bfloat16)


def dot(a, b):
    return jnp.dot(a, b, preferred_element_type=jnp.float32)


def on_line(pairs):
    return [(2 * a + c, 2 * b + c) for a, b in pairs for c in range(2)]


XOR = {s: on_line([(z, z ^ s) for z in range(4)]) for s in (1, 2, 3)}
MIDDLE = on_line([(1, 2), (2, 1)])
OUTWARD = on_line([(1, 0), (2, 3)])
INWARD = on_line([(0, 1), (3, 2)])
ACROSS = on_line([(1, 3), (2, 0)])
SIBLING = [(p, p ^ 1) for p in range(8)]

NEAR = 2048
TILE = 256
PIECE = 64
INNER, CORE, ZPOS, NAMES = 0, 1, 2, 3


def send(x, pairs):
    return lax.ppermute(x, "pool", pairs)


def params(limit):
    return pltpu.CompilerParams(vmem_limit_bytes=limit * 1024 * 1024)


CHEAP = pl.CostEstimate(flops=1000, bytes_accessed=1000, transcendentals=0)


def narrow(a, b):
    return dot(a, b).astype(jnp.bfloat16)


def shrink_sums(meta, slot, x, adapters, out, wide):
    rows = x.shape[0] // 4
    z, c = meta[ZPOS], meta[CORE]
    products = [
        lax.dot_general(x[...], a[...], (((1,), (1,)), ((), ())), preferred_element_type=jnp.float32)
        for a in adapters
    ]
    for b in range(4):
        name = meta[NAMES + 4 * slot + b]
        chip = name >> 2
        place = jnp.where(chip == z, 0, 4) + ((((name >> 1) & 1) ^ c) << 1) + (name & 1)
        here = (meta[INNER] == 1) & ((chip == z) | (chip == (z ^ 1)))
        place = jnp.where(here, place, -1)
        total = jnp.zeros((rows, 64), jnp.float32)
        for k in range(8):
            part = products[k // 2][b * rows : (b + 1) * rows, (k % 2) * 64 : (k % 2) * 64 + 64]
            total = total + jnp.where(place == k, part, 0.0)
        padded = jnp.concatenate([total, jnp.zeros_like(total)], axis=1)
        out[b * rows : (b + 1) * rows, wide : wide + 128] = padded.astype(jnp.bfloat16)


def columns_kernel(slot, steps, shared, has_outer, meta, x, *refs):
    refs = list(refs)
    x_outer = refs.pop(0) if has_outer else None
    w_own, w_other, *adapters, out = refs
    n = pl.program_id(0)
    wide = steps * TILE
    inner = meta[INNER] == 1
    for half, w in ((0, w_own), (1, w_other)):
        mine = (n // (steps // 2)) == half
        place = pl.ds(pl.multiple_of(n * TILE, TILE), TILE)

        @pl.when(mine if shared else mine & inner)
        def _(w=w, place=place):
            out[:, place] = narrow(x[...], w[...])

        if has_outer:

            @pl.when(mine & jnp.logical_not(inner))
            def _(w=w, place=place):
                out[:, place] = narrow(x_outer[...], w[:NEAR, :])

    @pl.when(n == steps)
    def _():
        shrink_sums(meta, slot, x, adapters, out, wide)


def columns(meta, slot, x, x_outer, w_own, w_other, adapters, shared):
    rows, feat = x.shape
    span = w_own.shape[1]
    half = span // TILE
    steps = 2 * half
    whole = lambda shape: pl.BlockSpec(shape, lambda n, m: (0, 0))
    in_specs = [whole((rows, feat))]
    args = [x]
    if x_outer is not None:
        in_specs.append(whole(x_outer.shape))
        args.append(x_outer)
    in_specs.append(pl.BlockSpec((feat, TILE), lambda n, m: (0, jnp.minimum(n, half - 1))))
    in_specs.append(pl.BlockSpec((feat, TILE), lambda n, m: (0, jnp.clip(n - half, 0, half - 1))))
    in_specs += [whole(a.shape) for a in adapters]
    return pl.pallas_call(
        functools.partial(columns_kernel, slot, steps, shared, x_outer is not None),
        grid_spec=pltpu.PrefetchScalarGridSpec(
            num_scalar_prefetch=1,
            grid=(steps + 1,),
            in_specs=in_specs,
            out_specs=whole((rows, 2 * span + 128)),
        ),
        out_shape=jax.ShapeDtypeStruct((rows, 2 * span + 128), jnp.bfloat16),
        compiler_params=params(48),
        cost_estimate=CHEAP,
    )(meta, *args, w_own, w_other, *adapters)


def remainder_kernel(steps, has_outer, meta, x, *refs):
    refs = list(refs)
    x_outer = refs.pop(0) if has_outer else None
    v_own, v_other = refs[:2]
    w_own, w_other = refs[2:4] if has_outer else (None, None)
    out = refs[-1]
    n = pl.program_id(0)
    inner = meta[INNER] == 1
    for half, v, w in ((0, v_own, w_own), (1, v_other, w_other)):
        mine = (n // (steps // 2)) == half
        place = pl.ds(pl.multiple_of(n * TILE, TILE), TILE)

        @pl.when(mine & inner)
        def _(v=v, place=place):
            out[:, place] = narrow(x[:, NEAR:], v[...])

        if has_outer:

            @pl.when(mine & jnp.logical_not(inner))
            def _(w=w, place=place):
                out[:, place] = narrow(x_outer[...], w[...])


def remainder(meta, x, x_outer, v_own, v_other, w_own, w_other):
    rows, feat = x.shape
    rest, span = v_own.shape
    half = span // TILE
    steps = 2 * half
    whole = lambda shape: pl.BlockSpec(shape, lambda n, m: (0, 0))
    first = lambda n: jnp.minimum(n, half - 1)
    second = lambda n: jnp.clip(n - half, 0, half - 1)
    in_specs = [whole((rows, feat))]
    args = [x]
    has_outer = x_outer is not None
    if has_outer:
        in_specs.append(whole(x_outer.shape))
        args.append(x_outer)
    in_specs.append(pl.BlockSpec((rest, TILE), lambda n, m: (0, first(n) * m[INNER])))
    in_specs.append(pl.BlockSpec((rest, TILE), lambda n, m: (0, second(n) * m[INNER])))
    args += [v_own, v_other]
    if has_outer:
        in_specs.append(pl.BlockSpec((NEAR, TILE), lambda n, m: (0, first(n) * (1 - m[INNER]))))
        in_specs.append(pl.BlockSpec((NEAR, TILE), lambda n, m: (0, second(n) * (1 - m[INNER]))))
        args += [w_own, w_other]
    return pl.pallas_call(
        functools.partial(remainder_kernel, steps, has_outer),
        grid_spec=pltpu.PrefetchScalarGridSpec(
            num_scalar_prefetch=1,
            grid=(steps,),
            in_specs=in_specs,
            out_specs=whole((rows, 2 * span)),
        ),
        out_shape=jax.ShapeDtypeStruct((rows, 2 * span), jnp.bfloat16),
        compiler_params=params(48),
        cost_estimate=CHEAP,
    )(meta, *args)


def finish_kernel(role, pieces, has_delta, has_more, meta, *refs):
    refs = list(refs)
    parts = [refs.pop(0) for _ in range(pieces)]
    if has_delta:
        low, expand = refs.pop(0), refs.pop(0)
    more = refs.pop(0) if has_more else None
    out = refs.pop(0)

    def run():
        for k, part in enumerate(parts):
            rows = part.shape[0] // 4
            total = part[0:rows, :].astype(jnp.float32)
            for b in range(1, 4):
                total = total + part[b * rows : (b + 1) * rows, :].astype(jnp.float32)
            at = slice(k * rows, (k + 1) * rows)
            if has_delta:
                share = expand.shape[-1]
                delta = [dot(low[at, :], expand[i, 0]) for i in range(expand.shape[0])]
                total = total + SCALE * jnp.concatenate(delta, axis=1)
            if has_more:
                total = total + more[at, :].astype(jnp.float32)
            out[at, :] = total.astype(jnp.bfloat16)

    if role is None:
        run()
    else:
        pl.when(meta[INNER] == role)(run)


def finish(meta, role, parts, low=None, expand=None, slot=0, more=None):
    rows = sum(part.shape[0] // 4 for part in parts)
    wide = 2048
    span = wide // 2
    in_specs = [pl.BlockSpec((part.shape[0], span), lambda h, m: (0, h)) for part in parts]
    args = list(parts)
    if low is not None:
        share = expand.shape[-1]
        in_specs.append(pl.BlockSpec(low.shape, lambda h, m: (0, 0)))
        in_specs.append(
            pl.BlockSpec((span // share, 1, low.shape[1], share), lambda h, m: (h ^ m[CORE], slot, 0, 0))
        )
        args += [low, expand]
    if more is not None:
        in_specs.append(pl.BlockSpec((rows, span), lambda h, m: (0, h)))
        args.append(more)
    return pl.pallas_call(
        functools.partial(finish_kernel, role, len(parts), low is not None, more is not None),
        grid_spec=pltpu.PrefetchScalarGridSpec(
            num_scalar_prefetch=1,
            grid=(2,),
            in_specs=in_specs,
            out_specs=pl.BlockSpec((rows, span), lambda h, m: (0, h)),
        ),
        out_shape=jax.ShapeDtypeStruct((rows, wide), jnp.bfloat16),
        compiler_params=params(32),
        cost_estimate=CHEAP,
    )(meta, *args)


def assemble_kernel(span, pieces, meta, count, own, partner, *refs):
    out = refs[-1]
    refs = list(refs[:-1])
    groups = []
    for size in pieces:
        groups.append([refs.pop(0) for _ in range(size)])
    z, c, inner = meta[ZPOS], meta[CORE], meta[INNER] == 1
    rows = own.shape[0]
    valid = lax.broadcasted_iota(jnp.int32, (rows, 1), 0) < count[0]

    def put(j, sources):
        for h in range(2):
            at = pl.ds(pl.multiple_of((2 * j + h) * span, span), span)
            part = pl.ds(pl.multiple_of((h ^ c) * span, span), span)
            first = 0
            for source in sources:
                size = source.shape[0]
                keep = valid[first : first + size]
                out[first : first + size, at] = jnp.where(keep, source[:, part], jnp.zeros((), jnp.bfloat16))
                first += size

    put(z, [own])
    put(z ^ 1, [partner])

    @pl.when(inner)
    def _():
        put(z ^ 3, groups[0])
        put(z ^ 2, groups[1])

    @pl.when(jnp.logical_not(inner))
    def _():
        put(z ^ 2, groups[2])
        put(z ^ 3, groups[3])


def assemble(meta, count, own, partner, groups):
    rows, wide = own.shape
    args = [own, partner] + [x for group in groups for x in group]
    return pl.pallas_call(
        functools.partial(assemble_kernel, wide // 2, [len(g) for g in groups]),
        grid_spec=pltpu.PrefetchScalarGridSpec(
            num_scalar_prefetch=2,
            grid=(1,),
            in_specs=[pl.BlockSpec(a.shape, lambda n, m, k: (0, 0)) for a in args],
            out_specs=pl.BlockSpec((rows, 4 * wide), lambda n, m, k: (0, 0)),
        ),
        out_shape=jax.ShapeDtypeStruct((rows, 4 * wide), jnp.bfloat16),
        compiler_params=params(32),
        cost_estimate=CHEAP,
    )(meta, count, *args)


def line_of_four(hidden, down_weight, adapter_shrink, adapter_expand, block_adapter, block_rows):
    rows, feat = hidden.shape
    span = down_weight.shape[1]
    wide = 2 * span
    adp, _, rank = adapter_shrink.shape
    p = lax.axis_index("pool")
    t = lax.axis_index("tensor")
    tensors = lax.axis_size("tensor")
    z, c = p // 2, p % 2
    outer = (z == 0) | (z == 3)

    def exchange(x):
        return lax.all_to_all(x, "tensor", split_axis=0, concat_axis=0, tiled=True)

    names = [block_adapter] + [send(block_adapter, XOR[s]) for s in (1, 2, 3)]
    middle = jnp.where(outer, names[2], names[3])
    far = jnp.where(outer, names[3], names[2])
    names = jnp.stack([names[0], names[1], middle, far])
    role = jnp.where(outer, 0, 1)
    meta = jnp.concatenate([jnp.stack([role, c, z]).astype(jnp.int32), names.reshape(-1)])

    shrink_w = adapter_shrink.transpose(0, 2, 1).reshape(adp * rank, feat)
    shrink_o = send(shrink_w, INWARD)
    shrink_s = send(shrink_w, SIBLING)
    shrink_os = send(shrink_o, SIBLING)
    adapters = [shrink_w, shrink_s, shrink_o, shrink_os]
    w_other = send(down_weight, SIBLING)

    split = hidden.reshape(rows // BLOCK, 2, PIECE, feat)
    h = [split[:, k].reshape(rows // 2, feat) for k in range(2)]
    partner = [send(h[k], XOR[1]) for k in range(2)]
    mid = [send(h[k], MIDDLE) for k in range(2)]
    mid_far = [send(partner[k], MIDDLE) for k in range(2)]
    out_mid = [send(mid[k][:, :NEAR], OUTWARD) for k in range(2)]
    out_far = [send(mid_far[k][:, :NEAR], OUTWARD) for k in range(2)]

    v_own = send(down_weight[NEAR:], INWARD)
    v_other = send(v_own, SIBLING)

    expand = adapter_expand.transpose(0, 2, 1)
    share = wide // tensors
    shares = expand.reshape(adp, rank, tensors, share).transpose(2, 0, 1, 3)
    shares = exchange(shares)
    held = [lax.dynamic_index_in_dim(shares, z, 0, keepdims=False)]
    for s in (1, 2, 3):
        held.append(send(lax.dynamic_index_in_dim(shares, z ^ s, 0, keepdims=False), XOR[s]))
    held = jnp.stack(held)
    held_s = send(held, SIBLING)
    held = jnp.stack([jnp.where(c == 0, held, held_s), jnp.where(c == 0, held_s, held)], axis=1)
    held = held.reshape(4 * 2 * adp, rank, share)
    wanted = (names ^ (z * 2 * adp)).T
    picked = jnp.take(held, wanted.reshape(-1), axis=0).reshape(tensors, 4, rank, share)
    expand_rows = exchange(picked)

    def low_of(parts):
        return jnp.concatenate(
            [
                jnp.sum(
                    x[:, wide : wide + rank].reshape(4, -1, rank).astype(jnp.float32), axis=0
                ).astype(jnp.bfloat16)
                for x in parts
            ],
            axis=0,
        )

    r_own = [exchange(columns(meta, 0, hidden, None, down_weight, w_other, adapters, True))]
    r_partner = [
        exchange(columns(meta, 1, partner[k], None, down_weight, w_other, adapters, True)) for k in range(2)
    ]
    r_mid = [exchange(columns(meta, 2, mid[k], None, down_weight, w_other, adapters, False)) for k in range(2)]

    early = jnp.stack([low_of(r_own), low_of(r_mid)])
    early = (early.astype(jnp.float32) + send(early[::-1], MIDDLE).astype(jnp.float32)).astype(jnp.bfloat16)
    early_out = send(early, OUTWARD)

    r_far = [
        exchange(columns(meta, 3, mid_far[k], out_mid[k], down_weight, w_other, adapters, False)) for k in range(2)
    ]
    late = jnp.stack([low_of(r_partner), low_of(r_far)])
    late = (late.astype(jnp.float32) + send(late[::-1], MIDDLE).astype(jnp.float32)).astype(jnp.bfloat16)
    late_out = send(late, OUTWARD)

    low_own = jnp.where(outer, late_out[0], early[0])
    low_partner = jnp.where(outer, early_out[0], late[0])

    x_mid_o = finish(meta, 0, r_far, early_out[1], expand_rows, 2)
    to_inner = send(x_mid_o, INWARD)

    r_rest_m = [
        exchange(remainder(meta, mid[k], out_far[k], v_own, v_other, down_weight, w_other)) for k in range(2)
    ]
    r_rest_f = [exchange(remainder(meta, mid_far[k], None, v_own, v_other, None, None)) for k in range(2)]

    x_own = finish(meta, None, r_own, low_own, expand_rows, 0)
    x_partner = finish(meta, None, r_partner, low_partner, expand_rows, 1)
    x_mid = finish(meta, 1, r_mid, early[1], expand_rows, 2)
    x_far = finish(meta, 1, r_far, late[1], expand_rows, 3)
    x_rest_m = finish(meta, 1, r_rest_m, more=to_inner)
    x_far_o = [
        finish(meta, 0, [r_rest_m[k]], late_out[1][k * PIECE : (k + 1) * PIECE], expand_rows, 3) for k in range(2)
    ]
    to_inner_far = [send(x, INWARD) for x in x_far_o]
    x_rest_f = [finish(meta, 1, [r_rest_f[k]], more=to_inner_far[k]) for k in range(2)]

    home_partner = send(x_partner, XOR[1])
    home_mid = send(x_mid, MIDDLE)
    home_rest_m = send(x_rest_m, MIDDLE)
    home_far = send(x_far, ACROSS)
    home_rest_f = [send(x, ACROSS) for x in x_rest_f]
    count = lax.dynamic_slice_in_dim(block_rows, t, 1, 0)
    return assemble(
        meta, count, x_own, home_partner, [[home_mid], [home_rest_m], [home_far], home_rest_f]
    )


def solution(mesh):
    in_specs = (
        P("pool", "tensor"),
        P("tensor", "pool"),
        P("pool", "tensor", None),
        P("pool", "tensor", None),
        P("pool"),
        P("pool"),
    )
    out_specs = P(("pool", "tensor"), None)
    body = line_of_four if dict(mesh.shape) == {"pool": 8, "tensor": 4} else general
    return jax.shard_map(body, mesh=mesh, in_specs=in_specs, out_specs=out_specs, check_vma=False)
```

```python
import functools

import jax
import jax.numpy as jnp
from jax import lax
from jax.experimental import pallas as pl
from jax.experimental.pallas import tpu as pltpu
from jax.sharding import PartitionSpec as P

BLOCK = 128
SCALE = 0.5


def general(hidden, down_weight, adapter_shrink, adapter_expand, block_adapter, block_rows):
    input_rows, feat = hidden.shape
    block_count = block_adapter.shape[0]
    column_span = adapter_expand.shape[1]
    tensor_pos = lax.axis_index("tensor")
    tensor_count = lax.axis_size("tensor")
    own_rows = input_rows // tensor_count
    blocks = hidden.reshape(block_count, BLOCK, feat)
    partial_value = jnp.dot(
        hidden,
        lax.all_gather(down_weight, "pool", axis=1, tiled=True),
        preferred_element_type=jnp.float32,
    )
    total = lax.psum_scatter(
        partial_value.astype(jnp.bfloat16), "tensor", scatter_dimension=0, tiled=True
    ).astype(jnp.float32)
    shrink_piece = lax.all_gather(adapter_shrink, "pool", axis=0, tiled=True)
    expand_piece = lax.all_gather(adapter_expand, "pool", axis=0, tiled=True)
    idents = jnp.arange(shrink_piece.shape[0], dtype=jnp.int32)
    pick = (block_adapter[:, None] == idents[None, :]).astype(jnp.bfloat16)
    first = jnp.einsum("bk,kfr->bfr", pick, shrink_piece, preferred_element_type=jnp.float32)
    second = jnp.einsum("bk,kcr->bcr", pick, expand_piece, preferred_element_type=jnp.float32)
    shrink = jnp.einsum(
        "bnf,bfr->bnr", blocks, first.astype(jnp.bfloat16), preferred_element_type=jnp.float32
    )
    summed_shrink = lax.psum(shrink.astype(jnp.bfloat16), "tensor")
    enlarged_rows = jnp.einsum(
        "bnr,bcr->bnc",
        summed_shrink,
        second.astype(jnp.bfloat16),
        preferred_element_type=jnp.float32,
    )
    adapter_delta_columns = (
        (SCALE * enlarged_rows).astype(jnp.bfloat16).reshape(input_rows, column_span)
    )
    delta_mine = lax.all_to_all(
        adapter_delta_columns, "tensor", split_axis=0, concat_axis=1, tiled=True
    )
    total = total + delta_mine.astype(jnp.float32)
    row_ids = tensor_pos * own_rows + jnp.arange(own_rows, dtype=jnp.int32)
    owning = (row_ids // BLOCK)[:, None] == jnp.arange(block_count, dtype=jnp.int32)[None, :]
    lengths = jnp.sum(jnp.where(owning, block_rows[None, :], 0), axis=1)
    valid = (row_ids % BLOCK < lengths).astype(jnp.float32)
    return (total * valid[:, None]).astype(jnp.bfloat16)


def dot(a, b):
    return jnp.dot(a, b, preferred_element_type=jnp.float32)


def on_line(pairs):
    return [(2 * a + c, 2 * b + c) for a, b in pairs for c in range(2)]


XOR = {s: on_line([(z, z ^ s) for z in range(4)]) for s in (1, 2, 3)}
MIDDLE = on_line([(1, 2), (2, 1)])
OUTWARD = on_line([(1, 0), (2, 3)])
INWARD = on_line([(0, 1), (3, 2)])
ACROSS = on_line([(1, 3), (2, 0)])
SIBLING = [(p, p ^ 1) for p in range(8)]

NEAR = 2048
TILE = 512
NEAR_TILES = NEAR // TILE
PIECE = 64
WIDE = 2048
INNER, CORE, ZPOS, NAMES = 0, 1, 2, 3
CHEAP = pl.CostEstimate(flops=1000, bytes_accessed=1000, transcendentals=0)


def send(x, pairs):
    return lax.ppermute(x, "pool", pairs)


def after(events, *xs):
    tied = lax.optimization_barrier((tuple(events), xs))
    return tied[1] if len(xs) > 1 else tied[1][0]


def params(limit):
    return pltpu.CompilerParams(vmem_limit_bytes=limit * 1024 * 1024)


class Rows:
    def __init__(self, parts, role, at, weights):
        self.parts, self.role, self.at, self.weights = parts, role, at, weights
        self.rows = parts[0].shape[0]
        self.tiles = [part.shape[1] // TILE for part in parts]


def products_kernel(jobs, steps, weights, tail, meta, *refs):
    refs = list(refs)
    xs = [[refs.pop(0) for _ in job.parts] for job in jobs]
    ws = [(refs.pop(0), refs.pop(0)) for _ in range(weights)]
    out, acc = refs
    k = pl.program_id(0)
    first = {}
    top = {None: 0, 0: 0, 1: 0}
    for i, job in enumerate(jobs):
        if job.role is None:
            first[i] = top[None]
            top = {role: top[role] + job.rows for role in top}
        else:
            first[i] = top[job.role]
            top[job.role] += job.rows
    for i, job in enumerate(jobs):
        base = 0
        mine = slice(first[i], first[i] + job.rows)
        role = True if job.role is None else meta[INNER] == job.role
        total = sum(job.tiles)
        own, other = ws[job.weights]
        for x, tiles in zip(xs[i], job.tiles):

            def step(x=x, mine=mine, own=own, other=other, begin=base == 0):
                for h, w in ((0, own), (1, other)):
                    for n in range(0, WIDE // 2, 512):
                        at = slice(h * (WIDE // 2) + n, h * (WIDE // 2) + n + 512)
                        value = dot(x[...], w[:, n : n + 512])
                        if begin:
                            value = value + jnp.where(k == 0, 0.0, acc[mine, at])
                        else:
                            value = value + acc[mine, at]
                        acc[mine, at] = value

            pl.when(role & (k >= base) & (k < base + tiles))(step)
            base += tiles

        def store(job=job, start=first[i]):
            count = job.rows // 4
            for b in range(4):
                out[b, job.at : job.at + count, :] = acc[start + b * count : start + (b + 1) * count, :].astype(
                    jnp.bfloat16
                )

        pl.when(role & (k == total - 1))(store)


def products(meta, jobs, weights, rows, skip=0, follow=()):
    steps = max(sum(job.tiles) for job in jobs) - skip
    in_specs, args = [], []
    if follow:
        jobs[0].parts[0] = after(follow, jobs[0].parts[0])
    if skip:
        for job in jobs:
            job.tiles = [job.tiles[0] - skip]
    for job in jobs:
        base = 0
        for part, tiles in zip(job.parts, job.tiles):
            low, role = base, job.role

            def index(k, m, low=low, tiles=tiles, role=role):
                at = jnp.clip(k - low, 0, tiles - 1)
                if role is not None:
                    at = at * (m[INNER] if role == 1 else 1 - m[INNER])
                return (0, at + skip)

            in_specs.append(pl.BlockSpec((part.shape[0], TILE), index))
            args.append(part)
            base += tiles
    for i, pair in enumerate(weights):
        users = [job for job in jobs if job.weights == i]
        roles = {job.role for job in users}
        role = roles.pop() if len(roles) == 1 else None
        tiles = max(sum(job.tiles) for job in users)

        def index(k, m, tiles=tiles, role=role):
            at = jnp.minimum(k, tiles - 1)
            if role is not None:
                at = at * (m[INNER] if role == 1 else 1 - m[INNER])
            return (at, 0)

        for w in pair:
            in_specs.append(pl.BlockSpec((TILE, w.shape[1]), index))
            args.append(w)
    both = sum(job.rows for job in jobs if job.role is None)
    height = both + max(sum(job.rows for job in jobs if job.role == r) for r in (0, 1))
    return pl.pallas_call(
        functools.partial(products_kernel, jobs, steps, len(weights), None),
        grid_spec=pltpu.PrefetchScalarGridSpec(
            num_scalar_prefetch=1,
            grid=(steps,),
            in_specs=in_specs,
            out_specs=pl.BlockSpec((4, rows, WIDE), lambda k, m: (0, 0, 0)),
            scratch_shapes=[pltpu.VMEM((height, WIDE), jnp.float32)],
        ),
        out_shape=jax.ShapeDtypeStruct((4, rows, WIDE), jnp.bfloat16),
        compiler_params=params(48),
        cost_estimate=CHEAP,
    )(meta, *args)


def shrink_kernel(jobs, steps, meta, *refs):
    refs = list(refs)
    xs = [[refs.pop(0) for _ in parts] for parts, _, _, _ in jobs]
    mine, other, out, acc = refs
    k = pl.program_id(0)
    z, c = meta[ZPOS], meta[CORE]
    start = 0
    for (parts, slot, lane, at), x in zip(jobs, xs):
        rows = parts[0].shape[0]
        here = slice(start, start + rows)
        base = 0
        for x_part, part in zip(x, parts):
            tiles = part.shape[1] // TILE

            def step(x_part=x_part, here=here, begin=base == 0):
                for h, a in ((0, mine), (1, other)):
                    value = lax.dot_general(
                        x_part[...], a[...], (((1,), (1,)), ((), ())), preferred_element_type=jnp.float32
                    )
                    cols = slice(h * 256, h * 256 + 256)
                    if begin:
                        value = value + jnp.where(k == 0, 0.0, acc[here, cols])
                    else:
                        value = value + acc[here, cols]
                    acc[here, cols] = value

            pl.when((meta[INNER] == 1) & (k >= base) & (k < base + tiles))(step)
            base += tiles

        def store(slot=slot, lane=lane, at=at, start=start, count=rows // 4):
            for b in range(4):
                name = meta[NAMES + 4 * slot + b]
                chip = name >> 2
                place = ((((name >> 1) & 1) ^ c) << 2) + jnp.where(chip == z, 0, 2) + (name & 1)
                place = jnp.where((chip == z) | (chip == (z ^ 1)), place, -1)
                total = jnp.zeros((count, 64), jnp.float32)
                for i in range(8):
                    part = acc[start + b * count : start + (b + 1) * count, i * 64 : i * 64 + 64]
                    total = total + jnp.where(place == i, part, 0.0)
                out[b, at : at + count, lane : lane + 64] = total.astype(jnp.bfloat16)

        pl.when((meta[INNER] == 1) & (k == steps - 1))(store)
        start += rows


def shrink_sums(meta, jobs, mine, other):
    steps = sum(part.shape[1] // TILE for part in jobs[0][0])
    in_specs, args = [], []
    for parts, _, _, _ in jobs:
        base = 0
        for part in parts:
            tiles = part.shape[1] // TILE
            in_specs.append(
                pl.BlockSpec(
                    (part.shape[0], TILE),
                    lambda k, m, base=base, tiles=tiles: (0, jnp.clip(k - base, 0, tiles - 1) * m[INNER]),
                )
            )
            args.append(part)
            base += tiles
    for a in (mine, other):
        in_specs.append(pl.BlockSpec((a.shape[0], TILE), lambda k, m: (0, k * m[INNER])))
        args.append(a)
    height = sum(parts[0].shape[0] for parts, _, _, _ in jobs)
    return pl.pallas_call(
        functools.partial(shrink_kernel, jobs, steps),
        grid_spec=pltpu.PrefetchScalarGridSpec(
            num_scalar_prefetch=1,
            grid=(steps,),
            in_specs=in_specs,
            out_specs=pl.BlockSpec((4, BLOCK, 128), lambda k, m: (0, 0, 0)),
            scratch_shapes=[pltpu.VMEM((height, 512), jnp.float32)],
        ),
        out_shape=jax.ShapeDtypeStruct((4, BLOCK, 128), jnp.bfloat16),
        compiler_params=params(32),
        cost_estimate=CHEAP,
    )(meta, *args, )


def low_kernel(x, out, swapped):
    total = x[0].astype(jnp.float32)
    for b in range(1, 4):
        total = total + x[b].astype(jnp.float32)
    total = total.astype(jnp.bfloat16)
    out[...] = total
    swapped[...] = jnp.concatenate([total[:, 64:], total[:, :64]], axis=1)


def low_sum(x):
    shape = jax.ShapeDtypeStruct(x.shape[1:], jnp.bfloat16)
    return pl.pallas_call(low_kernel, out_shape=(shape, shape), cost_estimate=CHEAP)(x)


def add_kernel(x, y, out):
    out[...] = (x[...].astype(jnp.float32) + y[...].astype(jnp.float32)).astype(jnp.bfloat16)


def add(x, y):
    return pl.pallas_call(add_kernel, out_shape=jax.ShapeDtypeStruct(x.shape, x.dtype), cost_estimate=CHEAP)(x, y)


def finish_kernel(role, places, low_at, has_delta, has_more, meta, *refs):
    refs = list(refs)
    parts = [refs.pop(0) for _ in places]
    if has_delta:
        low_in, low_out, expand = refs.pop(0), refs.pop(0), refs.pop(0)
    more = refs.pop(0) if has_more else None
    out = refs.pop(0)

    def run():
        done = 0
        for part, (start, rows) in zip(parts, places):
            total = part[0, start : start + rows, :].astype(jnp.float32)
            for b in range(1, 4):
                total = total + part[b, start : start + rows, :].astype(jnp.float32)
            at = slice(done, done + rows)
            if has_delta:
                (lane_in, row_in), (lane_out, row_out) = low_at
                x = low_in[row_in + done : row_in + done + rows, lane_in : lane_in + 64]
                y = low_out[row_out + done : row_out + done + rows, lane_out : lane_out + 64]
                x = jnp.where(meta[INNER] == 1, x, y)
                delta = [dot(x, expand[i, 0]) for i in range(expand.shape[0])]
                total = total + SCALE * jnp.concatenate(delta, axis=1)
            if has_more:
                total = total + more[at, :].astype(jnp.float32)
            out[at, :] = total.astype(jnp.bfloat16)
            done += rows

    if role is None:
        run()
    else:
        pl.when(meta[INNER] == role)(run)


def finish(meta, role, parts, low=None, expand=None, slot=0, more=None):
    places = [(start, rows) for _, start, rows in parts]
    rows = sum(r for _, r in places)
    span = WIDE // 2
    in_specs = [pl.BlockSpec((4, part.shape[1], span), lambda h, m: (0, 0, h)) for part, _, _ in parts]
    args = [part for part, _, _ in parts]
    low_at = None
    if low is not None:
        share = expand.shape[-1]
        for sums, _, _ in low:
            in_specs.append(pl.BlockSpec(sums.shape, lambda h, m: (0, 0)))
            args.append(sums)
        in_specs.append(
            pl.BlockSpec((span // share, 1, expand.shape[2], share), lambda h, m: (h ^ m[CORE], slot, 0, 0))
        )
        args.append(expand)
        low_at = [(lane, row) for _, lane, row in low]
    if more is not None:
        in_specs.append(pl.BlockSpec((rows, span), lambda h, m: (0, h)))
        args.append(more)
    return pl.pallas_call(
        functools.partial(finish_kernel, role, places, low_at, low is not None, more is not None),
        grid_spec=pltpu.PrefetchScalarGridSpec(
            num_scalar_prefetch=1,
            grid=(2,),
            in_specs=in_specs,
            out_specs=pl.BlockSpec((rows, span), lambda h, m: (0, h)),
        ),
        out_shape=jax.ShapeDtypeStruct((rows, WIDE), jnp.bfloat16),
        compiler_params=params(32),
        cost_estimate=CHEAP,
    )(meta, *args)


def assemble_kernel(span, pieces, meta, count, own, partner, *refs):
    out = refs[-1]
    refs = list(refs[:-1])
    groups = []
    for size in pieces:
        groups.append([refs.pop(0) for _ in range(size)])
    z, c, inner = meta[ZPOS], meta[CORE], meta[INNER] == 1
    rows = own.shape[0]
    valid = lax.broadcasted_iota(jnp.int32, (rows, 1), 0) < count[0]

    def put(j, sources):
        for h in range(2):
            at = pl.ds(pl.multiple_of((2 * j + h) * span, span), span)
            part = pl.ds(pl.multiple_of((h ^ c) * span, span), span)
            first = 0
            for source in sources:
                size = source.shape[0]
                keep = valid[first : first + size]
                out[first : first + size, at] = jnp.where(keep, source[:, part], jnp.zeros((), jnp.bfloat16))
                first += size

    put(z, [own])
    put(z ^ 1, [partner])

    @pl.when(inner)
    def _():
        put(z ^ 3, groups[0])
        put(z ^ 2, groups[1])

    @pl.when(jnp.logical_not(inner))
    def _():
        put(z ^ 2, groups[2])
        put(z ^ 3, groups[3])


def assemble(meta, count, own, partner, groups):
    rows, wide = own.shape
    args = [own, partner] + [x for group in groups for x in group]
    return pl.pallas_call(
        functools.partial(assemble_kernel, wide // 2, [len(g) for g in groups]),
        grid_spec=pltpu.PrefetchScalarGridSpec(
            num_scalar_prefetch=2,
            grid=(1,),
            in_specs=[pl.BlockSpec(a.shape, lambda n, m, k: (0, 0)) for a in args],
            out_specs=pl.BlockSpec((rows, 4 * wide), lambda n, m, k: (0, 0)),
        ),
        out_shape=jax.ShapeDtypeStruct((rows, 4 * wide), jnp.bfloat16),
        compiler_params=params(32),
        cost_estimate=CHEAP,
    )(meta, count, *args)


def line_of_four(hidden, down_weight, adapter_shrink, adapter_expand, block_adapter, block_rows):
    rows, feat = hidden.shape
    wide = 2 * down_weight.shape[1]
    adp, _, rank = adapter_shrink.shape
    p = lax.axis_index("pool")
    t = lax.axis_index("tensor")
    tensors = lax.axis_size("tensor")
    z, c = p // 2, p % 2
    outer = (z == 0) | (z == 3)

    def exchange(x):
        return lax.all_to_all(x, "tensor", split_axis=0, concat_axis=0, tiled=True)

    def piece(x, k, lo, hi):
        return x.reshape(rows // BLOCK, 2, PIECE, feat)[:, k, :, lo:hi].reshape(rows // 2, hi - lo)

    def piece_of(x, lo, hi):
        return x[:, lo:hi]

    share = wide // tensors
    w_other = send(down_weight, SIBLING)
    meta = jnp.stack([jnp.where(outer, 0, 1), c, z]).astype(jnp.int32)
    weights = [(down_weight, w_other)]

    h = [piece(hidden, k, 0, feat) for k in range(2)]
    partner = [send(h[0], XOR[1])]
    mid = [send(h[0], MIDDLE)]
    shares = exchange(
        adapter_expand.transpose(0, 2, 1).reshape(adp, rank, tensors, share).transpose(2, 0, 1, 3)
    ).reshape(tensors, adp * rank, share)
    label = jnp.zeros((16, share), jnp.bfloat16).at[0, : block_adapter.shape[0]].set(block_adapter.astype(jnp.bfloat16))

    def shares_of(s):
        return lax.dynamic_index_in_dim(shares, z ^ s, 0, keepdims=False)

    told = [send(jnp.concatenate([shares_of(s), label], axis=0), XOR[s]) for s in (1, 2, 3)]
    j_own = products(meta, [Rows([hidden], None, 0, 0)], weights, BLOCK)
    r_own = exchange(j_own)

    h1 = after([partner[0], mid[0], w_other], h[1])
    partner.append(send(h1, XOR[1]))
    mid.append(send(h1, MIDDLE))
    far_a0 = send(after([j_own], piece_of(partner[0], 0, NEAR)), MIDDLE)
    out_mid0 = send(after([j_own], piece_of(mid[0], 0, NEAR)), OUTWARD)
    shrink_w = adapter_shrink.transpose(0, 2, 1).reshape(adp * rank, feat)
    shrink_o = send(after([partner[0], mid[0]], shrink_w), INWARD)

    j_near0 = products(
        meta, [Rows([partner[0]], None, 0, 0), Rows([mid[0]], 1, PIECE, 0)], weights, BLOCK
    )
    r_near0 = exchange(j_near0)

    told = after([j_near0], *told)
    names = [block_adapter] + [x[adp * rank, : block_adapter.shape[0]].astype(jnp.int32) for x in told]
    middle = jnp.where(outer, names[2], names[3])
    far = jnp.where(outer, names[3], names[2])
    names = jnp.stack([names[0], names[1], middle, far])
    named = jnp.concatenate([meta, names.reshape(-1)])
    held = jnp.stack([shares_of(0)] + [x[: adp * rank] for x in told]).reshape(4, adp, rank, share)
    held_s = send(held, SIBLING)
    held = jnp.stack([jnp.where(c == 0, held, held_s), jnp.where(c == 0, held_s, held)], axis=1)
    held = held.reshape(4 * 2 * adp, rank, share)
    wanted = (names ^ (z * 2 * adp)).T
    picked = jnp.take(held, wanted.reshape(-1), axis=0).reshape(tensors, 4, rank, share)
    expand_rows = exchange(picked)

    far_b0 = send(after([far_a0, mid[1], j_near0, j_own], piece_of(partner[0], NEAR, feat)), MIDDLE)
    out_mid1 = send(after([out_mid0, j_near0, j_own], piece_of(mid[1], 0, NEAR)), OUTWARD)
    near1 = after([r_own, j_near0], partner[1])
    j_near1 = products(
        meta, [Rows([near1], None, 0, 0), Rows([mid[1]], 1, PIECE, 0)], weights, BLOCK
    )
    r_near1 = exchange(j_near1)

    far_a1 = send(after([far_b0, j_near1], piece_of(partner[1], 0, NEAR)), MIDDLE)
    out_far0 = send(after([out_mid1, j_near1], far_a0), OUTWARD)
    v_own = send(after([shrink_o, j_near1], down_weight[NEAR:]), INWARD)
    shrink_mine = jnp.concatenate([shrink_w, shrink_o], axis=0)
    shrink_other = send(shrink_mine, SIBLING)

    early = exchange(
        shrink_sums(
            named,
            [([after([r_near1], hidden)], 0, 0, 0), ([mid[0]], 2, 64, 0), ([mid[1]], 2, 64, PIECE)],
            shrink_mine,
            shrink_other,
        )
    )
    early_sum, early_swapped = low_sum(early)

    third = after([r_near0, early, expand_rows], far_a0)
    j_third = products(
        meta, [Rows([third, far_b0], 1, 0, 0), Rows([out_mid0], 0, 0, 0)], weights, PIECE
    )
    r_third = exchange(j_third)
    far_b1 = send(after([far_a1, j_third], piece_of(partner[1], NEAR, feat)), MIDDLE)
    out_far1 = send(after([out_far0, j_third], far_a1), OUTWARD)
    early = add(early_sum, send(after([j_third], early_swapped), MIDDLE))
    early_out = send(early, OUTWARD)
    v_other = send(v_own, SIBLING)

    fourth = after([r_near1], far_a1)
    j_fourth = products(
        meta, [Rows([fourth, far_b1], 1, 0, 0), Rows([out_mid1], 0, 0, 0)], weights, PIECE
    )
    r_fourth = exchange(j_fourth)
    late, late_swapped = low_sum(
        exchange(
            shrink_sums(
                named,
                [
                    ([partner[0]], 1, 0, 0),
                    ([partner[1]], 1, 0, PIECE),
                    ([far_a0, far_b0], 3, 64, 0),
                    ([far_a1, far_b1], 3, 64, PIECE),
                ],
                shrink_mine,
                shrink_other,
            )
        )
    )
    late = add(late, send(late_swapped, MIDDLE))
    late_out = send(late, OUTWARD)

    low_own = ((early, 0, 0), (late_out, 0, 0))
    low_partner = ((late, 0, 0), (early_out, 0, 0))
    low_mid = ((early, 64, 0), (early_out, 64, 0))

    def low_far(row):
        return ((late, 64, row), (late_out, 64, row))

    rest = [(v_own, v_other), (down_weight, w_other)]
    j_fifth = products(
        meta,
        [
            Rows([after([r_third], far_b0)], 1, 0, 0),
            Rows([far_b1], 1, PIECE, 0),
            Rows([out_far0], 0, 0, 1),
            Rows([out_far1], 0, PIECE, 1),
        ],
        rest,
        BLOCK,
    )
    r_fifth = exchange(j_fifth)
    j_sixth = products(
        meta,
        [Rows([mid[0]], 1, 0, 0), Rows([mid[1]], 1, PIECE, 0)],
        rest[:1],
        BLOCK,
        skip=NEAR_TILES,
        follow=[r_fourth, j_fifth],
    )
    r_sixth = exchange(j_sixth)

    r_near0, r_near1 = after([j_fourth], r_near0, r_near1)
    x_mid_o = finish(meta, 0, [(r_third, 0, PIECE), (r_fourth, 0, PIECE)], low_mid, expand_rows, 2)
    to_mid = send(x_mid_o, INWARD)
    x_mid = finish(meta, 1, [(r_near0, PIECE, PIECE), (r_near1, PIECE, PIECE)], low_mid, expand_rows, 2)
    home_mid = send(x_mid, MIDDLE)
    x_partner = finish(meta, None, [(r_near0, 0, PIECE), (r_near1, 0, PIECE)], low_partner, expand_rows, 1)
    home_partner = send(x_partner, XOR[1])
    x_far = finish(meta, 1, [(r_third, 0, PIECE), (r_fourth, 0, PIECE)], low_far(0), expand_rows, 3)
    home_far = send(x_far, ACROSS)
    x_far_o = [finish(meta, 0, [(r_fifth, k * PIECE, PIECE)], low_far(k * PIECE), expand_rows, 3) for k in range(2)]
    to_far = [send(x, INWARD) for x in x_far_o]
    home_rest_f = [
        send(finish(meta, 1, [(r_fifth, k * PIECE, PIECE)], more=to_far[k]), ACROSS) for k in range(2)
    ]
    home_rest_m = send(finish(meta, 1, [(r_sixth, 0, BLOCK)], more=to_mid), MIDDLE)
    x_own = finish(meta, None, [(r_own, 0, BLOCK)], low_own, expand_rows, 0)
    count = lax.dynamic_slice_in_dim(block_rows, t, 1, 0)
    return assemble(
        meta, count, x_own, home_partner, [[home_mid], [home_rest_m], [home_far], home_rest_f]
    )


def solution(mesh):
    in_specs = (
        P("pool", "tensor"),
        P("tensor", "pool"),
        P("pool", "tensor", None),
        P("pool", "tensor", None),
        P("pool"),
        P("pool"),
    )
    out_specs = P(("pool", "tensor"), None)
    body = line_of_four if dict(mesh.shape) == {"pool": 8, "tensor": 4} else general
    return jax.shard_map(body, mesh=mesh, in_specs=in_specs, out_specs=out_specs, check_vma=False)
```

```python
import functools

import jax
import jax.numpy as jnp
from jax import lax
from jax.experimental import pallas as pl
from jax.experimental.pallas import tpu as pltpu
from jax.sharding import PartitionSpec as P

BLOCK = 128
SCALE = 0.5


def general(hidden, down_weight, adapter_shrink, adapter_expand, block_adapter, block_rows):
    input_rows, feat = hidden.shape
    block_count = block_adapter.shape[0]
    column_span = adapter_expand.shape[1]
    tensor_pos = lax.axis_index("tensor")
    tensor_count = lax.axis_size("tensor")
    own_rows = input_rows // tensor_count
    blocks = hidden.reshape(block_count, BLOCK, feat)
    partial_value = jnp.dot(
        hidden,
        lax.all_gather(down_weight, "pool", axis=1, tiled=True),
        preferred_element_type=jnp.float32,
    )
    total = lax.psum_scatter(
        partial_value.astype(jnp.bfloat16), "tensor", scatter_dimension=0, tiled=True
    ).astype(jnp.float32)
    shrink_piece = lax.all_gather(adapter_shrink, "pool", axis=0, tiled=True)
    expand_piece = lax.all_gather(adapter_expand, "pool", axis=0, tiled=True)
    idents = jnp.arange(shrink_piece.shape[0], dtype=jnp.int32)
    pick = (block_adapter[:, None] == idents[None, :]).astype(jnp.bfloat16)
    first = jnp.einsum("bk,kfr->bfr", pick, shrink_piece, preferred_element_type=jnp.float32)
    second = jnp.einsum("bk,kcr->bcr", pick, expand_piece, preferred_element_type=jnp.float32)
    shrink = jnp.einsum(
        "bnf,bfr->bnr", blocks, first.astype(jnp.bfloat16), preferred_element_type=jnp.float32
    )
    summed_shrink = lax.psum(shrink.astype(jnp.bfloat16), "tensor")
    enlarged_rows = jnp.einsum(
        "bnr,bcr->bnc",
        summed_shrink,
        second.astype(jnp.bfloat16),
        preferred_element_type=jnp.float32,
    )
    adapter_delta_columns = (
        (SCALE * enlarged_rows).astype(jnp.bfloat16).reshape(input_rows, column_span)
    )
    delta_mine = lax.all_to_all(
        adapter_delta_columns, "tensor", split_axis=0, concat_axis=1, tiled=True
    )
    total = total + delta_mine.astype(jnp.float32)
    row_ids = tensor_pos * own_rows + jnp.arange(own_rows, dtype=jnp.int32)
    owning = (row_ids // BLOCK)[:, None] == jnp.arange(block_count, dtype=jnp.int32)[None, :]
    lengths = jnp.sum(jnp.where(owning, block_rows[None, :], 0), axis=1)
    valid = (row_ids % BLOCK < lengths).astype(jnp.float32)
    return (total * valid[:, None]).astype(jnp.bfloat16)


def dot(a, b):
    return jnp.dot(a, b, preferred_element_type=jnp.float32)


def on_line(pairs):
    return [(2 * a + c, 2 * b + c) for a, b in pairs for c in range(2)]


XOR = {s: on_line([(z, z ^ s) for z in range(4)]) for s in (1, 2, 3)}
MIDDLE = on_line([(1, 2), (2, 1)])
OUTWARD = on_line([(1, 0), (2, 3)])
INWARD = on_line([(0, 1), (3, 2)])
ACROSS = on_line([(1, 3), (2, 0)])
SIBLING = [(p, p ^ 1) for p in range(8)]

NEAR = 2048
TILE = 512
NEAR_TILES = NEAR // TILE
PIECE = 64
WIDE = 2048
INNER, CORE, ZPOS, NAMES = 0, 1, 2, 3
CHEAP = pl.CostEstimate(flops=1000, bytes_accessed=1000, transcendentals=0)


def send(x, pairs):
    return lax.ppermute(x, "pool", pairs)


def after(events, *xs):
    tied = lax.optimization_barrier((tuple(events), xs))
    return tied[1] if len(xs) > 1 else tied[1][0]


def params(limit):
    return pltpu.CompilerParams(vmem_limit_bytes=limit * 1024 * 1024)


class Rows:
    def __init__(self, parts, role, at, weights, slot=None):
        self.parts, self.role, self.at, self.weights, self.slot = parts, role, at, weights, slot
        self.rows = parts[0].shape[0]
        self.tiles = [part.shape[1] // TILE for part in parts]


def products_kernel(jobs, weights, shrink, meta, *refs):
    refs = list(refs)
    xs = [[refs.pop(0) for _ in job.parts] for job in jobs]
    ws = [(refs.pop(0), refs.pop(0)) for _ in range(weights)]
    adapters = (refs.pop(0), refs.pop(0)) if shrink else ()
    out, acc = refs[:2]
    low = refs[2] if shrink else None
    k = pl.program_id(0)
    z, c = meta[ZPOS], meta[CORE]
    inner = meta[INNER] == 1
    top = {0: 0, 1: 0}
    for x_parts, job in zip(xs, jobs):
        start = max(top.values()) if job.role is None else top[job.role]
        for role in top if job.role is None else (job.role,):
            top[role] = start + job.rows
        base = 0
        mine = slice(start, start + job.rows)
        role = True if job.role is None else meta[INNER] == job.role
        total = sum(job.tiles)
        own, other = ws[job.weights]
        for x, tiles in zip(x_parts, job.tiles):

            def step(x=x, mine=mine, own=own, other=other, begin=base == 0):
                for h, w in ((0, own), (1, other)):
                    for n in range(0, WIDE // 2, 512):
                        at = slice(h * (WIDE // 2) + n, h * (WIDE // 2) + n + 512)
                        value = dot(x[...], w[:, n : n + 512])
                        if begin:
                            value = value + jnp.where(k == 0, 0.0, acc[mine, at])
                        else:
                            value = value + acc[mine, at]
                        acc[mine, at] = value

            def shrink_step(x=x, mine=mine, begin=base == 0):
                for h, a in enumerate(adapters):
                    at = slice(h * 256, h * 256 + 256)
                    value = lax.dot_general(
                        x[...], a[...], (((1,), (1,)), ((), ())), preferred_element_type=jnp.float32
                    )
                    if begin:
                        value = value + jnp.where(k == 0, 0.0, low[mine, at])
                    else:
                        value = value + low[mine, at]
                    low[mine, at] = value

            now = (k >= base) & (k < base + tiles)
            pl.when(role & now)(step)
            if shrink and job.slot is not None:
                pl.when(inner & now)(shrink_step)
            base += tiles

        def store(job=job, start=start):
            count = job.rows // 4
            for b in range(4):
                out[b, job.at : job.at + count, :WIDE] = acc[start + b * count : start + (b + 1) * count, :].astype(
                    jnp.bfloat16
                )

        def shrink_store(job=job, start=start):
            count = job.rows // 4
            for b in range(4):
                name = meta[NAMES + 4 * job.slot + b]
                chip = name >> 2
                place = ((((name >> 1) & 1) ^ c) << 2) + jnp.where(chip == z, 0, 2) + (name & 1)
                place = jnp.where(inner & ((chip == z) | (chip == (z ^ 1))), place, -1)
                value = jnp.zeros((count, 64), jnp.float32)
                for i in range(8):
                    part = low[start + b * count : start + (b + 1) * count, i * 64 : i * 64 + 64]
                    value = value + jnp.where(place == i, part, 0.0)
                value = jnp.concatenate([value, jnp.zeros_like(value)], axis=1)
                out[b, job.at : job.at + count, WIDE : WIDE + 128] = value.astype(jnp.bfloat16)

        pl.when(role & (k == total - 1))(store)
        if shrink and job.slot is not None:
            pl.when(inner & (k == total - 1))(shrink_store)


def products(meta, jobs, weights, rows, adapters=()):
    steps = max(sum(job.tiles) for job in jobs)
    in_specs, args = [], []
    for job in jobs:
        base = 0
        for part, tiles in zip(job.parts, job.tiles):

            def index(k, m, low=base, tiles=tiles, role=job.role):
                at = jnp.clip(k - low, 0, tiles - 1)
                if role is not None:
                    at = at * (m[INNER] if role == 1 else 1 - m[INNER])
                return (0, at)

            in_specs.append(pl.BlockSpec((part.shape[0], TILE), index))
            args.append(part)
            base += tiles
    for i, pair in enumerate(weights):
        last = [
            max([sum(job.tiles) for job in jobs if job.weights == i and job.role in (None, role)], default=1) - 1
            for role in (0, 1)
        ]

        def index(k, m, last=last):
            return (jnp.minimum(k, jnp.where(m[INNER] == 1, last[1], last[0])), 0)

        for w in pair:
            in_specs.append(pl.BlockSpec((TILE, w.shape[1]), index))
            args.append(w)
    for a in adapters:
        in_specs.append(pl.BlockSpec((a.shape[0], TILE), lambda k, m: (0, k * m[INNER])))
        args.append(a)
    both = sum(job.rows for job in jobs if job.role is None)
    height = both + max(sum(job.rows for job in jobs if job.role == r) for r in (0, 1))
    scratch = [pltpu.VMEM((height, WIDE), jnp.float32)]
    if adapters:
        scratch.append(pltpu.VMEM((height, 512), jnp.float32))
    shape = (4, rows, WIDE + 128 if adapters else WIDE)
    return pl.pallas_call(
        functools.partial(products_kernel, jobs, len(weights), bool(adapters)),
        grid_spec=pltpu.PrefetchScalarGridSpec(
            num_scalar_prefetch=1,
            grid=(steps,),
            in_specs=in_specs,
            out_specs=pl.BlockSpec(shape, lambda k, m: (0, 0, 0)),
            scratch_shapes=scratch,
        ),
        out_shape=jax.ShapeDtypeStruct(shape, jnp.bfloat16),
        compiler_params=params(48),
        cost_estimate=CHEAP,
    )(meta, *args)


def low_kernel(x, y, out, swapped):
    def total(ref):
        value = ref[0, :, :64].astype(jnp.float32)
        for b in range(1, 4):
            value = value + ref[b, :, :64].astype(jnp.float32)
        return value.astype(jnp.bfloat16)

    one, two = total(x), total(y)
    out[...] = jnp.concatenate([one, two], axis=1)
    swapped[...] = jnp.concatenate([two, one], axis=1)


def low_sums(x, x_row, y, y_row):
    shape = jax.ShapeDtypeStruct((BLOCK, 128), jnp.bfloat16)
    spec = lambda row: pl.BlockSpec((4, BLOCK, 128), lambda i: (0, row // BLOCK, WIDE // 128))
    whole = pl.BlockSpec((BLOCK, 128), lambda i: (0, 0))
    return pl.pallas_call(
        low_kernel,
        grid=(1,),
        in_specs=[spec(x_row), spec(y_row)],
        out_specs=(whole, whole),
        out_shape=(shape, shape),
        cost_estimate=CHEAP,
    )(x, y)


def add_kernel(x, y, out):
    out[...] = (x[...].astype(jnp.float32) + y[...].astype(jnp.float32)).astype(jnp.bfloat16)


def add(x, y):
    return pl.pallas_call(add_kernel, out_shape=jax.ShapeDtypeStruct(x.shape, x.dtype), cost_estimate=CHEAP)(x, y)


def finish_kernel(role, places, low_at, has_delta, has_more, meta, *refs):
    refs = list(refs)
    parts = [refs.pop(0) for _ in places]
    if has_delta:
        low_in, low_out, expand = refs.pop(0), refs.pop(0), refs.pop(0)
    more = refs.pop(0) if has_more else None
    out = refs.pop(0)

    def run():
        done = 0
        for part, (start, rows) in zip(parts, places):
            total = part[0, start : start + rows, :].astype(jnp.float32)
            for b in range(1, 4):
                total = total + part[b, start : start + rows, :].astype(jnp.float32)
            at = slice(done, done + rows)
            if has_delta:
                (lane_in, row_in), (lane_out, row_out) = low_at
                x = low_in[row_in + done : row_in + done + rows, lane_in : lane_in + 64]
                y = low_out[row_out + done : row_out + done + rows, lane_out : lane_out + 64]
                x = jnp.where(meta[INNER] == 1, x, y)
                delta = [dot(x, expand[i, 0]) for i in range(expand.shape[0])]
                total = total + SCALE * jnp.concatenate(delta, axis=1)
            if has_more:
                total = total + more[at, :].astype(jnp.float32)
            out[at, :] = total.astype(jnp.bfloat16)
            done += rows

    if role is None:
        run()
    else:
        pl.when(meta[INNER] == role)(run)


def finish(meta, role, parts, low=None, expand=None, slot=0, more=None):
    places = [(start, rows) for _, start, rows in parts]
    rows = sum(r for _, r in places)
    span = WIDE // 2
    in_specs = [pl.BlockSpec((4, part.shape[1], span), lambda h, m: (0, 0, h)) for part, _, _ in parts]
    args = [part for part, _, _ in parts]
    low_at = None
    if low is not None:
        share = expand.shape[-1]
        for sums, _, _ in low:
            in_specs.append(pl.BlockSpec(sums.shape, lambda h, m: (0, 0)))
            args.append(sums)
        in_specs.append(
            pl.BlockSpec((span // share, 1, expand.shape[2], share), lambda h, m: (h ^ m[CORE], slot, 0, 0))
        )
        args.append(expand)
        low_at = [(lane, row) for _, lane, row in low]
    if more is not None:
        in_specs.append(pl.BlockSpec((rows, span), lambda h, m: (0, h)))
        args.append(more)
    return pl.pallas_call(
        functools.partial(finish_kernel, role, places, low_at, low is not None, more is not None),
        grid_spec=pltpu.PrefetchScalarGridSpec(
            num_scalar_prefetch=1,
            grid=(2,),
            in_specs=in_specs,
            out_specs=pl.BlockSpec((rows, span), lambda h, m: (0, h)),
        ),
        out_shape=jax.ShapeDtypeStruct((rows, WIDE), jnp.bfloat16),
        compiler_params=params(32),
        cost_estimate=CHEAP,
    )(meta, *args)


def assemble_kernel(span, pieces, meta, count, own, partner, *refs):
    out = refs[-1]
    refs = list(refs[:-1])
    groups = []
    for size in pieces:
        groups.append([refs.pop(0) for _ in range(size)])
    z, c, inner = meta[ZPOS], meta[CORE], meta[INNER] == 1
    rows = own.shape[0]
    valid = lax.broadcasted_iota(jnp.int32, (rows, 1), 0) < count[0]

    def put(j, sources):
        for h in range(2):
            at = pl.ds(pl.multiple_of((2 * j + h) * span, span), span)
            part = pl.ds(pl.multiple_of((h ^ c) * span, span), span)
            first = 0
            for source in sources:
                size = source.shape[0]
                keep = valid[first : first + size]
                out[first : first + size, at] = jnp.where(keep, source[:, part], jnp.zeros((), jnp.bfloat16))
                first += size

    put(z, [own])
    put(z ^ 1, [partner])

    @pl.when(inner)
    def _():
        put(z ^ 3, groups[0])
        put(z ^ 2, groups[1])

    @pl.when(jnp.logical_not(inner))
    def _():
        put(z ^ 2, groups[2])
        put(z ^ 3, groups[3])


def assemble(meta, count, own, partner, groups):
    rows, wide = own.shape
    args = [own, partner] + [x for group in groups for x in group]
    return pl.pallas_call(
        functools.partial(assemble_kernel, wide // 2, [len(g) for g in groups]),
        grid_spec=pltpu.PrefetchScalarGridSpec(
            num_scalar_prefetch=2,
            grid=(1,),
            in_specs=[pl.BlockSpec(a.shape, lambda n, m, k: (0, 0)) for a in args],
            out_specs=pl.BlockSpec((rows, 4 * wide), lambda n, m, k: (0, 0)),
        ),
        out_shape=jax.ShapeDtypeStruct((rows, 4 * wide), jnp.bfloat16),
        compiler_params=params(32),
        cost_estimate=CHEAP,
    )(meta, count, *args)


def line_of_four(hidden, down_weight, adapter_shrink, adapter_expand, block_adapter, block_rows):
    rows, feat = hidden.shape
    wide = 2 * down_weight.shape[1]
    adp, _, rank = adapter_shrink.shape
    p = lax.axis_index("pool")
    t = lax.axis_index("tensor")
    tensors = lax.axis_size("tensor")
    z, c = p // 2, p % 2
    outer = (z == 0) | (z == 3)

    def exchange(x):
        return lax.all_to_all(x, "tensor", split_axis=0, concat_axis=0, tiled=True)

    share = wide // tensors
    place = jnp.stack([jnp.where(outer, 0, 1), c, z]).astype(jnp.int32)
    meta = jnp.concatenate([place, block_adapter])

    shrink_w = adapter_shrink.transpose(0, 2, 1).reshape(adp * rank, feat)
    shrink_o = send(shrink_w, INWARD)
    w_other = send(down_weight, SIBLING)
    weights = [(down_weight, w_other)]
    own = [hidden[:, :NEAR], hidden[:, NEAR:]]
    partner = [send(own[0], XOR[1])]
    mid = [send(own[0], MIDDLE)]

    shares = exchange(
        adapter_expand.transpose(0, 2, 1).reshape(adp, rank, tensors, share).transpose(2, 0, 1, 3)
    ).reshape(tensors, adp * rank, share)
    label = jnp.zeros((16, share), jnp.bfloat16).at[0, : block_adapter.shape[0]].set(block_adapter.astype(jnp.bfloat16))

    def shares_of(s):
        return lax.dynamic_index_in_dim(shares, z ^ s, 0, keepdims=False)

    told = [send(jnp.concatenate([shares_of(s), label], axis=0), XOR[s]) for s in (1, 2, 3)]
    shrink_mine = jnp.concatenate([shrink_w, shrink_o], axis=0)
    adapters = (shrink_mine, send(shrink_mine, SIBLING))

    part = after([partner[0], mid[0], w_other, shares], own[1])
    partner.append(send(part, XOR[1]))
    mid.append(send(part, MIDDLE))

    j_own = products(meta, [Rows([hidden], None, 0, 0, 0)], weights, BLOCK, adapters)
    r_own = exchange(j_own)

    far = [send(after([j_own], partner[0]), MIDDLE)]
    out_mid = send(after([j_own], mid[0]), OUTWARD)

    told = after([j_own], *told)
    names = [block_adapter] + [x[adp * rank, : block_adapter.shape[0]].astype(jnp.int32) for x in told]
    name_m = jnp.where(outer, names[2], names[3])
    name_f = jnp.where(outer, names[3], names[2])
    names = jnp.stack([names[0], names[1], name_m, name_f])
    meta = jnp.concatenate([place, names.reshape(-1)])
    held = jnp.stack([shares_of(0)] + [x[: adp * rank] for x in told]).reshape(4, adp, rank, share)
    held_s = send(held, SIBLING)
    held = jnp.stack([jnp.where(c == 0, held, held_s), jnp.where(c == 0, held_s, held)], axis=1)
    held = held.reshape(4 * 2 * adp, rank, share)
    wanted = (names ^ (z * 2 * adp)).T
    picked = jnp.take(held, wanted.reshape(-1), axis=0).reshape(tensors, 4, rank, share)
    expand_rows = exchange(picked)

    v_own = send(after([mid[1], j_own], down_weight[NEAR:]), INWARD)
    far.append(send(after([mid[1], j_own], partner[1]), MIDDLE))
    j_near = products(
        meta,
        [Rows([partner[0], after([r_own, expand_rows], partner[1])], None, 0, 0, 1), Rows(mid, 1, BLOCK, 0, 2)],
        weights,
        2 * BLOCK,
        adapters,
    )
    r_near = exchange(j_near)
    out_far = send(after([out_mid, j_near], far[0]), OUTWARD)
    v_other = send(v_own, SIBLING)

    early_sum, early_swapped = low_sums(r_own, 0, r_near, BLOCK)
    early = add(early_sum, send(early_swapped, MIDDLE))
    early_out = send(early, OUTWARD)

    j_third = products(
        meta,
        [Rows([far[0], after([r_near], far[1])], 1, 0, 0, 3), Rows([out_mid], 0, 0, 0)],
        weights,
        BLOCK,
        adapters,
    )
    r_third = exchange(j_third)

    rest = [(v_own, v_other), (down_weight, w_other)]
    j_fifth = products(
        meta,
        [Rows([after([j_third], far[1])], 1, 0, 0), Rows([out_far], 0, 0, 1)],
        rest,
        BLOCK,
    )
    r_fifth = exchange(j_fifth)
    j_sixth = products(meta, [Rows([after([j_fifth], mid[1])], 1, 0, 0)], rest[:1], BLOCK)
    r_sixth = exchange(j_sixth)

    late_sum, late_swapped = low_sums(r_near, 0, r_third, 0)
    late = add(late_sum, send(late_swapped, MIDDLE))
    late_out = send(late, OUTWARD)

    low_own = ((early, 0, 0), (late_out, 0, 0))
    low_partner = ((late, 0, 0), (early_out, 0, 0))
    low_mid = ((early, 64, 0), (early_out, 64, 0))
    low_far = ((late, 64, 0), (late_out, 64, 0))

    r_near = after([j_third], r_near)
    x_mid = finish(meta, 1, [(r_near, BLOCK, BLOCK)], low_mid, expand_rows, 2)
    home_mid = send(x_mid, MIDDLE)
    x_mid_o = finish(meta, 0, [(r_third, 0, BLOCK)], low_mid, expand_rows, 2)
    to_mid = send(x_mid_o, INWARD)
    x_far = finish(meta, 1, [(r_third, 0, BLOCK)], low_far, expand_rows, 3)
    home_far = send(x_far, ACROSS)
    x_partner = finish(meta, None, [(r_near, 0, BLOCK)], low_partner, expand_rows, 1)
    home_partner = send(x_partner, XOR[1])
    x_far_o = finish(meta, 0, [(r_fifth, 0, BLOCK)], low_far, expand_rows, 3)
    to_far = send(x_far_o, INWARD)
    home_rest_f = send(finish(meta, 1, [(r_fifth, 0, BLOCK)], more=to_far), ACROSS)
    home_rest_m = send(finish(meta, 1, [(r_sixth, 0, BLOCK)], more=to_mid), MIDDLE)
    x_own = finish(meta, None, [(r_own, 0, BLOCK)], low_own, expand_rows, 0)
    count = lax.dynamic_slice_in_dim(block_rows, t, 1, 0)
    return assemble(
        meta, count, x_own, home_partner, [[home_mid], [home_rest_m], [home_far], [home_rest_f]]
    )


def solution(mesh):
    in_specs = (
        P("pool", "tensor"),
        P("tensor", "pool"),
        P("pool", "tensor", None),
        P("pool", "tensor", None),
        P("pool"),
        P("pool"),
    )
    out_specs = P(("pool", "tensor"), None)
    body = line_of_four if dict(mesh.shape) == {"pool": 8, "tensor": 4} else general
    return jax.shard_map(body, mesh=mesh, in_specs=in_specs, out_specs=out_specs, check_vma=False)
```

```python
import functools

import jax
import jax.numpy as jnp
from jax import lax
from jax.experimental import pallas as pl
from jax.experimental.pallas import tpu as pltpu
from jax.sharding import PartitionSpec as P

BLOCK = 128
SCALE = 0.5


def general(hidden, down_weight, adapter_shrink, adapter_expand, block_adapter, block_rows):
    input_rows, feat = hidden.shape
    block_count = block_adapter.shape[0]
    column_span = adapter_expand.shape[1]
    tensor_pos = lax.axis_index("tensor")
    tensor_count = lax.axis_size("tensor")
    own_rows = input_rows // tensor_count
    blocks = hidden.reshape(block_count, BLOCK, feat)
    partial_value = jnp.dot(
        hidden,
        lax.all_gather(down_weight, "pool", axis=1, tiled=True),
        preferred_element_type=jnp.float32,
    )
    total = lax.psum_scatter(
        partial_value.astype(jnp.bfloat16), "tensor", scatter_dimension=0, tiled=True
    ).astype(jnp.float32)
    shrink_piece = lax.all_gather(adapter_shrink, "pool", axis=0, tiled=True)
    expand_piece = lax.all_gather(adapter_expand, "pool", axis=0, tiled=True)
    idents = jnp.arange(shrink_piece.shape[0], dtype=jnp.int32)
    pick = (block_adapter[:, None] == idents[None, :]).astype(jnp.bfloat16)
    first = jnp.einsum("bk,kfr->bfr", pick, shrink_piece, preferred_element_type=jnp.float32)
    second = jnp.einsum("bk,kcr->bcr", pick, expand_piece, preferred_element_type=jnp.float32)
    shrink = jnp.einsum(
        "bnf,bfr->bnr", blocks, first.astype(jnp.bfloat16), preferred_element_type=jnp.float32
    )
    summed_shrink = lax.psum(shrink.astype(jnp.bfloat16), "tensor")
    enlarged_rows = jnp.einsum(
        "bnr,bcr->bnc",
        summed_shrink,
        second.astype(jnp.bfloat16),
        preferred_element_type=jnp.float32,
    )
    adapter_delta_columns = (
        (SCALE * enlarged_rows).astype(jnp.bfloat16).reshape(input_rows, column_span)
    )
    delta_mine = lax.all_to_all(
        adapter_delta_columns, "tensor", split_axis=0, concat_axis=1, tiled=True
    )
    total = total + delta_mine.astype(jnp.float32)
    row_ids = tensor_pos * own_rows + jnp.arange(own_rows, dtype=jnp.int32)
    owning = (row_ids // BLOCK)[:, None] == jnp.arange(block_count, dtype=jnp.int32)[None, :]
    lengths = jnp.sum(jnp.where(owning, block_rows[None, :], 0), axis=1)
    valid = (row_ids % BLOCK < lengths).astype(jnp.float32)
    return (total * valid[:, None]).astype(jnp.bfloat16)


def dot(a, b):
    return jnp.dot(a, b, preferred_element_type=jnp.float32)


def on_line(pairs):
    return [(2 * a + c, 2 * b + c) for a, b in pairs for c in range(2)]


XOR = {s: on_line([(z, z ^ s) for z in range(4)]) for s in (1, 2, 3)}
MIDDLE = on_line([(1, 2), (2, 1)])
OUTWARD = on_line([(1, 0), (2, 3)])
INWARD = on_line([(0, 1), (3, 2)])
ACROSS = on_line([(1, 3), (2, 0)])
SIBLING = [(p, p ^ 1) for p in range(8)]

NEAR = 2048
TILE = 512
NEAR_TILES = NEAR // TILE
PIECE = 64
WIDE = 2048
INNER, CORE, ZPOS, NAMES = 0, 1, 2, 3
CHEAP = pl.CostEstimate(flops=1000, bytes_accessed=1000, transcendentals=0)


def send(x, pairs):
    return lax.ppermute(x, "pool", pairs)


def after(events, *xs):
    tied = lax.optimization_barrier((tuple(events), xs))
    return tied[1] if len(xs) > 1 else tied[1][0]


def params(limit):
    return pltpu.CompilerParams(vmem_limit_bytes=limit * 1024 * 1024)


class Rows:
    def __init__(self, parts, role, at, weights, slot=None):
        self.parts, self.role, self.at, self.weights, self.slot = parts, role, at, weights, slot
        self.rows = parts[0].shape[0]
        self.tiles = [part.shape[1] // TILE for part in parts]


def products_kernel(jobs, weights, shrink, pick, meta, *refs):
    refs = list(refs)
    xs = [[refs.pop(0) for _ in job.parts] for job in jobs]
    ws = [(refs.pop(0), refs.pop(0)) for _ in range(weights)]
    adapters = (refs.pop(0), refs.pop(0)) if shrink else ()
    held = (refs.pop(0), refs.pop(0)) if pick else ()
    out, acc = refs[:2]
    low = refs[2] if shrink else None
    k = pl.program_id(0)
    z, c = meta[ZPOS], meta[CORE]
    inner = meta[INNER] == 1
    low_at = WIDE + 512 if pick else WIDE

    def choose():
        for b in range(4):
            for slot in range(4):
                name = meta[NAMES + 4 * slot + b]
                mine = ((name >> 1) & 1) == c
                index = 2 * ((name >> 2) ^ z) + (name & 1)
                value = jnp.where(mine, held[0][index], held[1][index])
                out[b, slot * 64 : slot * 64 + 64, WIDE : WIDE + 512] = value

    if pick:
        pl.when(k == 0)(choose)
    top = {0: 0, 1: 0}
    for x_parts, job in zip(xs, jobs):
        start = max(top.values()) if job.role is None else top[job.role]
        for role in top if job.role is None else (job.role,):
            top[role] = start + job.rows
        base = 0
        mine = slice(start, start + job.rows)
        role = True if job.role is None else meta[INNER] == job.role
        total = sum(job.tiles)
        own, other = ws[job.weights]
        for x, tiles in zip(x_parts, job.tiles):

            def step(x=x, mine=mine, own=own, other=other, begin=base == 0):
                for h, w in ((0, own), (1, other)):
                    for n in range(0, WIDE // 2, 512):
                        at = slice(h * (WIDE // 2) + n, h * (WIDE // 2) + n + 512)
                        value = dot(x[...], w[:, n : n + 512])
                        if begin:
                            value = value + jnp.where(k == 0, 0.0, acc[mine, at])
                        else:
                            value = value + acc[mine, at]
                        acc[mine, at] = value

            def shrink_step(x=x, mine=mine, begin=base == 0):
                for h, a in enumerate(adapters):
                    at = slice(h * 256, h * 256 + 256)
                    value = lax.dot_general(
                        x[...], a[...], (((1,), (1,)), ((), ())), preferred_element_type=jnp.float32
                    )
                    if begin:
                        value = value + jnp.where(k == 0, 0.0, low[mine, at])
                    else:
                        value = value + low[mine, at]
                    low[mine, at] = value

            now = (k >= base) & (k < base + tiles)
            pl.when(role & now)(step)
            if shrink and job.slot is not None:
                pl.when(inner & now)(shrink_step)
            base += tiles

        def store(job=job, start=start):
            count = job.rows // 4
            for b in range(4):
                out[b, job.at : job.at + count, :WIDE] = acc[start + b * count : start + (b + 1) * count, :].astype(
                    jnp.bfloat16
                )

        def shrink_store(job=job, start=start):
            count = job.rows // 4
            for b in range(4):
                name = meta[NAMES + 4 * job.slot + b]
                chip = name >> 2
                place = ((((name >> 1) & 1) ^ c) << 2) + jnp.where(chip == z, 0, 2) + (name & 1)
                place = jnp.where(inner & ((chip == z) | (chip == (z ^ 1))), place, -1)
                value = jnp.zeros((count, 64), jnp.float32)
                for i in range(8):
                    part = low[start + b * count : start + (b + 1) * count, i * 64 : i * 64 + 64]
                    value = value + jnp.where(place == i, part, 0.0)
                value = jnp.concatenate([value, jnp.zeros_like(value)], axis=1)
                out[b, job.at : job.at + count, low_at : low_at + 128] = value.astype(jnp.bfloat16)

        pl.when(role & (k == total - 1))(store)
        if shrink and job.slot is not None:
            pl.when(inner & (k == total - 1))(shrink_store)


def products(meta, jobs, weights, rows, adapters=(), held=()):
    steps = max(sum(job.tiles) for job in jobs)
    in_specs, args = [], []
    for job in jobs:
        base = 0
        for part, tiles in zip(job.parts, job.tiles):

            def index(k, m, low=base, tiles=tiles, role=job.role):
                at = jnp.clip(k - low, 0, tiles - 1)
                if role is not None:
                    at = at * (m[INNER] if role == 1 else 1 - m[INNER])
                return (0, at)

            in_specs.append(pl.BlockSpec((part.shape[0], TILE), index))
            args.append(part)
            base += tiles
    for i, pair in enumerate(weights):
        last = [
            max([sum(job.tiles) for job in jobs if job.weights == i and job.role in (None, role)], default=1) - 1
            for role in (0, 1)
        ]

        def index(k, m, last=last):
            return (jnp.minimum(k, jnp.where(m[INNER] == 1, last[1], last[0])), 0)

        for w in pair:
            in_specs.append(pl.BlockSpec((TILE, w.shape[1]), index))
            args.append(w)
    for a in adapters:
        in_specs.append(pl.BlockSpec((a.shape[0], TILE), lambda k, m: (0, k * m[INNER])))
        args.append(a)
    for a in held:
        in_specs.append(pl.BlockSpec(a.shape, lambda k, m: (0, 0, 0)))
        args.append(a)
    both = sum(job.rows for job in jobs if job.role is None)
    height = both + max(sum(job.rows for job in jobs if job.role == r) for r in (0, 1))
    scratch = [pltpu.VMEM((height, WIDE), jnp.float32)]
    if adapters:
        scratch.append(pltpu.VMEM((height, 512), jnp.float32))
    shape = (4, rows, WIDE + (128 if adapters else 0) + (512 if held else 0))
    return pl.pallas_call(
        functools.partial(products_kernel, jobs, len(weights), bool(adapters), bool(held)),
        grid_spec=pltpu.PrefetchScalarGridSpec(
            num_scalar_prefetch=1,
            grid=(steps,),
            in_specs=in_specs,
            out_specs=pl.BlockSpec(shape, lambda k, m: (0, 0, 0)),
            scratch_shapes=scratch,
        ),
        out_shape=jax.ShapeDtypeStruct(shape, jnp.bfloat16),
        compiler_params=params(48),
        cost_estimate=CHEAP,
    )(meta, *args)


def low_kernel(x, y, out, swapped):
    def total(ref):
        value = ref[0, :, :64].astype(jnp.float32)
        for b in range(1, 4):
            value = value + ref[b, :, :64].astype(jnp.float32)
        return value.astype(jnp.bfloat16)

    one, two = total(x), total(y)
    out[...] = jnp.concatenate([one, two], axis=1)
    swapped[...] = jnp.concatenate([two, one], axis=1)


def low_sums(x, x_row, y, y_row):
    shape = jax.ShapeDtypeStruct((BLOCK, 128), jnp.bfloat16)
    spec = lambda a, row: pl.BlockSpec((4, BLOCK, 128), lambda i: (0, row // BLOCK, a.shape[2] // 128 - 1))
    whole = pl.BlockSpec((BLOCK, 128), lambda i: (0, 0))
    return pl.pallas_call(
        low_kernel,
        grid=(1,),
        in_specs=[spec(x, x_row), spec(y, y_row)],
        out_specs=(whole, whole),
        out_shape=(shape, shape),
        cost_estimate=CHEAP,
    )(x, y)


def add_kernel(x, y, out):
    out[...] = (x[...].astype(jnp.float32) + y[...].astype(jnp.float32)).astype(jnp.bfloat16)


def add(x, y):
    return pl.pallas_call(add_kernel, out_shape=jax.ShapeDtypeStruct(x.shape, x.dtype), cost_estimate=CHEAP)(x, y)


def finish_kernel(role, places, low_at, has_delta, has_more, meta, *refs):
    refs = list(refs)
    parts = [refs.pop(0) for _ in places]
    if has_delta:
        low_in, low_out, expand = refs.pop(0), refs.pop(0), refs.pop(0)
    more = refs.pop(0) if has_more else None
    out = refs.pop(0)

    def run():
        done = 0
        for part, (start, rows) in zip(parts, places):
            total = part[0, start : start + rows, :].astype(jnp.float32)
            for b in range(1, 4):
                total = total + part[b, start : start + rows, :].astype(jnp.float32)
            at = slice(done, done + rows)
            if has_delta:
                (lane_in, row_in), (lane_out, row_out) = low_at
                x = low_in[row_in + done : row_in + done + rows, lane_in : lane_in + 64]
                y = low_out[row_out + done : row_out + done + rows, lane_out : lane_out + 64]
                x = jnp.where(meta[INNER] == 1, x, y)
                delta = [dot(x, expand[i]) for i in range(expand.shape[0])]
                total = total + SCALE * jnp.concatenate(delta, axis=1)
            if has_more:
                total = total + more[at, :].astype(jnp.float32)
            out[at, :] = total.astype(jnp.bfloat16)
            done += rows

    if role is None:
        run()
    else:
        pl.when(meta[INNER] == role)(run)


def finish(meta, role, parts, low=None, expand=None, slot=0, more=None):
    places = [(start, rows) for _, start, rows in parts]
    rows = sum(r for _, r in places)
    span = WIDE // 2
    in_specs = [pl.BlockSpec((4, part.shape[1], span), lambda h, m: (0, 0, h)) for part, _, _ in parts]
    args = [part for part, _, _ in parts]
    low_at = None
    if low is not None:
        share = 512
        for sums, _, _ in low:
            in_specs.append(pl.BlockSpec(sums.shape, lambda h, m: (0, 0)))
            args.append(sums)
        in_specs.append(
            pl.BlockSpec((span // share, 64, share), lambda h, m: (h ^ m[CORE], slot, WIDE // share))
        )
        args.append(expand)
        low_at = [(lane, row) for _, lane, row in low]
    if more is not None:
        in_specs.append(pl.BlockSpec((rows, span), lambda h, m: (0, h)))
        args.append(more)
    return pl.pallas_call(
        functools.partial(finish_kernel, role, places, low_at, low is not None, more is not None),
        grid_spec=pltpu.PrefetchScalarGridSpec(
            num_scalar_prefetch=1,
            grid=(2,),
            in_specs=in_specs,
            out_specs=pl.BlockSpec((rows, span), lambda h, m: (0, h)),
        ),
        out_shape=jax.ShapeDtypeStruct((rows, WIDE), jnp.bfloat16),
        compiler_params=params(32),
        cost_estimate=CHEAP,
    )(meta, *args)


def assemble_kernel(span, pieces, meta, count, own, partner, *refs):
    out = refs[-1]
    refs = list(refs[:-1])
    groups = []
    for size in pieces:
        groups.append([refs.pop(0) for _ in range(size)])
    z, c, inner = meta[ZPOS], meta[CORE], meta[INNER] == 1
    rows = own.shape[0]
    valid = lax.broadcasted_iota(jnp.int32, (rows, 1), 0) < count[0]

    def put(j, sources):
        for h in range(2):
            at = pl.ds(pl.multiple_of((2 * j + h) * span, span), span)
            part = pl.ds(pl.multiple_of((h ^ c) * span, span), span)
            first = 0
            for source in sources:
                size = source.shape[0]
                keep = valid[first : first + size]
                out[first : first + size, at] = jnp.where(keep, source[:, part], jnp.zeros((), jnp.bfloat16))
                first += size

    put(z, [own])
    put(z ^ 1, [partner])

    @pl.when(inner)
    def _():
        put(z ^ 3, groups[0])
        put(z ^ 2, groups[1])

    @pl.when(jnp.logical_not(inner))
    def _():
        put(z ^ 2, groups[2])
        put(z ^ 3, groups[3])


def assemble(meta, count, own, partner, groups):
    rows, wide = own.shape
    args = [own, partner] + [x for group in groups for x in group]
    return pl.pallas_call(
        functools.partial(assemble_kernel, wide // 2, [len(g) for g in groups]),
        grid_spec=pltpu.PrefetchScalarGridSpec(
            num_scalar_prefetch=2,
            grid=(1,),
            in_specs=[pl.BlockSpec(a.shape, lambda n, m, k: (0, 0)) for a in args],
            out_specs=pl.BlockSpec((rows, 4 * wide), lambda n, m, k: (0, 0)),
        ),
        out_shape=jax.ShapeDtypeStruct((rows, 4 * wide), jnp.bfloat16),
        compiler_params=params(32),
        cost_estimate=CHEAP,
    )(meta, count, *args)


def line_of_four(hidden, down_weight, adapter_shrink, adapter_expand, block_adapter, block_rows):
    rows, feat = hidden.shape
    wide = 2 * down_weight.shape[1]
    adp, _, rank = adapter_shrink.shape
    p = lax.axis_index("pool")
    t = lax.axis_index("tensor")
    tensors = lax.axis_size("tensor")
    z, c = p // 2, p % 2
    outer = (z == 0) | (z == 3)

    def exchange(x):
        return lax.all_to_all(x, "tensor", split_axis=0, concat_axis=0, tiled=True)

    share = wide // tensors
    place = jnp.stack([jnp.where(outer, 0, 1), c, z]).astype(jnp.int32)
    meta = jnp.concatenate([place, block_adapter])

    shrink_w = adapter_shrink.transpose(0, 2, 1).reshape(adp * rank, feat)
    shrink_o = send(shrink_w, INWARD)
    w_other = send(down_weight, SIBLING)
    weights = [(down_weight, w_other)]
    own = [hidden[:, :NEAR], hidden[:, NEAR:]]
    partner = [send(own[0], XOR[1])]
    mid = [send(own[0], MIDDLE)]

    shares = exchange(
        adapter_expand.transpose(0, 2, 1).reshape(adp, rank, tensors, share).transpose(2, 0, 1, 3)
    ).reshape(tensors, adp * rank, share)
    label = jnp.zeros((16, share), jnp.bfloat16).at[0, : block_adapter.shape[0]].set(block_adapter.astype(jnp.bfloat16))

    def shares_of(s):
        return lax.dynamic_index_in_dim(shares, z ^ s, 0, keepdims=False)

    shares = after([partner[0], mid[0]], shares)
    told = [send(jnp.concatenate([shares_of(s), label], axis=0), XOR[s]) for s in (1, 2, 3)]
    shrink_mine = jnp.concatenate([shrink_w, after([partner[0], mid[0]], shrink_o)], axis=0)
    adapters = (shrink_mine, send(shrink_mine, SIBLING))

    part = after([partner[0], mid[0], w_other], own[1])
    partner.append(send(part, XOR[1]))
    mid.append(send(part, MIDDLE))

    j_own = products(meta, [Rows([hidden], None, 0, 0, 0)], weights, BLOCK, adapters)
    r_own = exchange(j_own)

    far = [send(after([j_own], partner[0]), MIDDLE)]
    out_mid = send(after([j_own], mid[0]), OUTWARD)

    told = after([j_own], *told)
    names = [block_adapter] + [x[adp * rank, : block_adapter.shape[0]].astype(jnp.int32) for x in told]
    name_m = jnp.where(outer, names[2], names[3])
    name_f = jnp.where(outer, names[3], names[2])
    names = jnp.stack([names[0], names[1], name_m, name_f])
    meta = jnp.concatenate([place, names.reshape(-1)])
    held = jnp.concatenate([shares_of(0)] + [x[: adp * rank] for x in told]).reshape(4 * adp, rank, share)
    held = (held, send(held, SIBLING))

    v_own = send(after([mid[1]], down_weight[NEAR:]), INWARD)
    far.append(send(after([mid[1]], partner[1]), MIDDLE))
    j_near = products(
        meta,
        [Rows([partner[0], after([r_own], partner[1])], None, 0, 0, 1), Rows(mid, 1, BLOCK, 0, 2)],
        weights,
        2 * BLOCK,
        adapters,
        held,
    )
    r_near = exchange(j_near)
    out_far = send(after([out_mid, j_near], far[0]), OUTWARD)
    j_third = products(
        meta,
        [Rows([far[0], after([r_near], far[1])], 1, 0, 0, 3), Rows([out_mid], 0, 0, 0)],
        weights,
        BLOCK,
        adapters,
    )
    r_third = exchange(j_third)
    v_other = send(after([j_third, out_far], v_own), SIBLING)

    r_near = after([j_third], r_near)
    early_sum, early_swapped = low_sums(r_own, 0, r_near, BLOCK)
    early = add(early_sum, send(early_swapped, MIDDLE))
    early_out = send(early, OUTWARD)


    rest = [(v_own, v_other), (down_weight, w_other)]
    j_fifth = products(
        meta,
        [Rows([after([j_third], far[1])], 1, 0, 0), Rows([out_far], 0, 0, 1)],
        rest,
        BLOCK,
    )
    r_fifth = exchange(j_fifth)
    j_sixth = products(meta, [Rows([after([j_fifth, early], mid[1])], 1, 0, 0)], rest[:1], BLOCK)
    r_sixth = exchange(j_sixth)

    late_sum, late_swapped = low_sums(r_near, 0, r_third, 0)
    late = add(late_sum, send(late_swapped, MIDDLE))
    late_out = send(late, OUTWARD)

    low_own = ((early, 0, 0), (late_out, 0, 0))
    low_partner = ((late, 0, 0), (early_out, 0, 0))
    low_mid = ((early, 64, 0), (early_out, 64, 0))
    low_far = ((late, 64, 0), (late_out, 64, 0))

    x_mid = finish(meta, 1, [(r_near, BLOCK, BLOCK)], low_mid, r_near, 2)
    home_mid = send(x_mid, MIDDLE)
    x_mid_o = finish(meta, 0, [(r_third, 0, BLOCK)], low_mid, r_near, 2)
    to_mid = send(x_mid_o, INWARD)
    x_far = finish(meta, 1, [(r_third, 0, BLOCK)], low_far, r_near, 3)
    home_far = send(x_far, ACROSS)
    x_partner = finish(meta, None, [(r_near, 0, BLOCK)], low_partner, r_near, 1)
    home_partner = send(x_partner, XOR[1])
    x_far_o = finish(meta, 0, [(r_fifth, 0, BLOCK)], low_far, r_near, 3)
    to_far = send(x_far_o, INWARD)
    home_rest_f = send(finish(meta, 1, [(r_fifth, 0, BLOCK)], more=to_far), ACROSS)
    home_rest_m = send(finish(meta, 1, [(r_sixth, 0, BLOCK)], more=to_mid), MIDDLE)
    x_own = finish(meta, None, [(r_own, 0, BLOCK)], low_own, r_near, 0)
    count = lax.dynamic_slice_in_dim(block_rows, t, 1, 0)
    return assemble(
        meta, count, x_own, home_partner, [[home_mid], [home_rest_m], [home_far], [home_rest_f]]
    )


def solution(mesh):
    in_specs = (
        P("pool", "tensor"),
        P("tensor", "pool"),
        P("pool", "tensor", None),
        P("pool", "tensor", None),
        P("pool"),
        P("pool"),
    )
    out_specs = P(("pool", "tensor"), None)
    body = line_of_four if dict(mesh.shape) == {"pool": 8, "tensor": 4} else general
    return jax.shard_map(body, mesh=mesh, in_specs=in_specs, out_specs=out_specs, check_vma=False)
```

```python
import functools

import jax
import jax.numpy as jnp
from jax import lax
from jax.experimental import pallas as pl
from jax.experimental.pallas import tpu as pltpu
from jax.sharding import PartitionSpec as P

BLOCK = 128
SCALE = 0.5


def general(hidden, down_weight, adapter_shrink, adapter_expand, block_adapter, block_rows):
    input_rows, feat = hidden.shape
    block_count = block_adapter.shape[0]
    column_span = adapter_expand.shape[1]
    tensor_pos = lax.axis_index("tensor")
    tensor_count = lax.axis_size("tensor")
    own_rows = input_rows // tensor_count
    blocks = hidden.reshape(block_count, BLOCK, feat)
    partial_value = jnp.dot(
        hidden,
        lax.all_gather(down_weight, "pool", axis=1, tiled=True),
        preferred_element_type=jnp.float32,
    )
    total = lax.psum_scatter(
        partial_value.astype(jnp.bfloat16), "tensor", scatter_dimension=0, tiled=True
    ).astype(jnp.float32)
    shrink_piece = lax.all_gather(adapter_shrink, "pool", axis=0, tiled=True)
    expand_piece = lax.all_gather(adapter_expand, "pool", axis=0, tiled=True)
    idents = jnp.arange(shrink_piece.shape[0], dtype=jnp.int32)
    pick = (block_adapter[:, None] == idents[None, :]).astype(jnp.bfloat16)
    first = jnp.einsum("bk,kfr->bfr", pick, shrink_piece, preferred_element_type=jnp.float32)
    second = jnp.einsum("bk,kcr->bcr", pick, expand_piece, preferred_element_type=jnp.float32)
    shrink = jnp.einsum(
        "bnf,bfr->bnr", blocks, first.astype(jnp.bfloat16), preferred_element_type=jnp.float32
    )
    summed_shrink = lax.psum(shrink.astype(jnp.bfloat16), "tensor")
    enlarged_rows = jnp.einsum(
        "bnr,bcr->bnc",
        summed_shrink,
        second.astype(jnp.bfloat16),
        preferred_element_type=jnp.float32,
    )
    adapter_delta_columns = (
        (SCALE * enlarged_rows).astype(jnp.bfloat16).reshape(input_rows, column_span)
    )
    delta_mine = lax.all_to_all(
        adapter_delta_columns, "tensor", split_axis=0, concat_axis=1, tiled=True
    )
    total = total + delta_mine.astype(jnp.float32)
    row_ids = tensor_pos * own_rows + jnp.arange(own_rows, dtype=jnp.int32)
    owning = (row_ids // BLOCK)[:, None] == jnp.arange(block_count, dtype=jnp.int32)[None, :]
    lengths = jnp.sum(jnp.where(owning, block_rows[None, :], 0), axis=1)
    valid = (row_ids % BLOCK < lengths).astype(jnp.float32)
    return (total * valid[:, None]).astype(jnp.bfloat16)


def dot(a, b):
    return jnp.dot(a, b, preferred_element_type=jnp.float32)


def on_line(pairs):
    return [(2 * a + c, 2 * b + c) for a, b in pairs for c in range(2)]


XOR = {s: on_line([(z, z ^ s) for z in range(4)]) for s in (1, 2, 3)}
MIDDLE = on_line([(1, 2), (2, 1)])
OUTWARD = on_line([(1, 0), (2, 3)])
INWARD = on_line([(0, 1), (3, 2)])
ACROSS = on_line([(1, 3), (2, 0)])
SIBLING = [(p, p ^ 1) for p in range(8)]

TILE = 512
NEAR = 3 * TILE
WIDE = 2048
SHARE = 512
INNER, CORE, ZPOS, NAMES = 0, 1, 2, 3
CHEAP = pl.CostEstimate(flops=1000, bytes_accessed=1000, transcendentals=0)


def send(x, pairs):
    return lax.ppermute(x, "pool", pairs)


def after(events, *xs):
    tied = lax.optimization_barrier((tuple(events), xs))
    return tied[1] if len(xs) > 1 else tied[1][0]


def params(limit):
    return pltpu.CompilerParams(vmem_limit_bytes=limit * 1024 * 1024)


class Rows:
    def __init__(self, parts, role, at, shrink=False):
        self.parts, self.role, self.at, self.shrink = parts, role, at, shrink
        self.rows = parts[0][0].shape[0]
        self.total = sum(part[2] for part in parts)


def block_sums(meta, slot, low, start, count, b):
    name = meta[NAMES + 4 * slot + b]
    chip = name >> 2
    place = ((((name >> 1) & 1) ^ meta[CORE]) << 2) + jnp.where(chip == meta[ZPOS], 0, 2) + (name & 1)
    place = jnp.where((chip == meta[ZPOS]) | (chip == (meta[ZPOS] ^ 1)), place, -1)
    value = jnp.zeros((count, 64), jnp.float32)
    for i in range(8):
        part = low[start + b * count : start + (b + 1) * count, i * 64 : i * 64 + 64]
        value = value + jnp.where(place == i, part, 0.0)
    return value.astype(jnp.bfloat16)


def accumulate(ref, rows, cols, value, k, first):
    if first:
        value = value + jnp.where(k == 0, 0.0, ref[rows, cols])
    else:
        value = value + ref[rows, cols]
    ref[rows, cols] = value


def times_transposed(x, a):
    return lax.dot_general(x, a, (((1,), (1,)), ((), ())), preferred_element_type=jnp.float32)


def products_kernel(jobs, weights, shrink, pick, meta, *refs):
    refs = list(refs)
    xs = [[refs.pop(0) for _ in job.parts] for job in jobs]
    ws = [(refs.pop(0), refs.pop(0)) for _ in range(weights)]
    if shrink:
        adapters, sums = (refs.pop(0), refs.pop(0)), refs.pop(0)
    held = (refs.pop(0), refs.pop(0)) if pick else ()
    out, acc = refs[:2]
    low = refs[2] if shrink else None
    k = pl.program_id(0)
    z, c = meta[ZPOS], meta[CORE]
    inner = meta[INNER] == 1

    def choose():
        for b in range(4):
            for slot in range(4):
                name = meta[NAMES + 4 * slot + b]
                index = 2 * ((name >> 2) ^ z) + (name & 1)
                value = jnp.where(((name >> 1) & 1) == c, held[0][index], held[1][index])
                out[b, slot * 64 : slot * 64 + 64, WIDE : WIDE + SHARE] = value

    if pick:
        pl.when(k == 0)(choose)
    if shrink:

        @pl.when(k == 0)
        def _():
            out[:, :, WIDE : WIDE + 256] = sums[...]

    top = {0: 0, 1: 0}
    for x_parts, job in zip(xs, jobs):
        start = max(top.values()) if job.role is None else top[job.role]
        for role in top if job.role is None else (job.role,):
            top[role] = start + job.rows
        mine = slice(start, start + job.rows)
        role = True if job.role is None else meta[INNER] == job.role
        base = 0
        for x, (_, _, tiles, weight) in zip(x_parts, job.parts):

            def step(x=x, mine=mine, pair=ws[weight], first=base == 0):
                for h, w in enumerate(pair):
                    for n in range(0, WIDE // 2, 512):
                        at = slice(h * (WIDE // 2) + n, h * (WIDE // 2) + n + 512)
                        accumulate(acc, mine, at, dot(x[...], w[:, n : n + 512]), k, first)

            def shrink_step(x=x, mine=mine, first=base == 0):
                for h, a in enumerate(adapters):
                    accumulate(low, mine, slice(h * 256, h * 256 + 256), times_transposed(x[...], a[...]), k, first)

            now = (k >= base) & (k < base + tiles)
            pl.when(role & now)(step)
            if job.shrink:
                pl.when(inner & now)(shrink_step)
            base += tiles

        def store(job=job, start=start):
            count = job.rows // 4
            for b in range(4):
                value = acc[start + b * count : start + (b + 1) * count, :]
                out[b, job.at : job.at + count, :WIDE] = value.astype(jnp.bfloat16)

        def shrink_store(job=job, start=start):
            count = job.rows // 4
            for b in range(4):
                out[b, job.at : job.at + count, WIDE + 192 : WIDE + 256] = block_sums(meta, 3, low, start, count, b)

        pl.when(role & (k == job.total - 1))(store)
        if job.shrink:
            pl.when(inner & (k == job.total - 1))(shrink_store)


def products(meta, jobs, weights, rows, shrink=(), held=()):
    steps = max(job.total for job in jobs)
    in_specs, args, uses = [], [], {}
    for job in jobs:
        base = 0
        for x, tile, tiles, weight in job.parts:

            def index(k, m, base=base, tile=tile, tiles=tiles, role=job.role):
                at = jnp.clip(k - base, 0, tiles - 1)
                if role is not None:
                    at = at * (m[INNER] if role == 1 else 1 - m[INNER])
                return (0, at + tile)

            in_specs.append(pl.BlockSpec((x.shape[0], TILE), index))
            args.append(x)
            for role in (0, 1) if job.role is None else (job.role,):
                uses[weight, role] = (base, tiles)
            base += tiles
    for i, (own, own_tile, other, other_tile) in enumerate(weights):
        for w, tile in ((own, own_tile), (other, other_tile)):

            def index(k, m, i=i, tile=tile):
                at = [jnp.clip(k - base, 0, tiles - 1) for base, tiles in (uses.get((i, r), (0, 1)) for r in (0, 1))]
                return (jnp.where(m[INNER] == 1, at[1], at[0]) + tile, 0)

            in_specs.append(pl.BlockSpec((TILE, w.shape[1]), index))
            args.append(w)
    if shrink:
        for a in shrink[:2]:
            in_specs.append(pl.BlockSpec((a.shape[0], TILE), lambda k, m: (0, k * m[INNER])))
            args.append(a)
        in_specs.append(pl.BlockSpec(shrink[2].shape, lambda k, m: (0, 0, 0)))
        args.append(shrink[2])
    for a in held:
        in_specs.append(pl.BlockSpec(a.shape, lambda k, m: (0, 0, 0)))
        args.append(a)
    both = sum(job.rows for job in jobs if job.role is None)
    height = both + max(sum(job.rows for job in jobs if job.role == r) for r in (0, 1))
    scratch = [pltpu.VMEM((height, WIDE), jnp.float32)]
    if shrink:
        scratch.append(pltpu.VMEM((height, 512), jnp.float32))
    shape = (4, rows, WIDE + (256 if shrink else 0) + (SHARE if held else 0))
    return pl.pallas_call(
        functools.partial(products_kernel, jobs, len(weights), bool(shrink), bool(held)),
        grid_spec=pltpu.PrefetchScalarGridSpec(
            num_scalar_prefetch=1,
            grid=(steps,),
            in_specs=in_specs,
            out_specs=pl.BlockSpec(shape, lambda k, m: (0, 0, 0)),
            scratch_shapes=scratch,
        ),
        out_shape=jax.ShapeDtypeStruct(shape, jnp.bfloat16),
        compiler_params=params(50),
        cost_estimate=CHEAP,
    )(meta, *args)


def shrink_kernel(tiles, slots, steps, meta, *refs):
    refs = list(refs)
    xs = [[refs.pop(0) for _ in part] for part in tiles]
    mine, other, out, low = refs
    k = pl.program_id(0)
    inner = meta[INNER] == 1
    rows = BLOCK * 4
    for i, x_parts in enumerate(xs):
        base = 0
        for x, count in zip(x_parts, tiles[i]):

            @pl.when(inner & (k >= base) & (k < base + count))
            def _(i=i, x=x, first=base == 0):
                here = slice(i * rows, (i + 1) * rows)
                for h, a in enumerate((mine, other)):
                    accumulate(low, here, slice(h * 256, h * 256 + 256), times_transposed(x[...], a[...]), k, first)

            base += count

    @pl.when(inner & (k == steps - 1))
    def _():
        for i, slot in enumerate(slots):
            for b in range(4):
                out[b, :, i * 64 : i * 64 + 64] = block_sums(meta, slot, low, i * rows, BLOCK, b)


def shrink_sums(meta, xs, slots, mine, other):
    tiles = [[part.shape[1] // TILE for part in x] for x in xs]
    steps = sum(tiles[0])
    in_specs, args = [], []
    for x, counts in zip(xs, tiles):
        base = 0
        for part, count in zip(x, counts):

            def index(k, m, base=base, count=count):
                return (0, jnp.clip(k - base, 0, count - 1) * m[INNER])

            in_specs.append(pl.BlockSpec((part.shape[0], TILE), index))
            args.append(part)
            base += count
    for a in (mine, other):
        in_specs.append(pl.BlockSpec((a.shape[0], TILE), lambda k, m: (0, k * m[INNER])))
        args.append(a)
    return pl.pallas_call(
        functools.partial(shrink_kernel, tiles, slots, steps),
        grid_spec=pltpu.PrefetchScalarGridSpec(
            num_scalar_prefetch=1,
            grid=(steps,),
            in_specs=in_specs,
            out_specs=pl.BlockSpec((4, BLOCK, 256), lambda k, m: (0, 0, 0)),
            scratch_shapes=[pltpu.VMEM((4 * BLOCK * len(xs), 512), jnp.float32)],
        ),
        out_shape=jax.ShapeDtypeStruct((4, BLOCK, 256), jnp.bfloat16),
        compiler_params=params(40),
        cost_estimate=CHEAP,
    )(meta, *args)


def low_kernel(x, out, swapped):
    value = x[0].astype(jnp.float32)
    for b in range(1, 4):
        value = value + x[b].astype(jnp.float32)
    value = value.astype(jnp.bfloat16)
    out[...] = value
    swapped[...] = jnp.concatenate([value[:, i * 64 : i * 64 + 64] for i in (1, 0, 3, 2)], axis=1)


def low_sums(x):
    shape = jax.ShapeDtypeStruct((BLOCK, 256), jnp.bfloat16)
    whole = pl.BlockSpec((BLOCK, 256), lambda i: (0, 0))
    return pl.pallas_call(
        low_kernel,
        grid=(1,),
        in_specs=[pl.BlockSpec((4, BLOCK, 256), lambda i: (0, 0, WIDE // 256))],
        out_specs=(whole, whole),
        out_shape=(shape, shape),
        cost_estimate=CHEAP,
    )(x)


def add_kernel(x, y, out):
    out[...] = (x[...].astype(jnp.float32) + y[...].astype(jnp.float32)).astype(jnp.bfloat16)


def add(x, y):
    return pl.pallas_call(add_kernel, out_shape=jax.ShapeDtypeStruct(x.shape, x.dtype), cost_estimate=CHEAP)(x, y)


def finish_kernel(role, row, rows, lanes, has_more, meta, *refs):
    refs = list(refs)
    part = refs.pop(0)
    if lanes:
        low_in, low_out, expand = refs.pop(0), refs.pop(0), refs.pop(0)
    more = refs.pop(0) if has_more else None
    out = refs.pop(0)

    def run():
        total = part[0, row : row + rows, :].astype(jnp.float32)
        for b in range(1, 4):
            total = total + part[b, row : row + rows, :].astype(jnp.float32)
        if lanes:
            x = low_in[:rows, lanes[0] : lanes[0] + 64]
            y = low_out[:rows, lanes[1] : lanes[1] + 64]
            x = jnp.where(meta[INNER] == 1, x, y)
            delta = [dot(x, expand[i]) for i in range(expand.shape[0])]
            total = total + SCALE * jnp.concatenate(delta, axis=1)
        if has_more:
            total = total + more[...].astype(jnp.float32)
        out[...] = total.astype(jnp.bfloat16)

    if role is None:
        run()
    else:
        pl.when(meta[INNER] == role)(run)


def finish(meta, role, part, row, low=None, more=None, rows=BLOCK):
    span = WIDE // 2
    in_specs = [pl.BlockSpec((4, part.shape[1], span), lambda h, m: (0, 0, h))]
    args = [part]
    lanes = None
    if low is not None:
        *sums, expand, slots = low
        for x in sums:
            in_specs.append(pl.BlockSpec(x.shape, lambda h, m: (0, 0)))
            args.append(x)
        in_specs.append(
            pl.BlockSpec(
                (span // SHARE, 64, SHARE),
                lambda h, m: (h ^ m[CORE], slots[1] + (slots[0] - slots[1]) * m[INNER], WIDE // SHARE),
            )
        )
        args.append(expand)
        lanes = [64 * (0, 2, 1, 3)[slots[0]], 64 * (2, 0, 1, 3)[slots[1]]]
    if more is not None:
        in_specs.append(pl.BlockSpec((rows, span), lambda h, m: (0, h)))
        args.append(more)
    return pl.pallas_call(
        functools.partial(finish_kernel, role, row, rows, lanes, more is not None),
        grid_spec=pltpu.PrefetchScalarGridSpec(
            num_scalar_prefetch=1,
            grid=(2,),
            in_specs=in_specs,
            out_specs=pl.BlockSpec((rows, span), lambda h, m: (0, h)),
        ),
        out_shape=jax.ShapeDtypeStruct((rows, WIDE), jnp.bfloat16),
        compiler_params=params(32),
        cost_estimate=CHEAP,
    )(meta, *args)


def assemble_kernel(span, meta, count, own, one, two, inner_three, outer_three, out):
    z, c, inner = meta[ZPOS], meta[CORE], meta[INNER] == 1
    rows = own.shape[0]
    valid = lax.broadcasted_iota(jnp.int32, (rows, 1), 0) < count[0]

    def put(j, source):
        for h in range(2):
            at = pl.ds(pl.multiple_of((2 * j + h) * span, span), span)
            part = pl.ds(pl.multiple_of((h ^ c) * span, span), span)
            out[:, at] = jnp.where(valid, source[:, part], jnp.zeros((), jnp.bfloat16))

    put(z, own)
    put(z ^ 1, one)
    put(z ^ 2, two)

    @pl.when(inner)
    def _():
        put(z ^ 3, inner_three)

    @pl.when(jnp.logical_not(inner))
    def _():
        put(z ^ 3, outer_three)


def assemble(meta, count, *args):
    rows, wide = args[0].shape
    return pl.pallas_call(
        functools.partial(assemble_kernel, wide // 2),
        grid_spec=pltpu.PrefetchScalarGridSpec(
            num_scalar_prefetch=2,
            grid=(1,),
            in_specs=[pl.BlockSpec(a.shape, lambda n, m, k: (0, 0)) for a in args],
            out_specs=pl.BlockSpec((rows, 4 * wide), lambda n, m, k: (0, 0)),
        ),
        out_shape=jax.ShapeDtypeStruct((rows, 4 * wide), jnp.bfloat16),
        compiler_params=params(32),
        cost_estimate=CHEAP,
    )(meta, count, *args)


def line_of_four(hidden, down_weight, adapter_shrink, adapter_expand, block_adapter, block_rows):
    rows, feat = hidden.shape
    adp, _, rank = adapter_shrink.shape
    p = lax.axis_index("pool")
    t = lax.axis_index("tensor")
    tensors = lax.axis_size("tensor")
    z, c = p // 2, p % 2
    outer = (z == 0) | (z == 3)

    def exchange(x):
        return lax.all_to_all(x, "tensor", split_axis=0, concat_axis=0, tiled=True)

    place = jnp.stack([jnp.where(outer, 0, 1), c, z]).astype(jnp.int32)

    mid = send(hidden, MIDDLE)
    partner = send(hidden, XOR[1])
    cuts = [(0, NEAR), (NEAR, NEAR + 2 * TILE), (NEAR + 2 * TILE, feat)]
    pieces = [down_weight[lo:hi] for lo, hi in cuts]
    others = [send(w, SIBLING) for w in pieces]
    weights = [(down_weight, lo // TILE, w, 0) for (lo, _), w in zip(cuts, others)]

    def whole(x):
        return [(x, lo // TILE, (hi - lo) // TILE, i) for i, (lo, hi) in enumerate(cuts)]

    shares = exchange(
        adapter_expand.transpose(0, 2, 1).reshape(adp, rank, tensors, SHARE).transpose(2, 0, 1, 3)
    ).reshape(tensors, adp * rank, SHARE)
    label = jnp.zeros((16, SHARE), jnp.bfloat16).at[0, : block_adapter.shape[0]].set(block_adapter.astype(jnp.bfloat16))

    def shares_of(s):
        return lax.dynamic_index_in_dim(shares, z ^ s, 0, keepdims=False)

    told = [send(jnp.concatenate([shares_of(s), label], axis=0), XOR[s]) for s in (1, 2, 3)]
    j_own = products(place, [Rows(whole(hidden), None, 0)], weights, BLOCK)

    ready = [partner, mid, j_own, *told]
    far = send(after(ready, partner), MIDDLE)
    out_mid = send(after(ready, mid), OUTWARD)
    shrink_w = after([partner, mid], adapter_shrink.transpose(0, 2, 1).reshape(adp * rank, feat))
    shrink_o = send(shrink_w, INWARD)
    v_own = [send(after([partner, mid], w), INWARD) for w in pieces[1:]]

    names = [block_adapter] + [x[adp * rank, : block_adapter.shape[0]].astype(jnp.int32) for x in told]
    name_m = jnp.where(outer, names[2], names[3])
    name_f = jnp.where(outer, names[3], names[2])
    meta = jnp.concatenate([place, names[0], names[1], name_m, name_f])
    held = jnp.concatenate([shares_of(0)] + [x[: adp * rank] for x in told]).reshape(4 * adp, rank, SHARE)
    held = (held, send(held, SIBLING))
    j_near = products(
        meta, [Rows(whole(partner), None, 0), Rows(whole(mid), 1, BLOCK)], weights, 2 * BLOCK, held=held
    )
    r_near = exchange(j_near)

    shrink_mine = jnp.concatenate([shrink_w, after([j_near], shrink_o)], axis=0)
    shrink_other = send(shrink_mine, SIBLING)
    sums = shrink_sums(meta, [[hidden], [mid], [partner]], [0, 2, 1], shrink_mine, shrink_other)

    far_near = far[:, :NEAR]
    out_far = send(after([out_mid], far_near), OUTWARD)
    j_third = products(
        meta,
        [Rows(whole(after([r_near, far_near, sums], far)), 1, 0, True), Rows(whole(out_mid), 0, 0)],
        weights,
        BLOCK,
        (shrink_mine, shrink_other, sums),
    )
    r_third = exchange(j_third)
    v_other = [send(after([j_third], w), SIBLING) for w in v_own]

    low, swapped = low_sums(r_third)
    low = add(low, send(swapped, MIDDLE))
    low_out = send(low, OUTWARD)

    rest = [(a, 0, b, 0) for a, b in zip(v_own, v_other)] + weights[:1]
    j_fifth = products(
        meta,
        [
            Rows([(after([j_third], far), 3, 2, 0), (far, 5, 2, 1)], 1, 0),
            Rows([(out_far, 0, 3, 2)], 0, 0),
        ],
        rest,
        BLOCK,
    )
    r_fifth = exchange(j_fifth)
    r_own = exchange(j_own)

    def term(inner_slot, outer_slot):
        return (low, low_out, r_near, (inner_slot, outer_slot))

    x_two = finish(meta, None, r_third, 0, term(3, 2))
    home_two = send(x_two, XOR[2])
    x_mid = finish(meta, 1, r_near, BLOCK, term(2, 2))
    home_mid = send(x_mid, MIDDLE)
    x_partner = finish(meta, None, r_near, 0, term(1, 1))
    home_partner = send(x_partner, XOR[1])
    x_far = finish(meta, 0, r_fifth, 0, term(3, 3))
    to_far = send(x_far, INWARD)
    home_far = send(finish(meta, 1, r_fifth, 0, more=to_far), ACROSS)
    x_own = finish(meta, None, r_own, 0, term(0, 0))
    count = lax.dynamic_slice_in_dim(block_rows, t, 1, 0)
    return assemble(meta, count, x_own, home_partner, home_two, home_mid, home_far)


def solution(mesh):
    in_specs = (
        P("pool", "tensor"),
        P("tensor", "pool"),
        P("pool", "tensor", None),
        P("pool", "tensor", None),
        P("pool"),
        P("pool"),
    )
    out_specs = P(("pool", "tensor"), None)
    body = line_of_four if dict(mesh.shape) == {"pool": 8, "tensor": 4} else general
    return jax.shard_map(body, mesh=mesh, in_specs=in_specs, out_specs=out_specs, check_vma=False)
```

```python
import functools

import jax
import jax.numpy as jnp
from jax import lax
from jax.experimental import pallas as pl
from jax.experimental.pallas import tpu as pltpu
from jax.sharding import PartitionSpec as P

BLOCK = 128
SCALE = 0.5


def general(hidden, down_weight, adapter_shrink, adapter_expand, block_adapter, block_rows):
    input_rows, feat = hidden.shape
    block_count = block_adapter.shape[0]
    column_span = adapter_expand.shape[1]
    tensor_pos = lax.axis_index("tensor")
    tensor_count = lax.axis_size("tensor")
    own_rows = input_rows // tensor_count
    blocks = hidden.reshape(block_count, BLOCK, feat)
    partial_value = jnp.dot(
        hidden,
        lax.all_gather(down_weight, "pool", axis=1, tiled=True),
        preferred_element_type=jnp.float32,
    )
    total = lax.psum_scatter(
        partial_value.astype(jnp.bfloat16), "tensor", scatter_dimension=0, tiled=True
    ).astype(jnp.float32)
    shrink_piece = lax.all_gather(adapter_shrink, "pool", axis=0, tiled=True)
    expand_piece = lax.all_gather(adapter_expand, "pool", axis=0, tiled=True)
    idents = jnp.arange(shrink_piece.shape[0], dtype=jnp.int32)
    pick = (block_adapter[:, None] == idents[None, :]).astype(jnp.bfloat16)
    first = jnp.einsum("bk,kfr->bfr", pick, shrink_piece, preferred_element_type=jnp.float32)
    second = jnp.einsum("bk,kcr->bcr", pick, expand_piece, preferred_element_type=jnp.float32)
    shrink = jnp.einsum(
        "bnf,bfr->bnr", blocks, first.astype(jnp.bfloat16), preferred_element_type=jnp.float32
    )
    summed_shrink = lax.psum(shrink.astype(jnp.bfloat16), "tensor")
    enlarged_rows = jnp.einsum(
        "bnr,bcr->bnc",
        summed_shrink,
        second.astype(jnp.bfloat16),
        preferred_element_type=jnp.float32,
    )
    adapter_delta_columns = (
        (SCALE * enlarged_rows).astype(jnp.bfloat16).reshape(input_rows, column_span)
    )
    delta_mine = lax.all_to_all(
        adapter_delta_columns, "tensor", split_axis=0, concat_axis=1, tiled=True
    )
    total = total + delta_mine.astype(jnp.float32)
    row_ids = tensor_pos * own_rows + jnp.arange(own_rows, dtype=jnp.int32)
    owning = (row_ids // BLOCK)[:, None] == jnp.arange(block_count, dtype=jnp.int32)[None, :]
    lengths = jnp.sum(jnp.where(owning, block_rows[None, :], 0), axis=1)
    valid = (row_ids % BLOCK < lengths).astype(jnp.float32)
    return (total * valid[:, None]).astype(jnp.bfloat16)


def dot(a, b):
    return jnp.dot(a, b, preferred_element_type=jnp.float32)


def on_line(pairs):
    return [(2 * a + c, 2 * b + c) for a, b in pairs for c in range(2)]


XOR = {s: on_line([(z, z ^ s) for z in range(4)]) for s in (1, 2, 3)}
MIDDLE = on_line([(1, 2), (2, 1)])
OUTWARD = on_line([(1, 0), (2, 3)])
INWARD = on_line([(0, 1), (3, 2)])
ACROSS = on_line([(1, 3), (2, 0)])
SIBLING = [(p, p ^ 1) for p in range(8)]
LINES = [[2 * z + c for z in range(4)] for c in range(2)]

TILE = 512
NEAR = 3 * TILE
WIDE = 2048
SHARE = 512
INNER, CORE, ZPOS, NAMES = 0, 1, 2, 3
CHEAP = pl.CostEstimate(flops=1000, bytes_accessed=1000, transcendentals=0)


def send(x, pairs):
    return lax.ppermute(x, "pool", pairs)


def after(events, *xs):
    tied = lax.optimization_barrier((tuple(events), xs))
    return tied[1] if len(xs) > 1 else tied[1][0]


def params(limit):
    return pltpu.CompilerParams(vmem_limit_bytes=limit * 1024 * 1024)


class Rows:
    def __init__(self, parts, role, at, shrink=False):
        self.parts, self.role, self.at, self.shrink = parts, role, at, shrink
        self.rows = parts[0][0].shape[0]
        self.total = sum(part[2] for part in parts)


def block_sums(meta, slot, low, start, count, b):
    name = meta[NAMES + 4 * slot + b]
    chip = name >> 2
    place = ((((name >> 1) & 1) ^ meta[CORE]) << 2) + jnp.where(chip == meta[ZPOS], 0, 2) + (name & 1)
    place = jnp.where((chip == meta[ZPOS]) | (chip == (meta[ZPOS] ^ 1)), place, -1)
    value = jnp.zeros((count, 64), jnp.float32)
    for i in range(8):
        part = low[start + b * count : start + (b + 1) * count, i * 64 : i * 64 + 64]
        value = value + jnp.where(place == i, part, 0.0)
    return value.astype(jnp.bfloat16)


def accumulate(ref, rows, cols, value, k, first):
    if first:
        value = value + jnp.where(k == 0, 0.0, ref[rows, cols])
    else:
        value = value + ref[rows, cols]
    ref[rows, cols] = value


def times_transposed(x, a):
    return lax.dot_general(x, a, (((1,), (1,)), ((), ())), preferred_element_type=jnp.float32)


def products_kernel(jobs, weights, shrink, pick, meta, *refs):
    refs = list(refs)
    xs = [[refs.pop(0) for _ in job.parts] for job in jobs]
    ws = [(refs.pop(0), refs.pop(0)) for _ in range(weights)]
    if shrink:
        adapters, sums = (refs.pop(0), refs.pop(0)), refs.pop(0)
    held = (refs.pop(0), refs.pop(0)) if pick else ()
    out, acc = refs[:2]
    low = refs[2] if shrink else None
    k = pl.program_id(0)
    z, c = meta[ZPOS], meta[CORE]
    inner = meta[INNER] == 1

    def choose():
        for b in range(4):
            for slot in range(4):
                name = meta[NAMES + 4 * slot + b]
                index = 2 * (name >> 2) + (name & 1)
                value = jnp.where(((name >> 1) & 1) == c, held[0][index], held[1][index])
                out[b, slot * 64 : slot * 64 + 64, WIDE : WIDE + SHARE] = value

    if pick:
        pl.when(k == 0)(choose)
    if shrink:

        @pl.when(k == 0)
        def _():
            out[:, :, WIDE : WIDE + 256] = sums[...]

    top = {0: 0, 1: 0}
    for x_parts, job in zip(xs, jobs):
        start = max(top.values()) if job.role is None else top[job.role]
        for role in top if job.role is None else (job.role,):
            top[role] = start + job.rows
        mine = slice(start, start + job.rows)
        role = True if job.role is None else meta[INNER] == job.role
        base = 0
        for x, (_, _, tiles, weight) in zip(x_parts, job.parts):

            def step(x=x, mine=mine, pair=ws[weight], first=base == 0):
                for h, w in enumerate(pair):
                    for n in range(0, WIDE // 2, 512):
                        at = slice(h * (WIDE // 2) + n, h * (WIDE // 2) + n + 512)
                        accumulate(acc, mine, at, dot(x[...], w[:, n : n + 512]), k, first)

            def shrink_step(x=x, mine=mine, first=base == 0):
                for h, a in enumerate(adapters):
                    accumulate(low, mine, slice(h * 256, h * 256 + 256), times_transposed(x[...], a[...]), k, first)

            now = (k >= base) & (k < base + tiles)
            pl.when(role & now)(step)
            if job.shrink:
                pl.when(inner & now)(shrink_step)
            base += tiles

        def store(job=job, start=start):
            count = job.rows // 4
            for b in range(4):
                value = acc[start + b * count : start + (b + 1) * count, :]
                out[b, job.at : job.at + count, :WIDE] = value.astype(jnp.bfloat16)

        def shrink_store(job=job, start=start):
            count = job.rows // 4
            for b in range(4):
                out[b, job.at : job.at + count, WIDE + 192 : WIDE + 256] = block_sums(meta, 3, low, start, count, b)

        pl.when(role & (k == job.total - 1))(store)
        if job.shrink:
            pl.when(inner & (k == job.total - 1))(shrink_store)


def products(meta, jobs, weights, rows, shrink=(), held=()):
    steps = max(job.total for job in jobs)
    in_specs, args, uses = [], [], {}
    for job in jobs:
        base = 0
        for x, tile, tiles, weight in job.parts:

            def index(k, m, base=base, tile=tile, tiles=tiles, role=job.role):
                at = jnp.clip(k - base, 0, tiles - 1)
                if role is not None:
                    at = at * (m[INNER] if role == 1 else 1 - m[INNER])
                return (0, at + tile)

            in_specs.append(pl.BlockSpec((x.shape[0], TILE), index))
            args.append(x)
            for role in (0, 1) if job.role is None else (job.role,):
                uses[weight, role] = (base, tiles)
            base += tiles
    for i, (own, own_tile, other, other_tile) in enumerate(weights):
        for w, tile in ((own, own_tile), (other, other_tile)):

            def index(k, m, i=i, tile=tile):
                at = [jnp.clip(k - base, 0, tiles - 1) for base, tiles in (uses.get((i, r), (0, 1)) for r in (0, 1))]
                return (jnp.where(m[INNER] == 1, at[1], at[0]) + tile, 0)

            in_specs.append(pl.BlockSpec((TILE, w.shape[1]), index))
            args.append(w)
    if shrink:
        for a in shrink[:2]:
            in_specs.append(pl.BlockSpec((a.shape[0], TILE), lambda k, m: (0, k * m[INNER])))
            args.append(a)
        in_specs.append(pl.BlockSpec(shrink[2].shape, lambda k, m: (0, 0, 0)))
        args.append(shrink[2])
    for a in held:
        in_specs.append(pl.BlockSpec(a.shape, lambda k, m: (0, 0, 0)))
        args.append(a)
    both = sum(job.rows for job in jobs if job.role is None)
    height = both + max(sum(job.rows for job in jobs if job.role == r) for r in (0, 1))
    scratch = [pltpu.VMEM((height, WIDE), jnp.float32)]
    if shrink:
        scratch.append(pltpu.VMEM((height, 512), jnp.float32))
    shape = (4, rows, WIDE + (256 if shrink else 0) + (SHARE if held else 0))
    return pl.pallas_call(
        functools.partial(products_kernel, jobs, len(weights), bool(shrink), bool(held)),
        grid_spec=pltpu.PrefetchScalarGridSpec(
            num_scalar_prefetch=1,
            grid=(steps,),
            in_specs=in_specs,
            out_specs=pl.BlockSpec(shape, lambda k, m: (0, 0, 0)),
            scratch_shapes=scratch,
        ),
        out_shape=pltpu.HBM(shape, jnp.bfloat16),
        compiler_params=params(50),
        cost_estimate=CHEAP,
    )(meta, *args)


def shrink_kernel(tiles, slots, steps, meta, *refs):
    refs = list(refs)
    xs = [[refs.pop(0) for _ in part] for part in tiles]
    mine, other, out, low = refs
    k = pl.program_id(0)
    inner = meta[INNER] == 1
    rows = BLOCK * 4
    for i, x_parts in enumerate(xs):
        base = 0
        for x, count in zip(x_parts, tiles[i]):

            @pl.when(inner & (k >= base) & (k < base + count))
            def _(i=i, x=x, first=base == 0):
                here = slice(i * rows, (i + 1) * rows)
                for h, a in enumerate((mine, other)):
                    accumulate(low, here, slice(h * 256, h * 256 + 256), times_transposed(x[...], a[...]), k, first)

            base += count

    @pl.when(inner & (k == steps - 1))
    def _():
        for i, slot in enumerate(slots):
            for b in range(4):
                out[b, :, i * 64 : i * 64 + 64] = block_sums(meta, slot, low, i * rows, BLOCK, b)


def shrink_sums(meta, xs, slots, mine, other):
    tiles = [[part.shape[1] // TILE for part in x] for x in xs]
    steps = sum(tiles[0])
    in_specs, args = [], []
    for x, counts in zip(xs, tiles):
        base = 0
        for part, count in zip(x, counts):

            def index(k, m, base=base, count=count):
                return (0, jnp.clip(k - base, 0, count - 1) * m[INNER])

            in_specs.append(pl.BlockSpec((part.shape[0], TILE), index))
            args.append(part)
            base += count
    for a in (mine, other):
        in_specs.append(pl.BlockSpec((a.shape[0], TILE), lambda k, m: (0, k * m[INNER])))
        args.append(a)
    return pl.pallas_call(
        functools.partial(shrink_kernel, tiles, slots, steps),
        grid_spec=pltpu.PrefetchScalarGridSpec(
            num_scalar_prefetch=1,
            grid=(steps,),
            in_specs=in_specs,
            out_specs=pl.BlockSpec((4, BLOCK, 256), lambda k, m: (0, 0, 0)),
            scratch_shapes=[pltpu.VMEM((4 * BLOCK * len(xs), 512), jnp.float32)],
        ),
        out_shape=jax.ShapeDtypeStruct((4, BLOCK, 256), jnp.bfloat16),
        compiler_params=params(40),
        cost_estimate=CHEAP,
    )(meta, *args)


def low_kernel(x, out, swapped):
    value = x[0].astype(jnp.float32)
    for b in range(1, 4):
        value = value + x[b].astype(jnp.float32)
    value = value.astype(jnp.bfloat16)
    out[...] = value
    swapped[...] = jnp.concatenate([value[:, i * 64 : i * 64 + 64] for i in (1, 0, 3, 2)], axis=1)


def low_sums(x):
    shape = jax.ShapeDtypeStruct((BLOCK, 256), jnp.bfloat16)
    whole = pl.BlockSpec((BLOCK, 256), lambda i: (0, 0))
    return pl.pallas_call(
        low_kernel,
        grid=(1,),
        in_specs=[pl.BlockSpec((4, BLOCK, 256), lambda i: (0, 0, WIDE // 256))],
        out_specs=(whole, whole),
        out_shape=(shape, shape),
        cost_estimate=CHEAP,
    )(x)


def add_kernel(x, y, out):
    out[...] = (x[...].astype(jnp.float32) + y[...].astype(jnp.float32)).astype(jnp.bfloat16)


def add(x, y):
    return pl.pallas_call(add_kernel, out_shape=jax.ShapeDtypeStruct(x.shape, x.dtype), cost_estimate=CHEAP)(x, y)


def finish_kernel(role, row, rows, lanes, has_more, meta, *refs):
    refs = list(refs)
    part = refs.pop(0)
    if lanes:
        low_in, low_out, expand = refs.pop(0), refs.pop(0), refs.pop(0)
    more = refs.pop(0) if has_more else None
    out = refs.pop(0)

    def run():
        total = part[0, row : row + rows, :].astype(jnp.float32)
        for b in range(1, 4):
            total = total + part[b, row : row + rows, :].astype(jnp.float32)
        if lanes:
            x = low_in[:rows, lanes[0] : lanes[0] + 64]
            y = low_out[:rows, lanes[1] : lanes[1] + 64]
            x = jnp.where(meta[INNER] == 1, x, y)
            delta = [dot(x, expand[i]) for i in range(expand.shape[0])]
            total = total + SCALE * jnp.concatenate(delta, axis=1)
        if has_more:
            total = total + more[...].astype(jnp.float32)
        out[...] = total.astype(jnp.bfloat16)

    if role is None:
        run()
    else:
        pl.when(meta[INNER] == role)(run)


def finish(meta, role, part, row, low=None, more=None, rows=BLOCK):
    span = WIDE // 2
    in_specs = [pl.BlockSpec((4, part.shape[1], span), lambda h, m: (0, 0, h))]
    args = [part]
    lanes = None
    if low is not None:
        *sums, expand, slots = low
        for x in sums:
            in_specs.append(pl.BlockSpec(x.shape, lambda h, m: (0, 0)))
            args.append(x)
        in_specs.append(
            pl.BlockSpec(
                (span // SHARE, 64, SHARE),
                lambda h, m: (h ^ m[CORE], slots[1] + (slots[0] - slots[1]) * m[INNER], WIDE // SHARE),
            )
        )
        args.append(expand)
        lanes = [64 * (0, 2, 1, 3)[slots[0]], 64 * (2, 0, 1, 3)[slots[1]]]
    if more is not None:
        in_specs.append(pl.BlockSpec((rows, span), lambda h, m: (0, h)))
        args.append(more)
    return pl.pallas_call(
        functools.partial(finish_kernel, role, row, rows, lanes, more is not None),
        grid_spec=pltpu.PrefetchScalarGridSpec(
            num_scalar_prefetch=1,
            grid=(2,),
            in_specs=in_specs,
            out_specs=pl.BlockSpec((rows, span), lambda h, m: (0, h)),
        ),
        out_shape=jax.ShapeDtypeStruct((rows, WIDE), jnp.bfloat16),
        compiler_params=params(32),
        cost_estimate=CHEAP,
    )(meta, *args)


def assemble_kernel(span, meta, count, own, one, two, inner_three, outer_three, out):
    z, c, inner = meta[ZPOS], meta[CORE], meta[INNER] == 1
    rows = own.shape[0]
    valid = lax.broadcasted_iota(jnp.int32, (rows, 1), 0) < count[0]

    def put(j, source):
        for h in range(2):
            at = pl.ds(pl.multiple_of((2 * j + h) * span, span), span)
            part = pl.ds(pl.multiple_of((h ^ c) * span, span), span)
            out[:, at] = jnp.where(valid, source[:, part], jnp.zeros((), jnp.bfloat16))

    put(z, own)
    put(z ^ 1, one)
    put(z ^ 2, two)

    @pl.when(inner)
    def _():
        put(z ^ 3, inner_three)

    @pl.when(jnp.logical_not(inner))
    def _():
        put(z ^ 3, outer_three)


def assemble(meta, count, *args):
    rows, wide = args[0].shape
    return pl.pallas_call(
        functools.partial(assemble_kernel, wide // 2),
        grid_spec=pltpu.PrefetchScalarGridSpec(
            num_scalar_prefetch=2,
            grid=(1,),
            in_specs=[pl.BlockSpec(a.shape, lambda n, m, k: (0, 0)) for a in args],
            out_specs=pl.BlockSpec((rows, 4 * wide), lambda n, m, k: (0, 0)),
        ),
        out_shape=jax.ShapeDtypeStruct((rows, 4 * wide), jnp.bfloat16),
        compiler_params=params(32),
        cost_estimate=CHEAP,
    )(meta, count, *args)


def line_of_four(hidden, down_weight, adapter_shrink, adapter_expand, block_adapter, block_rows):
    rows, feat = hidden.shape
    adp, _, rank = adapter_shrink.shape
    p = lax.axis_index("pool")
    t = lax.axis_index("tensor")
    tensors = lax.axis_size("tensor")
    z, c = p // 2, p % 2
    outer = (z == 0) | (z == 3)

    def exchange(x):
        return lax.all_to_all(x, "tensor", split_axis=0, concat_axis=0, tiled=True)

    place = jnp.stack([jnp.where(outer, 0, 1), c, z]).astype(jnp.int32)

    mid = send(hidden, MIDDLE)
    partner = send(hidden, XOR[1])
    cuts = [(0, NEAR), (NEAR, NEAR + 2 * TILE), (NEAR + 2 * TILE, feat)]
    pieces = [down_weight[lo:hi] for lo, hi in cuts]
    others = [send(w, SIBLING) for w in pieces]
    weights = [(down_weight, lo // TILE, w, 0) for (lo, _), w in zip(cuts, others)]

    def whole(x):
        return [(x, lo // TILE, (hi - lo) // TILE, i) for i, (lo, hi) in enumerate(cuts)]

    shares = exchange(
        adapter_expand.transpose(0, 2, 1).reshape(adp, rank, tensors, SHARE).transpose(2, 0, 1, 3)
    ).reshape(tensors, adp * rank, SHARE)
    label = jnp.zeros((tensors, 16, SHARE), jnp.bfloat16)
    label = label.at[:, 0, : block_adapter.shape[0]].set(block_adapter.astype(jnp.bfloat16))
    told = lax.all_to_all(
        jnp.concatenate([shares, label], axis=1), "pool", 0, 0, axis_index_groups=LINES, tiled=True
    )
    j_own = products(place, [Rows(whole(hidden), None, 0)], weights, BLOCK)

    far = send(after([partner, mid, j_own], partner), MIDDLE)
    out_mid = send(after([partner, mid, j_own], mid), OUTWARD)
    shrink_w = after([partner, mid], adapter_shrink.transpose(0, 2, 1).reshape(adp * rank, feat))
    shrink_o = send(shrink_w, INWARD)
    v_own = [send(after([partner, mid], w), INWARD) for w in pieces[1:]]

    told = after([partner, mid], told)
    held = told[:, : adp * rank].reshape(tensors * adp, rank, SHARE)
    held = (held, send(held, SIBLING))
    names = told[:, adp * rank, : block_adapter.shape[0]].astype(jnp.int32)
    name_m = jnp.where(outer, names[z ^ 2], names[z ^ 3])
    name_f = jnp.where(outer, names[z ^ 3], names[z ^ 2])
    meta = jnp.concatenate([place, block_adapter, names[z ^ 1], name_m, name_f])
    j_partner = products(meta, [Rows(whole(partner), None, 0)], weights, 2 * BLOCK, held=held)
    r_partner = exchange(j_partner)

    shrink_mine = jnp.concatenate([shrink_w, after([j_partner], shrink_o)], axis=0)
    shrink_other = send(shrink_mine, SIBLING)
    sums = shrink_sums(meta, [[hidden], [mid], [partner]], [0, 2, 1], shrink_mine, shrink_other)
    j_mid = products(meta, [Rows(whole(after([j_partner], mid)), 1, 0)], weights, BLOCK)
    r_mid = exchange(j_mid)

    far_near = far[:, :NEAR]
    out_far = send(after([out_mid, j_partner, j_mid, sums], far_near), OUTWARD)
    j_third = products(
        meta,
        [Rows(whole(after([r_partner, far_near], far)), 1, 0, True), Rows(whole(out_mid), 0, 0)],
        weights,
        BLOCK,
        (shrink_mine, shrink_other, sums),
    )
    r_third = exchange(j_third)
    v_other = [send(after([out_far, j_third], w), SIBLING) for w in v_own]

    low, swapped = low_sums(r_third)
    low = add(low, send(swapped, MIDDLE))
    low_out = send(low, OUTWARD)

    rest = [(a, 0, b, 0) for a, b in zip(v_own, v_other)] + weights[:1]
    j_fifth = products(
        meta,
        [
            Rows([(after([j_third, r_mid], far), 3, 2, 0), (far, 5, 2, 1)], 1, 0),
            Rows([(out_far, 0, 3, 2)], 0, 0),
        ],
        rest,
        BLOCK,
    )
    r_fifth = exchange(j_fifth)
    r_own = exchange(j_own)

    def term(inner_slot, outer_slot):
        return (low, low_out, r_partner, (inner_slot, outer_slot))

    x_partner = finish(meta, None, r_partner, 0, term(1, 1))
    home_partner = send(x_partner, XOR[1])
    x_two = finish(meta, None, r_third, 0, term(3, 2))
    home_two = send(x_two, XOR[2])
    x_mid = finish(meta, 1, r_mid, 0, term(2, 2))
    home_mid = send(x_mid, MIDDLE)
    x_far = finish(meta, 0, r_fifth, 0, term(3, 3))
    to_far = send(x_far, INWARD)
    to_far = after([home_partner, home_two, home_mid], to_far)
    home_far = send(finish(meta, 1, r_fifth, 0, more=to_far), ACROSS)
    x_own = finish(meta, None, r_own, 0, term(0, 0))
    count = lax.dynamic_slice_in_dim(block_rows, t, 1, 0)
    return assemble(meta, count, x_own, home_partner, home_two, home_mid, home_far)


def solution(mesh):
    in_specs = (
        P("pool", "tensor"),
        P("tensor", "pool"),
        P("pool", "tensor", None),
        P("pool", "tensor", None),
        P("pool"),
        P("pool"),
    )
    out_specs = P(("pool", "tensor"), None)
    body = line_of_four if dict(mesh.shape) == {"pool": 8, "tensor": 4} else general
    return jax.shard_map(body, mesh=mesh, in_specs=in_specs, out_specs=out_specs, check_vma=False)
```

```python
import functools

import jax
import jax.numpy as jnp
from jax import lax
from jax.experimental import pallas as pl
from jax.experimental.pallas import tpu as pltpu
from jax.sharding import PartitionSpec as P

BLOCK = 128
SCALE = 0.5


def general(hidden, down_weight, adapter_shrink, adapter_expand, block_adapter, block_rows):
    input_rows, feat = hidden.shape
    block_count = block_adapter.shape[0]
    column_span = adapter_expand.shape[1]
    tensor_pos = lax.axis_index("tensor")
    tensor_count = lax.axis_size("tensor")
    own_rows = input_rows // tensor_count
    blocks = hidden.reshape(block_count, BLOCK, feat)
    partial_value = jnp.dot(
        hidden,
        lax.all_gather(down_weight, "pool", axis=1, tiled=True),
        preferred_element_type=jnp.float32,
    )
    total = lax.psum_scatter(
        partial_value.astype(jnp.bfloat16), "tensor", scatter_dimension=0, tiled=True
    ).astype(jnp.float32)
    shrink_piece = lax.all_gather(adapter_shrink, "pool", axis=0, tiled=True)
    expand_piece = lax.all_gather(adapter_expand, "pool", axis=0, tiled=True)
    idents = jnp.arange(shrink_piece.shape[0], dtype=jnp.int32)
    pick = (block_adapter[:, None] == idents[None, :]).astype(jnp.bfloat16)
    first = jnp.einsum("bk,kfr->bfr", pick, shrink_piece, preferred_element_type=jnp.float32)
    second = jnp.einsum("bk,kcr->bcr", pick, expand_piece, preferred_element_type=jnp.float32)
    shrink = jnp.einsum(
        "bnf,bfr->bnr", blocks, first.astype(jnp.bfloat16), preferred_element_type=jnp.float32
    )
    summed_shrink = lax.psum(shrink.astype(jnp.bfloat16), "tensor")
    enlarged_rows = jnp.einsum(
        "bnr,bcr->bnc",
        summed_shrink,
        second.astype(jnp.bfloat16),
        preferred_element_type=jnp.float32,
    )
    adapter_delta_columns = (
        (SCALE * enlarged_rows).astype(jnp.bfloat16).reshape(input_rows, column_span)
    )
    delta_mine = lax.all_to_all(
        adapter_delta_columns, "tensor", split_axis=0, concat_axis=1, tiled=True
    )
    total = total + delta_mine.astype(jnp.float32)
    row_ids = tensor_pos * own_rows + jnp.arange(own_rows, dtype=jnp.int32)
    owning = (row_ids // BLOCK)[:, None] == jnp.arange(block_count, dtype=jnp.int32)[None, :]
    lengths = jnp.sum(jnp.where(owning, block_rows[None, :], 0), axis=1)
    valid = (row_ids % BLOCK < lengths).astype(jnp.float32)
    return (total * valid[:, None]).astype(jnp.bfloat16)


def dot(a, b):
    return jnp.dot(a, b, preferred_element_type=jnp.float32)


def on_line(pairs):
    return [(2 * a + c, 2 * b + c) for a, b in pairs for c in range(2)]


XOR = {s: on_line([(z, z ^ s) for z in range(4)]) for s in (1, 2, 3)}
MIDDLE = on_line([(1, 2), (2, 1)])
OUTWARD = on_line([(1, 0), (2, 3)])
INWARD = on_line([(0, 1), (3, 2)])
ACROSS = on_line([(1, 3), (2, 0)])
SIBLING = [(p, p ^ 1) for p in range(8)]

TILE = 512
NEAR = 3 * TILE
WIDE = 2048
SHARE = 512
INNER, CORE, ZPOS, NAMES = 0, 1, 2, 3
CHEAP = pl.CostEstimate(flops=1000, bytes_accessed=1000, transcendentals=0)


def send(x, pairs):
    return lax.ppermute(x, "pool", pairs)


def after(events, *xs):
    tied = lax.optimization_barrier((tuple(events), xs))
    return tied[1] if len(xs) > 1 else tied[1][0]


def params(limit):
    return pltpu.CompilerParams(vmem_limit_bytes=limit * 1024 * 1024)


class Rows:
    def __init__(self, parts, role, at, shrink=False):
        self.parts, self.role, self.at, self.shrink = parts, role, at, shrink
        self.rows = parts[0][0].shape[0]
        self.total = sum(part[2] for part in parts)


def block_sums(meta, slot, low, start, count, b):
    name = meta[NAMES + 4 * slot + b]
    chip = name >> 2
    place = ((((name >> 1) & 1) ^ meta[CORE]) << 2) + jnp.where(chip == meta[ZPOS], 0, 2) + (name & 1)
    place = jnp.where((chip == meta[ZPOS]) | (chip == (meta[ZPOS] ^ 1)), place, -1)
    value = jnp.zeros((count, 64), jnp.float32)
    for i in range(8):
        part = low[start + b * count : start + (b + 1) * count, i * 64 : i * 64 + 64]
        value = value + jnp.where(place == i, part, 0.0)
    return value.astype(jnp.bfloat16)


def accumulate(ref, rows, cols, value, k, first):
    if first:
        value = value + jnp.where(k == 0, 0.0, ref[rows, cols])
    else:
        value = value + ref[rows, cols]
    ref[rows, cols] = value


def times_transposed(x, a):
    return lax.dot_general(x, a, (((1,), (1,)), ((), ())), preferred_element_type=jnp.float32)


def products_kernel(jobs, weights, shrink, pick, meta, *refs):
    refs = list(refs)
    xs = [[refs.pop(0) for _ in job.parts] for job in jobs]
    ws = [(refs.pop(0), refs.pop(0)) for _ in range(weights)]
    if shrink:
        adapters, sums = (refs.pop(0), refs.pop(0)), refs.pop(0)
    held = (refs.pop(0), refs.pop(0)) if pick else ()
    out, acc = refs[:2]
    low = refs[2] if shrink else None
    k = pl.program_id(0)
    z, c = meta[ZPOS], meta[CORE]
    inner = meta[INNER] == 1

    def choose():
        for b in range(4):
            for slot in range(4):
                name = meta[NAMES + 4 * slot + b]
                index = 2 * ((name >> 2) ^ z) + (name & 1)
                value = jnp.where(((name >> 1) & 1) == c, held[0][index], held[1][index])
                at = WIDE + slot // 2 * SHARE
                out[b, slot % 2 * 64 : slot % 2 * 64 + 64, at : at + SHARE] = value

    if pick:
        pl.when(k == 0)(choose)
    if shrink:

        @pl.when(k == 0)
        def _():
            out[:, :, WIDE : WIDE + 256] = sums[...]

    top = {0: 0, 1: 0}
    for x_parts, job in zip(xs, jobs):
        start = max(top.values()) if job.role is None else top[job.role]
        for role in top if job.role is None else (job.role,):
            top[role] = start + job.rows
        mine = slice(start, start + job.rows)
        role = True if job.role is None else meta[INNER] == job.role
        base = 0
        for x, (_, _, tiles, weight) in zip(x_parts, job.parts):

            def step(x=x, mine=mine, pair=ws[weight], first=base == 0):
                for h, w in enumerate(pair):
                    for n in range(0, WIDE // 2, 512):
                        at = slice(h * (WIDE // 2) + n, h * (WIDE // 2) + n + 512)
                        accumulate(acc, mine, at, dot(x[...], w[:, n : n + 512]), k, first)

            def shrink_step(x=x, mine=mine, first=base == 0):
                for h, a in enumerate(adapters):
                    accumulate(low, mine, slice(h * 256, h * 256 + 256), times_transposed(x[...], a[...]), k, first)

            now = (k >= base) & (k < base + tiles)
            pl.when(role & now)(step)
            if job.shrink:
                pl.when(inner & now)(shrink_step)
            base += tiles

        def store(job=job, start=start):
            count = job.rows // 4
            for b in range(4):
                value = acc[start + b * count : start + (b + 1) * count, :]
                out[b, job.at : job.at + count, :WIDE] = value.astype(jnp.bfloat16)

        def shrink_store(job=job, start=start):
            count = job.rows // 4
            for b in range(4):
                out[b, job.at : job.at + count, WIDE + 192 : WIDE + 256] = block_sums(meta, 3, low, start, count, b)

        pl.when(role & (k == job.total - 1))(store)
        if job.shrink:
            pl.when(inner & (k == job.total - 1))(shrink_store)


def products(meta, jobs, weights, rows, shrink=(), held=()):
    steps = max(job.total for job in jobs)
    in_specs, args, uses = [], [], {}
    for job in jobs:
        base = 0
        for x, tile, tiles, weight in job.parts:

            def index(k, m, base=base, tile=tile, tiles=tiles, role=job.role):
                at = jnp.clip(k - base, 0, tiles - 1)
                if role is not None:
                    at = at * (m[INNER] if role == 1 else 1 - m[INNER])
                return (0, at + tile)

            in_specs.append(pl.BlockSpec((x.shape[0], TILE), index))
            args.append(x)
            for role in (0, 1) if job.role is None else (job.role,):
                uses[weight, role] = (base, tiles)
            base += tiles
    for i, (own, own_tile, other, other_tile) in enumerate(weights):
        for w, tile in ((own, own_tile), (other, other_tile)):

            def index(k, m, i=i, tile=tile):
                at = [jnp.clip(k - base, 0, tiles - 1) for base, tiles in (uses.get((i, r), (0, 1)) for r in (0, 1))]
                return (jnp.where(m[INNER] == 1, at[1], at[0]) + tile, 0)

            in_specs.append(pl.BlockSpec((TILE, w.shape[1]), index))
            args.append(w)
    if shrink:
        for a in shrink[:2]:
            in_specs.append(pl.BlockSpec((a.shape[0], TILE), lambda k, m: (0, k * m[INNER])))
            args.append(a)
        in_specs.append(pl.BlockSpec(shrink[2].shape, lambda k, m: (0, 0, 0)))
        args.append(shrink[2])
    for a in held:
        in_specs.append(pl.BlockSpec(a.shape, lambda k, m: (0, 0, 0)))
        args.append(a)
    both = sum(job.rows for job in jobs if job.role is None)
    height = both + max(sum(job.rows for job in jobs if job.role == r) for r in (0, 1))
    scratch = [pltpu.VMEM((height, WIDE), jnp.float32)]
    if shrink:
        scratch.append(pltpu.VMEM((height, 512), jnp.float32))
    shape = (4, rows, WIDE + (256 if shrink else 0) + (2 * SHARE if held else 0))
    return pl.pallas_call(
        functools.partial(products_kernel, jobs, len(weights), bool(shrink), bool(held)),
        grid_spec=pltpu.PrefetchScalarGridSpec(
            num_scalar_prefetch=1,
            grid=(steps,),
            in_specs=in_specs,
            out_specs=pl.BlockSpec(shape, lambda k, m: (0, 0, 0)),
            scratch_shapes=scratch,
        ),
        out_shape=pltpu.HBM(shape, jnp.bfloat16),
        compiler_params=params(50),
        cost_estimate=CHEAP,
    )(meta, *args)


def shrink_kernel(tiles, slots, steps, meta, *refs):
    refs = list(refs)
    xs = [[refs.pop(0) for _ in part] for part in tiles]
    mine, other, out, low = refs
    k = pl.program_id(0)
    inner = meta[INNER] == 1
    rows = BLOCK * 4
    for i, x_parts in enumerate(xs):
        base = 0
        for x, count in zip(x_parts, tiles[i]):

            @pl.when(inner & (k >= base) & (k < base + count))
            def _(i=i, x=x, first=base == 0):
                here = slice(i * rows, (i + 1) * rows)
                for h, a in enumerate((mine, other)):
                    accumulate(low, here, slice(h * 256, h * 256 + 256), times_transposed(x[...], a[...]), k, first)

            base += count

    @pl.when(inner & (k == steps - 1))
    def _():
        for i, slot in enumerate(slots):
            for b in range(4):
                out[b, :, i * 64 : i * 64 + 64] = block_sums(meta, slot, low, i * rows, BLOCK, b)


def shrink_sums(meta, xs, slots, mine, other):
    tiles = [[part.shape[1] // TILE for part in x] for x in xs]
    steps = sum(tiles[0])
    in_specs, args = [], []
    for x, counts in zip(xs, tiles):
        base = 0
        for part, count in zip(x, counts):

            def index(k, m, base=base, count=count):
                return (0, jnp.clip(k - base, 0, count - 1) * m[INNER])

            in_specs.append(pl.BlockSpec((part.shape[0], TILE), index))
            args.append(part)
            base += count
    for a in (mine, other):
        in_specs.append(pl.BlockSpec((a.shape[0], TILE), lambda k, m: (0, k * m[INNER])))
        args.append(a)
    return pl.pallas_call(
        functools.partial(shrink_kernel, tiles, slots, steps),
        grid_spec=pltpu.PrefetchScalarGridSpec(
            num_scalar_prefetch=1,
            grid=(steps,),
            in_specs=in_specs,
            out_specs=pl.BlockSpec((4, BLOCK, 256), lambda k, m: (0, 0, 0)),
            scratch_shapes=[pltpu.VMEM((4 * BLOCK * len(xs), 512), jnp.float32)],
        ),
        out_shape=jax.ShapeDtypeStruct((4, BLOCK, 256), jnp.bfloat16),
        compiler_params=params(40),
        cost_estimate=CHEAP,
    )(meta, *args)


def low_kernel(x, out, swapped):
    value = x[0].astype(jnp.float32)
    for b in range(1, 4):
        value = value + x[b].astype(jnp.float32)
    value = value.astype(jnp.bfloat16)
    out[...] = value
    swapped[...] = jnp.concatenate([value[:, i * 64 : i * 64 + 64] for i in (1, 0, 3, 2)], axis=1)


def low_sums(x):
    shape = jax.ShapeDtypeStruct((BLOCK, 256), jnp.bfloat16)
    whole = pl.BlockSpec((BLOCK, 256), lambda i: (0, 0))
    return pl.pallas_call(
        low_kernel,
        grid=(1,),
        in_specs=[pl.BlockSpec((4, BLOCK, 256), lambda i: (0, 0, 0))],
        out_specs=(whole, whole),
        out_shape=(shape, shape),
        cost_estimate=CHEAP,
    )(x)


def add_kernel(x, y, out):
    out[...] = (x[...].astype(jnp.float32) + y[...].astype(jnp.float32)).astype(jnp.bfloat16)


def add(x, y):
    return pl.pallas_call(add_kernel, out_shape=jax.ShapeDtypeStruct(x.shape, x.dtype), cost_estimate=CHEAP)(x, y)


def finish_kernel(role, row, rows, lanes, has_more, meta, *refs):
    refs = list(refs)
    part = refs.pop(0)
    if lanes:
        low_in, low_out, expand = refs.pop(0), refs.pop(0), refs.pop(0)
    more = refs.pop(0) if has_more else None
    out = refs.pop(0)

    def run():
        total = part[0, row : row + rows, :].astype(jnp.float32)
        for b in range(1, 4):
            total = total + part[b, row : row + rows, :].astype(jnp.float32)
        if lanes:
            x = low_in[:rows, lanes[0] : lanes[0] + 64]
            y = low_out[:rows, lanes[1] : lanes[1] + 64]
            x = jnp.where(meta[INNER] == 1, x, y)
            delta = [dot(x, expand[i]) for i in range(expand.shape[0])]
            total = total + SCALE * jnp.concatenate(delta, axis=1)
        if has_more:
            total = total + more[...].astype(jnp.float32)
        out[...] = total.astype(jnp.bfloat16)

    if role is None:
        run()
    else:
        pl.when(meta[INNER] == role)(run)


def finish(meta, role, part, row, low=None, more=None, rows=BLOCK):
    span = WIDE // 2
    in_specs = [pl.BlockSpec((4, part.shape[1], span), lambda h, m: (0, 0, h))]
    args = [part]
    lanes = None
    if low is not None:
        *sums, expand, slots = low
        for x in sums:
            in_specs.append(pl.BlockSpec(x.shape, lambda h, m: (0, 0)))
            args.append(x)

        def index(h, m):
            slot = slots[1] + (slots[0] - slots[1]) * m[INNER]
            return (h ^ m[CORE], slot & 1, WIDE // SHARE + (slot >> 1))

        in_specs.append(pl.BlockSpec((span // SHARE, 64, SHARE), index))
        args.append(expand)
        lanes = [64 * (0, 2, 1, 3)[slots[0]], 64 * (2, 0, 1, 3)[slots[1]]]
    if more is not None:
        in_specs.append(pl.BlockSpec((rows, span), lambda h, m: (0, h)))
        args.append(more)
    return pl.pallas_call(
        functools.partial(finish_kernel, role, row, rows, lanes, more is not None),
        grid_spec=pltpu.PrefetchScalarGridSpec(
            num_scalar_prefetch=1,
            grid=(2,),
            in_specs=in_specs,
            out_specs=pl.BlockSpec((rows, span), lambda h, m: (0, h)),
        ),
        out_shape=jax.ShapeDtypeStruct((rows, WIDE), jnp.bfloat16),
        compiler_params=params(32),
        cost_estimate=CHEAP,
    )(meta, *args)


def assemble_kernel(span, meta, count, own, one, two, inner_three, outer_three, out):
    z, c, inner = meta[ZPOS], meta[CORE], meta[INNER] == 1
    rows = own.shape[0]
    valid = lax.broadcasted_iota(jnp.int32, (rows, 1), 0) < count[0]

    def put(j, source):
        for h in range(2):
            at = pl.ds(pl.multiple_of((2 * j + h) * span, span), span)
            part = pl.ds(pl.multiple_of((h ^ c) * span, span), span)
            out[:, at] = jnp.where(valid, source[:, part], jnp.zeros((), jnp.bfloat16))

    put(z, own)
    put(z ^ 1, one)
    put(z ^ 2, two)

    @pl.when(inner)
    def _():
        put(z ^ 3, inner_three)

    @pl.when(jnp.logical_not(inner))
    def _():
        put(z ^ 3, outer_three)


def assemble(meta, count, *args):
    rows, wide = args[0].shape
    return pl.pallas_call(
        functools.partial(assemble_kernel, wide // 2),
        grid_spec=pltpu.PrefetchScalarGridSpec(
            num_scalar_prefetch=2,
            grid=(1,),
            in_specs=[pl.BlockSpec(a.shape, lambda n, m, k: (0, 0)) for a in args],
            out_specs=pl.BlockSpec((rows, 4 * wide), lambda n, m, k: (0, 0)),
        ),
        out_shape=jax.ShapeDtypeStruct((rows, 4 * wide), jnp.bfloat16),
        compiler_params=params(32),
        cost_estimate=CHEAP,
    )(meta, count, *args)


def line_of_four(hidden, down_weight, adapter_shrink, adapter_expand, block_adapter, block_rows):
    rows, feat = hidden.shape
    adp, _, rank = adapter_shrink.shape
    p = lax.axis_index("pool")
    t = lax.axis_index("tensor")
    tensors = lax.axis_size("tensor")
    z, c = p // 2, p % 2
    outer = (z == 0) | (z == 3)

    def exchange(x):
        return lax.all_to_all(x, "tensor", split_axis=0, concat_axis=0, tiled=True)

    place = jnp.stack([jnp.where(outer, 0, 1), c, z]).astype(jnp.int32)

    mid = send(hidden, MIDDLE)
    partner = send(hidden, XOR[1])
    cuts = [(0, NEAR), (NEAR, NEAR + 2 * TILE), (NEAR + 2 * TILE, feat)]
    pieces = [down_weight[lo:hi] for lo, hi in cuts]
    others = [send(w, SIBLING) for w in pieces]
    weights = [(down_weight, lo // TILE, w, 0) for (lo, _), w in zip(cuts, others)]

    def whole(x):
        return [(x, lo // TILE, (hi - lo) // TILE, i) for i, (lo, hi) in enumerate(cuts)]

    shares = exchange(
        adapter_expand.transpose(0, 2, 1).reshape(adp, rank, tensors, SHARE).transpose(2, 0, 1, 3)
    ).reshape(tensors, adp * rank, SHARE)
    label = jnp.zeros((16, SHARE), jnp.bfloat16).at[0, : block_adapter.shape[0]].set(block_adapter.astype(jnp.bfloat16))
    j_own = products(place, [Rows(whole(hidden), None, 0)], weights, BLOCK)
    shares = after([j_own], shares)

    def shares_of(s):
        return lax.dynamic_index_in_dim(shares, z ^ s, 0, keepdims=False)

    told = [send(jnp.concatenate([shares_of(s), label], axis=0), XOR[s]) for s in (1, 2, 3)]

    ready = [partner, mid, *told]
    far = send(after(ready, partner), MIDDLE)
    out_mid = send(after(ready, mid), OUTWARD)
    v_own = [send(after(ready, w), INWARD) for w in pieces[1:]]

    held = jnp.concatenate([shares_of(0)] + [x[: adp * rank] for x in told]).reshape(4 * adp, rank, SHARE)
    held = (held, send(held, SIBLING))
    names = [block_adapter] + [x[adp * rank, : block_adapter.shape[0]].astype(jnp.int32) for x in told]
    name_m = jnp.where(outer, names[2], names[3])
    name_f = jnp.where(outer, names[3], names[2])
    meta = jnp.concatenate([place, names[0], names[1], name_m, name_f])
    j_partner = products(meta, [Rows(whole(partner), None, 0)], weights, BLOCK, held=held)
    r_partner = exchange(j_partner)
    j_mid = products(meta, [Rows(whole(after([j_partner], mid)), 1, 0)], weights, BLOCK)
    r_mid = exchange(j_mid)

    far_near = far[:, :NEAR]
    out_far = send(after([j_partner, j_mid], far_near), OUTWARD)
    shrink_w = adapter_shrink.transpose(0, 2, 1).reshape(adp * rank, feat)
    shrink_o = send(after([j_mid], shrink_w), INWARD)
    j_third = products(
        meta,
        [Rows(whole(after([r_partner, far_near], far)), 1, 0), Rows(whole(out_mid), 0, 0)],
        weights,
        BLOCK,
    )
    r_third = exchange(j_third)
    v_other = [send(after([out_far, j_third], w), SIBLING) for w in v_own]

    shrink_mine = jnp.concatenate([shrink_w, after([out_far], shrink_o)], axis=0)
    shrink_other = send(shrink_mine, SIBLING)
    sums = shrink_sums(meta, [[hidden], [after([r_mid], mid)], [partner], [far]], [0, 2, 1, 3], shrink_mine, shrink_other)
    low, swapped = low_sums(exchange(sums))
    low = add(low, send(swapped, MIDDLE))
    low_out = send(low, OUTWARD)

    rest = [(a, 0, b, 0) for a, b in zip(v_own, v_other)] + weights[:1]
    j_fifth = products(
        meta,
        [
            Rows([(after([sums], far), 3, 2, 0), (far, 5, 2, 1)], 1, 0),
            Rows([(out_far, 0, 3, 2)], 0, 0),
        ],
        rest,
        BLOCK,
    )
    r_fifth = exchange(j_fifth)
    r_own = exchange(j_own)

    def term(inner_slot, outer_slot):
        return (low, low_out, r_partner, (inner_slot, outer_slot))

    x_partner = finish(meta, None, r_partner, 0, term(1, 1))
    home_partner = send(x_partner, XOR[1])
    x_two = finish(meta, None, r_third, 0, term(3, 2))
    home_two = send(x_two, XOR[2])
    x_mid = finish(meta, 1, r_mid, 0, term(2, 2))
    home_mid = send(x_mid, MIDDLE)
    r_fifth = after([x_partner, x_two, x_mid], r_fifth)
    x_far = finish(meta, 0, r_fifth, 0, term(3, 3))
    to_far = send(x_far, INWARD)
    to_far = after([home_partner, home_two, home_mid], to_far)
    home_far = send(finish(meta, 1, r_fifth, 0, more=to_far), ACROSS)
    x_own = finish(meta, None, r_own, 0, term(0, 0))
    count = lax.dynamic_slice_in_dim(block_rows, t, 1, 0)
    return assemble(meta, count, x_own, home_partner, home_two, home_mid, home_far)


def solution(mesh):
    in_specs = (
        P("pool", "tensor"),
        P("tensor", "pool"),
        P("pool", "tensor", None),
        P("pool", "tensor", None),
        P("pool"),
        P("pool"),
    )
    out_specs = P(("pool", "tensor"), None)
    body = line_of_four if dict(mesh.shape) == {"pool": 8, "tensor": 4} else general
    return jax.shard_map(body, mesh=mesh, in_specs=in_specs, out_specs=out_specs, check_vma=False)
```

```python
import functools

import jax
import jax.numpy as jnp
from jax import lax
from jax.experimental import pallas as pl
from jax.experimental.pallas import tpu as pltpu
from jax.sharding import PartitionSpec as P

BLOCK = 128
SCALE = 0.5


def general(hidden, down_weight, adapter_shrink, adapter_expand, block_adapter, block_rows):
    input_rows, feat = hidden.shape
    block_count = block_adapter.shape[0]
    column_span = adapter_expand.shape[1]
    tensor_pos = lax.axis_index("tensor")
    tensor_count = lax.axis_size("tensor")
    own_rows = input_rows // tensor_count
    blocks = hidden.reshape(block_count, BLOCK, feat)
    partial_value = jnp.dot(
        hidden,
        lax.all_gather(down_weight, "pool", axis=1, tiled=True),
        preferred_element_type=jnp.float32,
    )
    total = lax.psum_scatter(
        partial_value.astype(jnp.bfloat16), "tensor", scatter_dimension=0, tiled=True
    ).astype(jnp.float32)
    shrink_piece = lax.all_gather(adapter_shrink, "pool", axis=0, tiled=True)
    expand_piece = lax.all_gather(adapter_expand, "pool", axis=0, tiled=True)
    idents = jnp.arange(shrink_piece.shape[0], dtype=jnp.int32)
    pick = (block_adapter[:, None] == idents[None, :]).astype(jnp.bfloat16)
    first = jnp.einsum("bk,kfr->bfr", pick, shrink_piece, preferred_element_type=jnp.float32)
    second = jnp.einsum("bk,kcr->bcr", pick, expand_piece, preferred_element_type=jnp.float32)
    shrink = jnp.einsum(
        "bnf,bfr->bnr", blocks, first.astype(jnp.bfloat16), preferred_element_type=jnp.float32
    )
    summed_shrink = lax.psum(shrink.astype(jnp.bfloat16), "tensor")
    enlarged_rows = jnp.einsum(
        "bnr,bcr->bnc",
        summed_shrink,
        second.astype(jnp.bfloat16),
        preferred_element_type=jnp.float32,
    )
    adapter_delta_columns = (
        (SCALE * enlarged_rows).astype(jnp.bfloat16).reshape(input_rows, column_span)
    )
    delta_mine = lax.all_to_all(
        adapter_delta_columns, "tensor", split_axis=0, concat_axis=1, tiled=True
    )
    total = total + delta_mine.astype(jnp.float32)
    row_ids = tensor_pos * own_rows + jnp.arange(own_rows, dtype=jnp.int32)
    owning = (row_ids // BLOCK)[:, None] == jnp.arange(block_count, dtype=jnp.int32)[None, :]
    lengths = jnp.sum(jnp.where(owning, block_rows[None, :], 0), axis=1)
    valid = (row_ids % BLOCK < lengths).astype(jnp.float32)
    return (total * valid[:, None]).astype(jnp.bfloat16)


def dot(a, b):
    return jnp.dot(a, b, preferred_element_type=jnp.float32)


def on_line(pairs):
    return [(2 * a + c, 2 * b + c) for a, b in pairs for c in range(2)]


XOR = {s: on_line([(z, z ^ s) for z in range(4)]) for s in (1, 2, 3)}
MIDDLE = on_line([(1, 2), (2, 1)])
OUTWARD = on_line([(1, 0), (2, 3)])
INWARD = on_line([(0, 1), (3, 2)])
ACROSS = on_line([(1, 3), (2, 0)])
SIBLING = [(p, p ^ 1) for p in range(8)]

TILE = 512
NEAR = 4 * TILE
WIDE = 2048
SHARE = 512
INNER, CORE, ZPOS, NAMES = 0, 1, 2, 3
CHEAP = pl.CostEstimate(flops=1000, bytes_accessed=1000, transcendentals=0)


def send(x, pairs):
    return lax.ppermute(x, "pool", pairs)


def after(events, *xs):
    tied = lax.optimization_barrier((tuple(events), xs))
    return tied[1] if len(xs) > 1 else tied[1][0]


def params(limit):
    return pltpu.CompilerParams(vmem_limit_bytes=limit * 1024 * 1024)


class Rows:
    def __init__(self, parts, role, at):
        self.parts, self.role, self.at = parts, role, at
        self.rows = parts[0][0].shape[0]
        self.total = sum(part[2] for part in parts)


def block_sums(meta, slot, low, start, count, b):
    name = meta[NAMES + 4 * slot + b]
    chip = name >> 2
    place = ((((name >> 1) & 1) ^ meta[CORE]) << 2) + jnp.where(chip == meta[ZPOS], 0, 2) + (name & 1)
    place = jnp.where((chip == meta[ZPOS]) | (chip == (meta[ZPOS] ^ 1)), place, -1)
    value = jnp.zeros((count, 64), jnp.float32)
    for i in range(8):
        part = low[start + b * count : start + (b + 1) * count, i * 64 : i * 64 + 64]
        value = value + jnp.where(place == i, part, 0.0)
    return value.astype(jnp.bfloat16)


def accumulate(ref, rows, cols, value, k, first):
    if first:
        value = value + jnp.where(k == 0, 0.0, ref[rows, cols])
    else:
        value = value + ref[rows, cols]
    ref[rows, cols] = value


def times_transposed(x, a):
    return lax.dot_general(x, a, (((1,), (1,)), ((), ())), preferred_element_type=jnp.float32)


def products_kernel(jobs, weights, meta, *refs):
    refs = list(refs)
    xs = [[refs.pop(0) for _ in job.parts] for job in jobs]
    ws = [(refs.pop(0), refs.pop(0)) for _ in range(weights)]
    out, acc = refs
    k = pl.program_id(0)
    top = {0: 0, 1: 0}
    for x_parts, job in zip(xs, jobs):
        start = max(top.values()) if job.role is None else top[job.role]
        for role in top if job.role is None else (job.role,):
            top[role] = start + job.rows
        mine = slice(start, start + job.rows)
        role = True if job.role is None else meta[INNER] == job.role
        base = 0
        for x, (_, _, tiles, weight) in zip(x_parts, job.parts):

            def step(x=x, mine=mine, pair=ws[weight], first=base == 0):
                for h, w in enumerate(pair):
                    for n in range(0, WIDE // 2, 512):
                        at = slice(h * (WIDE // 2) + n, h * (WIDE // 2) + n + 512)
                        accumulate(acc, mine, at, dot(x[...], w[:, n : n + 512]), k, first)

            pl.when(role & (k >= base) & (k < base + tiles))(step)
            base += tiles

        def store(job=job, start=start):
            count = job.rows // 4
            for b in range(4):
                value = acc[start + b * count : start + (b + 1) * count, :]
                out[b, job.at : job.at + count, :] = value.astype(jnp.bfloat16)

        pl.when(role & (k == job.total - 1))(store)


def products(meta, jobs, weights, rows):
    steps = max(job.total for job in jobs)
    in_specs, args, uses = [], [], {}
    for job in jobs:
        base = 0
        for x, tile, tiles, weight in job.parts:

            def index(k, m, base=base, tile=tile, tiles=tiles, role=job.role):
                at = jnp.clip(k - base, 0, tiles - 1)
                if role is not None:
                    at = at * (m[INNER] if role == 1 else 1 - m[INNER])
                return (0, at + tile)

            in_specs.append(pl.BlockSpec((x.shape[0], TILE), index))
            args.append(x)
            for role in (0, 1) if job.role is None else (job.role,):
                uses[weight, role] = (base, tiles)
            base += tiles
    for i, (own, own_tile, other, other_tile) in enumerate(weights):
        for w, tile in ((own, own_tile), (other, other_tile)):

            def index(k, m, i=i, tile=tile):
                at = [jnp.clip(k - base, 0, tiles - 1) for base, tiles in (uses.get((i, r), (0, 1)) for r in (0, 1))]
                return (jnp.where(m[INNER] == 1, at[1], at[0]) + tile, 0)

            in_specs.append(pl.BlockSpec((TILE, w.shape[1]), index))
            args.append(w)
    both = sum(job.rows for job in jobs if job.role is None)
    height = both + max(sum(job.rows for job in jobs if job.role == r) for r in (0, 1))
    shape = (4, rows, WIDE)
    return pl.pallas_call(
        functools.partial(products_kernel, jobs, len(weights)),
        grid_spec=pltpu.PrefetchScalarGridSpec(
            num_scalar_prefetch=1,
            grid=(steps,),
            in_specs=in_specs,
            out_specs=pl.BlockSpec(shape, lambda k, m: (0, 0, 0)),
            scratch_shapes=[pltpu.VMEM((height, WIDE), jnp.float32)],
        ),
        out_shape=pltpu.HBM(shape, jnp.bfloat16),
        compiler_params=params(50),
        cost_estimate=CHEAP,
    )(meta, *args)


def shrink_kernel(tiles, slots, steps, meta, *refs):
    refs = list(refs)
    xs = [[refs.pop(0) for _ in part] for part in tiles]
    mine, other, held_mine, held_other, out, low = refs
    k = pl.program_id(0)
    inner = meta[INNER] == 1
    rows = BLOCK * 4
    for i, x_parts in enumerate(xs):
        base = 0
        for x, count in zip(x_parts, tiles[i]):

            @pl.when(inner & (k >= base) & (k < base + count))
            def _(i=i, x=x, first=base == 0):
                here = slice(i * rows, (i + 1) * rows)
                for h, a in enumerate((mine, other)):
                    accumulate(low, here, slice(h * 256, h * 256 + 256), times_transposed(x[...], a[...]), k, first)

            base += count

    @pl.when(inner & (k == steps - 1))
    def _():
        for i, slot in enumerate(slots):
            for b in range(4):
                at = 2 * SHARE + i * 64
                out[b, :, at : at + 64] = block_sums(meta, slot, low, i * rows, BLOCK, b)

    @pl.when(k == 0)
    def _():
        for b in range(4):
            for slot in range(4):
                name = meta[NAMES + 4 * slot + b]
                index = 2 * ((name >> 2) ^ meta[ZPOS]) + (name & 1)
                value = jnp.where(((name >> 1) & 1) == meta[CORE], held_mine[index], held_other[index])
                at = slot // 2 * SHARE
                out[b, slot % 2 * 64 : slot % 2 * 64 + 64, at : at + SHARE] = value


def shrink_sums(meta, xs, slots, mine, other, held):
    tiles = [[part.shape[1] // TILE for part in x] for x in xs]
    steps = sum(tiles[0])
    in_specs, args = [], []
    for x, counts in zip(xs, tiles):
        base = 0
        for part, count in zip(x, counts):

            def index(k, m, base=base, count=count):
                return (0, jnp.clip(k - base, 0, count - 1) * m[INNER])

            in_specs.append(pl.BlockSpec((part.shape[0], TILE), index))
            args.append(part)
            base += count
    for a in (mine, other):
        in_specs.append(pl.BlockSpec((a.shape[0], TILE), lambda k, m: (0, k * m[INNER])))
        args.append(a)
    for a in held:
        in_specs.append(pl.BlockSpec(a.shape, lambda k, m: (0, 0, 0)))
        args.append(a)
    shape = (4, BLOCK, 2 * SHARE + 256)
    return pl.pallas_call(
        functools.partial(shrink_kernel, tiles, slots, steps),
        grid_spec=pltpu.PrefetchScalarGridSpec(
            num_scalar_prefetch=1,
            grid=(steps,),
            in_specs=in_specs,
            out_specs=pl.BlockSpec(shape, lambda k, m: (0, 0, 0)),
            scratch_shapes=[pltpu.VMEM((4 * BLOCK * len(xs), 512), jnp.float32)],
        ),
        out_shape=pltpu.HBM(shape, jnp.bfloat16),
        compiler_params=params(40),
        cost_estimate=CHEAP,
    )(meta, *args)


def low_kernel(x, out, swapped):
    value = x[0].astype(jnp.float32)
    for b in range(1, 4):
        value = value + x[b].astype(jnp.float32)
    value = value.astype(jnp.bfloat16)
    out[...] = value
    swapped[...] = jnp.concatenate([value[:, i * 64 : i * 64 + 64] for i in (1, 0, 3, 2)], axis=1)


def low_sums(x):
    shape = jax.ShapeDtypeStruct((BLOCK, 256), jnp.bfloat16)
    whole = pl.BlockSpec((BLOCK, 256), lambda i: (0, 0))
    return pl.pallas_call(
        low_kernel,
        grid=(1,),
        in_specs=[pl.BlockSpec((4, BLOCK, 256), lambda i: (0, 0, 2 * SHARE // 256))],
        out_specs=(whole, whole),
        out_shape=(shape, shape),
        cost_estimate=CHEAP,
    )(x)


def add_kernel(x, y, out):
    out[...] = (x[...].astype(jnp.float32) + y[...].astype(jnp.float32)).astype(jnp.bfloat16)


def add(x, y):
    return pl.pallas_call(add_kernel, out_shape=jax.ShapeDtypeStruct(x.shape, x.dtype), cost_estimate=CHEAP)(x, y)


def finish_kernel(role, row, rows, lanes, has_more, meta, *refs):
    refs = list(refs)
    part = refs.pop(0)
    if lanes:
        low_in, low_out, expand = refs.pop(0), refs.pop(0), refs.pop(0)
    more = refs.pop(0) if has_more else None
    out = refs.pop(0)

    def run():
        total = part[0, row : row + rows, :].astype(jnp.float32)
        for b in range(1, 4):
            total = total + part[b, row : row + rows, :].astype(jnp.float32)
        if lanes:
            x = low_in[:rows, lanes[0] : lanes[0] + 64]
            y = low_out[:rows, lanes[1] : lanes[1] + 64]
            x = jnp.where(meta[INNER] == 1, x, y)
            delta = [dot(x, expand[i]) for i in range(expand.shape[0])]
            total = total + SCALE * jnp.concatenate(delta, axis=1)
        if has_more:
            total = total + more[...].astype(jnp.float32)
        out[...] = total.astype(jnp.bfloat16)

    if role is None:
        run()
    else:
        pl.when(meta[INNER] == role)(run)


def finish(meta, role, part, row, low=None, more=None, rows=BLOCK):
    span = WIDE // 2
    in_specs = [pl.BlockSpec((4, part.shape[1], span), lambda h, m: (0, 0, h))]
    args = [part]
    lanes = None
    if low is not None:
        *sums, expand, slots = low
        for x in sums:
            in_specs.append(pl.BlockSpec(x.shape, lambda h, m: (0, 0)))
            args.append(x)

        def index(h, m):
            slot = slots[1] + (slots[0] - slots[1]) * m[INNER]
            return (h ^ m[CORE], slot & 1, slot >> 1)

        in_specs.append(pl.BlockSpec((span // SHARE, 64, SHARE), index))
        args.append(expand)
        lanes = [64 * (0, 2, 1, 3)[slots[0]], 64 * (2, 0, 1, 3)[slots[1]]]
    if more is not None:
        in_specs.append(pl.BlockSpec((rows, span), lambda h, m: (0, h)))
        args.append(more)
    return pl.pallas_call(
        functools.partial(finish_kernel, role, row, rows, lanes, more is not None),
        grid_spec=pltpu.PrefetchScalarGridSpec(
            num_scalar_prefetch=1,
            grid=(2,),
            in_specs=in_specs,
            out_specs=pl.BlockSpec((rows, span), lambda h, m: (0, h)),
        ),
        out_shape=jax.ShapeDtypeStruct((rows, WIDE), jnp.bfloat16),
        compiler_params=params(32),
        cost_estimate=CHEAP,
    )(meta, *args)


def assemble_kernel(span, meta, count, own, one, two, inner_three, outer_three, out):
    z, c, inner = meta[ZPOS], meta[CORE], meta[INNER] == 1
    rows = own.shape[0]
    valid = lax.broadcasted_iota(jnp.int32, (rows, 1), 0) < count[0]

    def put(j, source):
        for h in range(2):
            at = pl.ds(pl.multiple_of((2 * j + h) * span, span), span)
            part = pl.ds(pl.multiple_of((h ^ c) * span, span), span)
            out[:, at] = jnp.where(valid, source[:, part], jnp.zeros((), jnp.bfloat16))

    put(z, own)
    put(z ^ 1, one)
    put(z ^ 2, two)

    @pl.when(inner)
    def _():
        put(z ^ 3, inner_three)

    @pl.when(jnp.logical_not(inner))
    def _():
        put(z ^ 3, outer_three)


def assemble(meta, count, *args):
    rows, wide = args[0].shape
    return pl.pallas_call(
        functools.partial(assemble_kernel, wide // 2),
        grid_spec=pltpu.PrefetchScalarGridSpec(
            num_scalar_prefetch=2,
            grid=(1,),
            in_specs=[pl.BlockSpec(a.shape, lambda n, m, k: (0, 0)) for a in args],
            out_specs=pl.BlockSpec((rows, 4 * wide), lambda n, m, k: (0, 0)),
        ),
        out_shape=jax.ShapeDtypeStruct((rows, 4 * wide), jnp.bfloat16),
        compiler_params=params(32),
        cost_estimate=CHEAP,
    )(meta, count, *args)


def line_of_four(hidden, down_weight, adapter_shrink, adapter_expand, block_adapter, block_rows):
    rows, feat = hidden.shape
    adp, _, rank = adapter_shrink.shape
    p = lax.axis_index("pool")
    t = lax.axis_index("tensor")
    tensors = lax.axis_size("tensor")
    z, c = p // 2, p % 2
    outer = (z == 0) | (z == 3)

    def exchange(x):
        return lax.all_to_all(x, "tensor", split_axis=0, concat_axis=0, tiled=True)

    place = jnp.stack([jnp.where(outer, 0, 1), c, z]).astype(jnp.int32)

    mid = send(hidden, MIDDLE)
    partner = send(hidden, XOR[1])
    cuts = [(lo, min(lo + 2 * TILE, feat)) for lo in range(0, feat, 2 * TILE)]
    pieces = [down_weight[lo:hi] for lo, hi in cuts]
    others = [send(w, SIBLING) for w in pieces]
    weights = [(down_weight, lo // TILE, w, 0) for (lo, _), w in zip(cuts, others)]

    def whole(x):
        return [(x, lo // TILE, (hi - lo) // TILE, i) for i, (lo, hi) in enumerate(cuts)]

    shares = exchange(
        adapter_expand.transpose(0, 2, 1).reshape(adp, rank, tensors, SHARE).transpose(2, 0, 1, 3)
    ).reshape(tensors, adp * rank, SHARE)
    label = jnp.zeros((16, SHARE), jnp.bfloat16).at[0, : block_adapter.shape[0]].set(block_adapter.astype(jnp.bfloat16))
    j_own = products(place, [Rows(whole(hidden), None, 0)], weights, BLOCK)

    ready = [partner, mid, j_own]
    far = send(after(ready, partner), MIDDLE)
    out_mid = send(after(ready, mid), OUTWARD)
    v_own = [send(after(ready, w), INWARD) for w in pieces[NEAR // (2 * TILE) :]]
    r_own = exchange(j_own)
    j_partner = products(place, [Rows(whole(partner), None, 0)], weights, BLOCK)
    r_partner = exchange(j_partner)
    j_mid = products(place, [Rows(whole(after([j_partner], mid)), 1, 0)], weights, BLOCK)
    r_mid = exchange(j_mid)
    shrink_w = adapter_shrink.transpose(0, 2, 1).reshape(adp * rank, feat)
    shrink_o = send(after([partner, mid], shrink_w), INWARD)
    shares = after([j_mid, *v_own, shrink_o], shares)

    def shares_of(s):
        return lax.dynamic_index_in_dim(shares, z ^ s, 0, keepdims=False)

    told = [send(jnp.concatenate([shares_of(s), label], axis=0), XOR[s]) for s in (1, 2, 3)]

    far_near = far[:, :NEAR]
    out_far = send(after([out_mid, *told], far_near), OUTWARD)
    j_third = products(
        place,
        [Rows(whole(after([r_partner, far_near], far)), 1, 0), Rows(whole(out_mid), 0, 0)],
        weights,
        BLOCK,
    )
    r_third = exchange(j_third)
    v_other = [send(after([j_third], w), SIBLING) for w in v_own]

    held = jnp.concatenate([shares_of(0)] + [x[: adp * rank] for x in told]).reshape(4 * adp, rank, SHARE)
    held = (held, send(held, SIBLING))
    names = [block_adapter] + [x[adp * rank, : block_adapter.shape[0]].astype(jnp.int32) for x in told]
    name_m = jnp.where(outer, names[2], names[3])
    name_f = jnp.where(outer, names[3], names[2])
    meta = jnp.concatenate([place, names[0], names[1], name_m, name_f])
    shrink_mine = jnp.concatenate([shrink_w, after([j_third], shrink_o)], axis=0)
    shrink_other = send(shrink_mine, SIBLING)
    sums = shrink_sums(meta, [[hidden], [mid], [partner], [far]], [0, 2, 1, 3], shrink_mine, shrink_other, held)
    r_sums = exchange(sums)
    low, swapped = low_sums(r_sums)
    low = add(low, send(swapped, MIDDLE))
    low_out = send(low, OUTWARD)

    rest = [(a, 0, b, 0) for a, b in zip(v_own, v_other)] + weights[: NEAR // (2 * TILE)]
    j_fifth = products(
        place,
        [
            Rows([(after([sums], far), NEAR // TILE, 2, 0), (far, NEAR // TILE + 2, 1, 1)], 1, 0),
            Rows([(out_far, 0, 2, 2), (out_far, 2, 2, 3)], 0, 0),
        ],
        rest,
        BLOCK,
    )
    r_fifth = exchange(j_fifth)

    def term(inner_slot, outer_slot):
        return (low, low_out, r_sums, (inner_slot, outer_slot))

    x_partner = finish(meta, None, r_partner, 0, term(1, 1))
    home_partner = send(x_partner, XOR[1])
    x_two = finish(meta, None, r_third, 0, term(3, 2))
    home_two = send(x_two, XOR[2])
    x_mid = finish(meta, 1, r_mid, 0, term(2, 2))
    home_mid = send(x_mid, MIDDLE)
    x_own = finish(meta, None, r_own, 0, term(0, 0))
    r_fifth = after([x_partner, x_two, x_mid, x_own], r_fifth)
    x_far = finish(meta, 0, r_fifth, 0, term(3, 3))
    to_far = send(x_far, INWARD)
    to_far = after([home_partner, home_two, home_mid], to_far)
    home_far = send(finish(meta, 1, r_fifth, 0, more=to_far), ACROSS)
    count = lax.dynamic_slice_in_dim(block_rows, t, 1, 0)
    return assemble(meta, count, x_own, home_partner, home_two, home_mid, home_far)


def solution(mesh):
    in_specs = (
        P("pool", "tensor"),
        P("tensor", "pool"),
        P("pool", "tensor", None),
        P("pool", "tensor", None),
        P("pool"),
        P("pool"),
    )
    out_specs = P(("pool", "tensor"), None)
    body = line_of_four if dict(mesh.shape) == {"pool": 8, "tensor": 4} else general
    return jax.shard_map(body, mesh=mesh, in_specs=in_specs, out_specs=out_specs, check_vma=False)
```

```python
import functools

import jax
import jax.numpy as jnp
from jax import lax
from jax.experimental import pallas as pl
from jax.experimental.pallas import tpu as pltpu
from jax.sharding import PartitionSpec as P

BLOCK = 128
SCALE = 0.5


def general(hidden, down_weight, adapter_shrink, adapter_expand, block_adapter, block_rows):
    input_rows, feat = hidden.shape
    block_count = block_adapter.shape[0]
    column_span = adapter_expand.shape[1]
    tensor_pos = lax.axis_index("tensor")
    tensor_count = lax.axis_size("tensor")
    own_rows = input_rows // tensor_count
    blocks = hidden.reshape(block_count, BLOCK, feat)
    partial_value = jnp.dot(
        hidden,
        lax.all_gather(down_weight, "pool", axis=1, tiled=True),
        preferred_element_type=jnp.float32,
    )
    total = lax.psum_scatter(
        partial_value.astype(jnp.bfloat16), "tensor", scatter_dimension=0, tiled=True
    ).astype(jnp.float32)
    shrink_piece = lax.all_gather(adapter_shrink, "pool", axis=0, tiled=True)
    expand_piece = lax.all_gather(adapter_expand, "pool", axis=0, tiled=True)
    idents = jnp.arange(shrink_piece.shape[0], dtype=jnp.int32)
    pick = (block_adapter[:, None] == idents[None, :]).astype(jnp.bfloat16)
    first = jnp.einsum("bk,kfr->bfr", pick, shrink_piece, preferred_element_type=jnp.float32)
    second = jnp.einsum("bk,kcr->bcr", pick, expand_piece, preferred_element_type=jnp.float32)
    shrink = jnp.einsum(
        "bnf,bfr->bnr", blocks, first.astype(jnp.bfloat16), preferred_element_type=jnp.float32
    )
    summed_shrink = lax.psum(shrink.astype(jnp.bfloat16), "tensor")
    enlarged_rows = jnp.einsum(
        "bnr,bcr->bnc",
        summed_shrink,
        second.astype(jnp.bfloat16),
        preferred_element_type=jnp.float32,
    )
    adapter_delta_columns = (
        (SCALE * enlarged_rows).astype(jnp.bfloat16).reshape(input_rows, column_span)
    )
    delta_mine = lax.all_to_all(
        adapter_delta_columns, "tensor", split_axis=0, concat_axis=1, tiled=True
    )
    total = total + delta_mine.astype(jnp.float32)
    row_ids = tensor_pos * own_rows + jnp.arange(own_rows, dtype=jnp.int32)
    owning = (row_ids // BLOCK)[:, None] == jnp.arange(block_count, dtype=jnp.int32)[None, :]
    lengths = jnp.sum(jnp.where(owning, block_rows[None, :], 0), axis=1)
    valid = (row_ids % BLOCK < lengths).astype(jnp.float32)
    return (total * valid[:, None]).astype(jnp.bfloat16)


def dot(a, b):
    return jnp.dot(a, b, preferred_element_type=jnp.float32)


def on_line(pairs):
    return [(2 * a + c, 2 * b + c) for a, b in pairs for c in range(2)]


XOR = {s: on_line([(z, z ^ s) for z in range(4)]) for s in (1, 2, 3)}
MIDDLE = on_line([(1, 2), (2, 1)])
OUTWARD = on_line([(1, 0), (2, 3)])
INWARD = on_line([(0, 1), (3, 2)])
ACROSS = on_line([(1, 3), (2, 0)])
SIBLING = [(p, p ^ 1) for p in range(8)]

TILE = 512
NEAR = 4 * TILE
WIDE = 2048
SHARE = 512
INNER, CORE, ZPOS, NAMES = 0, 1, 2, 3
CHEAP = pl.CostEstimate(flops=1000, bytes_accessed=1000, transcendentals=0)


def send(x, pairs):
    return lax.ppermute(x, "pool", pairs)


def after(events, *xs):
    tied = lax.optimization_barrier((tuple(events), xs))
    return tied[1] if len(xs) > 1 else tied[1][0]


def params(limit):
    return pltpu.CompilerParams(vmem_limit_bytes=limit * 1024 * 1024)


class Rows:
    def __init__(self, parts, role, at):
        self.parts, self.role, self.at = parts, role, at
        self.rows = parts[0][0].shape[0]
        self.total = sum(part[2] for part in parts)


def block_sums(meta, slot, low, start, count, b):
    name = meta[NAMES + 4 * slot + b]
    chip = name >> 2
    place = ((((name >> 1) & 1) ^ meta[CORE]) << 2) + jnp.where(chip == meta[ZPOS], 0, 2) + (name & 1)
    place = jnp.where((chip == meta[ZPOS]) | (chip == (meta[ZPOS] ^ 1)), place, -1)
    value = jnp.zeros((count, 64), jnp.float32)
    for i in range(8):
        part = low[start + b * count : start + (b + 1) * count, i * 64 : i * 64 + 64]
        value = value + jnp.where(place == i, part, 0.0)
    return value.astype(jnp.bfloat16)


def accumulate(ref, rows, cols, value, k, first):
    if first:
        value = value + jnp.where(k == 0, 0.0, ref[rows, cols])
    else:
        value = value + ref[rows, cols]
    ref[rows, cols] = value


def times_transposed(x, a):
    return lax.dot_general(x, a, (((1,), (1,)), ((), ())), preferred_element_type=jnp.float32)


def products_kernel(jobs, weights, meta, *refs):
    refs = list(refs)
    xs = [[refs.pop(0) for _ in job.parts] for job in jobs]
    ws = [(refs.pop(0), refs.pop(0)) for _ in range(weights)]
    out, acc = refs
    k = pl.program_id(0)
    top = {0: 0, 1: 0}
    for x_parts, job in zip(xs, jobs):
        start = max(top.values()) if job.role is None else top[job.role]
        for role in top if job.role is None else (job.role,):
            top[role] = start + job.rows
        mine = slice(start, start + job.rows)
        role = True if job.role is None else meta[INNER] == job.role
        base = 0
        for x, (_, _, tiles, weight) in zip(x_parts, job.parts):

            def step(x=x, mine=mine, pair=ws[weight], first=base == 0):
                for h, w in enumerate(pair):
                    for n in range(0, WIDE // 2, 512):
                        at = slice(h * (WIDE // 2) + n, h * (WIDE // 2) + n + 512)
                        accumulate(acc, mine, at, dot(x[...], w[:, n : n + 512]), k, first)

            pl.when(role & (k >= base) & (k < base + tiles))(step)
            base += tiles

        def store(job=job, start=start):
            count = job.rows // 4
            for b in range(4):
                value = acc[start + b * count : start + (b + 1) * count, :]
                out[b, job.at : job.at + count, :] = value.astype(jnp.bfloat16)

        pl.when(role & (k == job.total - 1))(store)


def products(meta, jobs, weights, rows):
    steps = max(job.total for job in jobs)
    in_specs, args, uses = [], [], {}
    for job in jobs:
        base = 0
        for x, tile, tiles, weight in job.parts:

            def index(k, m, base=base, tile=tile, tiles=tiles, role=job.role):
                at = jnp.clip(k - base, 0, tiles - 1)
                if role is not None:
                    at = at * (m[INNER] if role == 1 else 1 - m[INNER])
                return (0, at + tile)

            in_specs.append(pl.BlockSpec((x.shape[0], TILE), index))
            args.append(x)
            for role in (0, 1) if job.role is None else (job.role,):
                uses[weight, role] = (base, tiles)
            base += tiles
    for i, (own, own_tile, other, other_tile) in enumerate(weights):
        for w, tile in ((own, own_tile), (other, other_tile)):

            def index(k, m, i=i, tile=tile):
                at = [jnp.clip(k - base, 0, tiles - 1) for base, tiles in (uses.get((i, r), (0, 1)) for r in (0, 1))]
                return (jnp.where(m[INNER] == 1, at[1], at[0]) + tile, 0)

            in_specs.append(pl.BlockSpec((TILE, w.shape[1]), index))
            args.append(w)
    both = sum(job.rows for job in jobs if job.role is None)
    height = both + max(sum(job.rows for job in jobs if job.role == r) for r in (0, 1))
    shape = (4, rows, WIDE)
    return pl.pallas_call(
        functools.partial(products_kernel, jobs, len(weights)),
        grid_spec=pltpu.PrefetchScalarGridSpec(
            num_scalar_prefetch=1,
            grid=(steps,),
            in_specs=in_specs,
            out_specs=pl.BlockSpec(shape, lambda k, m: (0, 0, 0)),
            scratch_shapes=[pltpu.VMEM((height, WIDE), jnp.float32)],
        ),
        out_shape=pltpu.HBM(shape, jnp.bfloat16),
        compiler_params=params(50),
        cost_estimate=CHEAP,
    )(meta, *args)


def shrink_kernel(tiles, slots, steps, meta, *refs):
    refs = list(refs)
    xs = [[refs.pop(0) for _ in part] for part in tiles]
    mine, other, held_mine, held_other, out, low = refs
    k = pl.program_id(0)
    inner = meta[INNER] == 1
    rows = BLOCK * 4
    for i, x_parts in enumerate(xs):
        base = 0
        for x, count in zip(x_parts, tiles[i]):

            @pl.when(inner & (k >= base) & (k < base + count))
            def _(i=i, x=x, first=base == 0):
                here = slice(i * rows, (i + 1) * rows)
                for h, a in enumerate((mine, other)):
                    accumulate(low, here, slice(h * 256, h * 256 + 256), times_transposed(x[...], a[...]), k, first)

            base += count

    @pl.when(inner & (k == steps - 1))
    def _():
        for i, slot in enumerate(slots):
            for b in range(4):
                at = 2 * SHARE + i * 64
                out[b, :, at : at + 64] = block_sums(meta, slot, low, i * rows, BLOCK, b)

    @pl.when(k == 0)
    def _():
        for b in range(4):
            for slot in range(4):
                name = meta[NAMES + 4 * slot + b]
                index = 2 * ((name >> 2) ^ meta[ZPOS]) + (name & 1)
                value = jnp.where(((name >> 1) & 1) == meta[CORE], held_mine[index], held_other[index])
                at = slot // 2 * SHARE
                out[b, slot % 2 * 64 : slot % 2 * 64 + 64, at : at + SHARE] = value


def shrink_sums(meta, xs, slots, mine, other, held):
    tiles = [[part.shape[1] // TILE for part in x] for x in xs]
    steps = sum(tiles[0])
    in_specs, args = [], []
    for x, counts in zip(xs, tiles):
        base = 0
        for part, count in zip(x, counts):

            def index(k, m, base=base, count=count):
                return (0, jnp.clip(k - base, 0, count - 1) * m[INNER])

            in_specs.append(pl.BlockSpec((part.shape[0], TILE), index))
            args.append(part)
            base += count
    for a in (mine, other):
        in_specs.append(pl.BlockSpec((a.shape[0], TILE), lambda k, m: (0, k * m[INNER])))
        args.append(a)
    for a in held:
        in_specs.append(pl.BlockSpec(a.shape, lambda k, m: (0, 0, 0)))
        args.append(a)
    shape = (4, BLOCK, 2 * SHARE + 256)
    return pl.pallas_call(
        functools.partial(shrink_kernel, tiles, slots, steps),
        grid_spec=pltpu.PrefetchScalarGridSpec(
            num_scalar_prefetch=1,
            grid=(steps,),
            in_specs=in_specs,
            out_specs=pl.BlockSpec(shape, lambda k, m: (0, 0, 0)),
            scratch_shapes=[pltpu.VMEM((4 * BLOCK * len(xs), 512), jnp.float32)],
        ),
        out_shape=pltpu.HBM(shape, jnp.bfloat16),
        compiler_params=params(40),
        cost_estimate=CHEAP,
    )(meta, *args)


def low_kernel(x, out, swapped):
    value = x[0].astype(jnp.float32)
    for b in range(1, 4):
        value = value + x[b].astype(jnp.float32)
    value = value.astype(jnp.bfloat16)
    out[...] = value
    swapped[...] = jnp.concatenate([value[:, i * 64 : i * 64 + 64] for i in (1, 0, 3, 2)], axis=1)


def low_sums(x):
    shape = jax.ShapeDtypeStruct((BLOCK, 256), jnp.bfloat16)
    whole = pl.BlockSpec((BLOCK, 256), lambda i: (0, 0))
    return pl.pallas_call(
        low_kernel,
        grid=(1,),
        in_specs=[pl.BlockSpec((4, BLOCK, 256), lambda i: (0, 0, 2 * SHARE // 256))],
        out_specs=(whole, whole),
        out_shape=(shape, shape),
        cost_estimate=CHEAP,
    )(x)


def add_kernel(x, y, out):
    out[...] = (x[...].astype(jnp.float32) + y[...].astype(jnp.float32)).astype(jnp.bfloat16)


def add(x, y):
    return pl.pallas_call(add_kernel, out_shape=jax.ShapeDtypeStruct(x.shape, x.dtype), cost_estimate=CHEAP)(x, y)


def finish_kernel(role, row, rows, lanes, has_more, meta, *refs):
    refs = list(refs)
    part = refs.pop(0)
    if lanes:
        low_in, low_out, expand = refs.pop(0), refs.pop(0), refs.pop(0)
    more = refs.pop(0) if has_more else None
    out = refs.pop(0)

    def run():
        total = part[0, row : row + rows, :].astype(jnp.float32)
        for b in range(1, 4):
            total = total + part[b, row : row + rows, :].astype(jnp.float32)
        if lanes:
            x = low_in[:rows, lanes[0] : lanes[0] + 64]
            y = low_out[:rows, lanes[1] : lanes[1] + 64]
            x = jnp.where(meta[INNER] == 1, x, y)
            delta = [dot(x, expand[i]) for i in range(expand.shape[0])]
            total = total + SCALE * jnp.concatenate(delta, axis=1)
        if has_more:
            total = total + more[...].astype(jnp.float32)
        out[...] = total.astype(jnp.bfloat16)

    if role is None:
        run()
    else:
        pl.when(meta[INNER] == role)(run)


def finish(meta, role, part, row, low=None, more=None, rows=BLOCK):
    span = WIDE // 2
    in_specs = [pl.BlockSpec((4, part.shape[1], span), lambda h, m: (0, 0, h))]
    args = [part]
    lanes = None
    if low is not None:
        *sums, expand, slots = low
        for x in sums:
            in_specs.append(pl.BlockSpec(x.shape, lambda h, m: (0, 0)))
            args.append(x)

        def index(h, m):
            slot = slots[1] + (slots[0] - slots[1]) * m[INNER]
            return (h ^ m[CORE], slot & 1, slot >> 1)

        in_specs.append(pl.BlockSpec((span // SHARE, 64, SHARE), index))
        args.append(expand)
        lanes = [64 * (0, 2, 1, 3)[slots[0]], 64 * (2, 0, 1, 3)[slots[1]]]
    if more is not None:
        in_specs.append(pl.BlockSpec((rows, span), lambda h, m: (0, h)))
        args.append(more)
    return pl.pallas_call(
        functools.partial(finish_kernel, role, row, rows, lanes, more is not None),
        grid_spec=pltpu.PrefetchScalarGridSpec(
            num_scalar_prefetch=1,
            grid=(2,),
            in_specs=in_specs,
            out_specs=pl.BlockSpec((rows, span), lambda h, m: (0, h)),
        ),
        out_shape=jax.ShapeDtypeStruct((rows, WIDE), jnp.bfloat16),
        compiler_params=params(32),
        cost_estimate=CHEAP,
    )(meta, *args)


def assemble_kernel(span, meta, count, own, one, two, inner_three, outer_three, out):
    z, c, inner = meta[ZPOS], meta[CORE], meta[INNER] == 1
    rows = own.shape[0]
    valid = lax.broadcasted_iota(jnp.int32, (rows, 1), 0) < count[0]

    def put(j, source):
        for h in range(2):
            at = pl.ds(pl.multiple_of((2 * j + h) * span, span), span)
            part = pl.ds(pl.multiple_of((h ^ c) * span, span), span)
            out[:, at] = jnp.where(valid, source[:, part], jnp.zeros((), jnp.bfloat16))

    put(z, own)
    put(z ^ 1, one)
    put(z ^ 2, two)

    @pl.when(inner)
    def _():
        put(z ^ 3, inner_three)

    @pl.when(jnp.logical_not(inner))
    def _():
        put(z ^ 3, outer_three)


def assemble(meta, count, *args):
    rows, wide = args[0].shape
    return pl.pallas_call(
        functools.partial(assemble_kernel, wide // 2),
        grid_spec=pltpu.PrefetchScalarGridSpec(
            num_scalar_prefetch=2,
            grid=(1,),
            in_specs=[pl.BlockSpec(a.shape, lambda n, m, k: (0, 0)) for a in args],
            out_specs=pl.BlockSpec((rows, 4 * wide), lambda n, m, k: (0, 0)),
        ),
        out_shape=jax.ShapeDtypeStruct((rows, 4 * wide), jnp.bfloat16),
        compiler_params=params(32),
        cost_estimate=CHEAP,
    )(meta, count, *args)


def line_of_four(hidden, down_weight, adapter_shrink, adapter_expand, block_adapter, block_rows):
    rows, feat = hidden.shape
    adp, _, rank = adapter_shrink.shape
    p = lax.axis_index("pool")
    t = lax.axis_index("tensor")
    tensors = lax.axis_size("tensor")
    z, c = p // 2, p % 2
    outer = (z == 0) | (z == 3)

    def exchange(x):
        return lax.all_to_all(x, "tensor", split_axis=0, concat_axis=0, tiled=True)

    place = jnp.stack([jnp.where(outer, 0, 1), c, z]).astype(jnp.int32)

    mid = send(hidden, MIDDLE)
    partner = send(hidden, XOR[1])
    cuts = [(lo, min(lo + 2 * TILE, feat)) for lo in range(0, feat, 2 * TILE)]
    pieces = [down_weight[lo:hi] for lo, hi in cuts]
    others = [send(w, SIBLING) for w in pieces]
    weights = [(down_weight, lo // TILE, w, 0) for (lo, _), w in zip(cuts, others)]

    def whole(x):
        return [(x, lo // TILE, (hi - lo) // TILE, i) for i, (lo, hi) in enumerate(cuts)]

    shares = exchange(
        adapter_expand.transpose(0, 2, 1).reshape(adp, rank, tensors, SHARE).transpose(2, 0, 1, 3)
    ).reshape(tensors, adp * rank, SHARE)
    label = jnp.zeros((16, SHARE), jnp.bfloat16).at[0, : block_adapter.shape[0]].set(block_adapter.astype(jnp.bfloat16))
    j_own = products(place, [Rows(whole(hidden), None, 0)], weights, BLOCK)

    ready = [partner, mid, j_own]
    far = send(after(ready, partner), MIDDLE)
    out_mid = send(after(ready, mid), OUTWARD)
    v_own = [send(after(ready, w), INWARD) for w in pieces[NEAR // (2 * TILE) :]]
    r_own = exchange(j_own)
    j_partner = products(place, [Rows(whole(partner), None, 0)], weights, BLOCK)
    r_partner = exchange(j_partner)
    j_mid = products(place, [Rows(whole(after([j_partner], mid)), 1, 0)], weights, BLOCK)
    r_mid = exchange(j_mid)
    shrink_w = adapter_shrink.transpose(0, 2, 1).reshape(adp * rank, feat)
    shrink_o = send(after([partner, mid], shrink_w), INWARD)
    shares = after([far, out_mid, j_mid], shares)

    def shares_of(s):
        return lax.dynamic_index_in_dim(shares, z ^ s, 0, keepdims=False)

    told = [send(jnp.concatenate([shares_of(s), label], axis=0), XOR[s]) for s in (1, 2, 3)]

    far_near = far[:, :NEAR]
    out_far = send(after([out_mid, *told], far_near), OUTWARD)
    j_third = products(
        place,
        [Rows(whole(after([r_partner, far_near, *told], far)), 1, 0), Rows(whole(out_mid), 0, 0)],
        weights,
        BLOCK,
    )
    r_third = exchange(j_third)
    v_other = [send(after([j_third], w), SIBLING) for w in v_own]

    held = jnp.concatenate([shares_of(0)] + [x[: adp * rank] for x in told]).reshape(4 * adp, rank, SHARE)
    held = (held, send(held, SIBLING))
    names = [block_adapter] + [x[adp * rank, : block_adapter.shape[0]].astype(jnp.int32) for x in told]
    name_m = jnp.where(outer, names[2], names[3])
    name_f = jnp.where(outer, names[3], names[2])
    meta = jnp.concatenate([place, names[0], names[1], name_m, name_f])
    shrink_mine = jnp.concatenate([shrink_w, after([j_third], shrink_o)], axis=0)
    shrink_other = send(shrink_mine, SIBLING)
    sums = shrink_sums(meta, [[hidden], [mid], [partner], [far]], [0, 2, 1, 3], shrink_mine, shrink_other, held)
    r_sums = exchange(sums)
    low, swapped = low_sums(r_sums)
    low = add(low, send(swapped, MIDDLE))
    low_out = send(low, OUTWARD)

    rest = [(a, 0, b, 0) for a, b in zip(v_own, v_other)] + weights[: NEAR // (2 * TILE)]
    j_fifth = products(
        place,
        [
            Rows([(after([sums], far), NEAR // TILE, 2, 0), (far, NEAR // TILE + 2, 1, 1)], 1, 0),
            Rows([(out_far, 0, 2, 2), (out_far, 2, 2, 3)], 0, 0),
        ],
        rest,
        BLOCK,
    )
    r_fifth = exchange(j_fifth)

    def term(inner_slot, outer_slot):
        return (low, low_out, r_sums, (inner_slot, outer_slot))

    x_partner = finish(meta, None, r_partner, 0, term(1, 1))
    home_partner = send(x_partner, XOR[1])
    x_two = finish(meta, None, r_third, 0, term(3, 2))
    home_two = send(x_two, XOR[2])
    x_mid = finish(meta, 1, r_mid, 0, term(2, 2))
    home_mid = send(x_mid, MIDDLE)
    x_own = finish(meta, None, r_own, 0, term(0, 0))
    r_fifth = after([x_partner, x_two, x_mid, x_own], r_fifth)
    x_far = finish(meta, 0, r_fifth, 0, term(3, 3))
    to_far = send(x_far, INWARD)
    to_far = after([home_partner, home_two, home_mid], to_far)
    home_far = send(finish(meta, 1, r_fifth, 0, more=to_far), ACROSS)
    count = lax.dynamic_slice_in_dim(block_rows, t, 1, 0)
    return assemble(meta, count, x_own, home_partner, home_two, home_mid, home_far)


def solution(mesh):
    in_specs = (
        P("pool", "tensor"),
        P("tensor", "pool"),
        P("pool", "tensor", None),
        P("pool", "tensor", None),
        P("pool"),
        P("pool"),
    )
    out_specs = P(("pool", "tensor"), None)
    body = line_of_four if dict(mesh.shape) == {"pool": 8, "tensor": 4} else general
    return jax.shard_map(body, mesh=mesh, in_specs=in_specs, out_specs=out_specs, check_vma=False)
```

```python
import functools

import jax
import jax.numpy as jnp
from jax import lax
from jax.experimental import pallas as pl
from jax.experimental.pallas import tpu as pltpu
from jax.sharding import PartitionSpec as P

BLOCK = 128
SCALE = 0.5


def general(hidden, down_weight, adapter_shrink, adapter_expand, block_adapter, block_rows):
    input_rows, feat = hidden.shape
    block_count = block_adapter.shape[0]
    column_span = adapter_expand.shape[1]
    tensor_pos = lax.axis_index("tensor")
    tensor_count = lax.axis_size("tensor")
    own_rows = input_rows // tensor_count
    blocks = hidden.reshape(block_count, BLOCK, feat)
    partial_value = jnp.dot(
        hidden,
        lax.all_gather(down_weight, "pool", axis=1, tiled=True),
        preferred_element_type=jnp.float32,
    )
    total = lax.psum_scatter(
        partial_value.astype(jnp.bfloat16), "tensor", scatter_dimension=0, tiled=True
    ).astype(jnp.float32)
    shrink_piece = lax.all_gather(adapter_shrink, "pool", axis=0, tiled=True)
    expand_piece = lax.all_gather(adapter_expand, "pool", axis=0, tiled=True)
    idents = jnp.arange(shrink_piece.shape[0], dtype=jnp.int32)
    pick = (block_adapter[:, None] == idents[None, :]).astype(jnp.bfloat16)
    first = jnp.einsum("bk,kfr->bfr", pick, shrink_piece, preferred_element_type=jnp.float32)
    second = jnp.einsum("bk,kcr->bcr", pick, expand_piece, preferred_element_type=jnp.float32)
    shrink = jnp.einsum(
        "bnf,bfr->bnr", blocks, first.astype(jnp.bfloat16), preferred_element_type=jnp.float32
    )
    summed_shrink = lax.psum(shrink.astype(jnp.bfloat16), "tensor")
    enlarged_rows = jnp.einsum(
        "bnr,bcr->bnc",
        summed_shrink,
        second.astype(jnp.bfloat16),
        preferred_element_type=jnp.float32,
    )
    adapter_delta_columns = (
        (SCALE * enlarged_rows).astype(jnp.bfloat16).reshape(input_rows, column_span)
    )
    delta_mine = lax.all_to_all(
        adapter_delta_columns, "tensor", split_axis=0, concat_axis=1, tiled=True
    )
    total = total + delta_mine.astype(jnp.float32)
    row_ids = tensor_pos * own_rows + jnp.arange(own_rows, dtype=jnp.int32)
    owning = (row_ids // BLOCK)[:, None] == jnp.arange(block_count, dtype=jnp.int32)[None, :]
    lengths = jnp.sum(jnp.where(owning, block_rows[None, :], 0), axis=1)
    valid = (row_ids % BLOCK < lengths).astype(jnp.float32)
    return (total * valid[:, None]).astype(jnp.bfloat16)


def dot(a, b):
    return jnp.dot(a, b, preferred_element_type=jnp.float32)


def on_line(pairs):
    return [(2 * a + c, 2 * b + c) for a, b in pairs for c in range(2)]


XOR = {s: on_line([(z, z ^ s) for z in range(4)]) for s in (1, 2, 3)}
MIDDLE = on_line([(1, 2), (2, 1)])
OUTWARD = on_line([(1, 0), (2, 3)])
INWARD = on_line([(0, 1), (3, 2)])
ACROSS = on_line([(1, 3), (2, 0)])
SIBLING = [(p, p ^ 1) for p in range(8)]

TILE = 512
NEAR = 4 * TILE
WIDE = 2048
SHARE = 512
INNER, CORE, ZPOS, NAMES = 0, 1, 2, 3
CHEAP = pl.CostEstimate(flops=1000, bytes_accessed=1000, transcendentals=0)


def send(x, pairs):
    return lax.ppermute(x, "pool", pairs)


def after(events, *xs):
    tied = lax.optimization_barrier((tuple(events), xs))
    return tied[1] if len(xs) > 1 else tied[1][0]


def params(limit):
    return pltpu.CompilerParams(vmem_limit_bytes=limit * 1024 * 1024)


class Rows:
    def __init__(self, parts, role, at):
        self.parts, self.role, self.at = parts, role, at
        self.rows = parts[0][0].shape[0]
        self.total = sum(part[2] for part in parts)


def block_sums(meta, slot, low, start, count, b):
    name = meta[NAMES + 4 * slot + b]
    chip = name >> 2
    place = ((((name >> 1) & 1) ^ meta[CORE]) << 2) + jnp.where(chip == meta[ZPOS], 0, 2) + (name & 1)
    place = jnp.where((chip == meta[ZPOS]) | (chip == (meta[ZPOS] ^ 1)), place, -1)
    value = jnp.zeros((count, 64), jnp.float32)
    for i in range(8):
        part = low[start + b * count : start + (b + 1) * count, i * 64 : i * 64 + 64]
        value = value + jnp.where(place == i, part, 0.0)
    return value.astype(jnp.bfloat16)


def accumulate(ref, rows, cols, value, k, first):
    if first:
        value = value + jnp.where(k == 0, 0.0, ref[rows, cols])
    else:
        value = value + ref[rows, cols]
    ref[rows, cols] = value


def times_transposed(x, a):
    return lax.dot_general(x, a, (((1,), (1,)), ((), ())), preferred_element_type=jnp.float32)


def products_kernel(jobs, weights, meta, *refs):
    refs = list(refs)
    xs = [[refs.pop(0) for _ in job.parts] for job in jobs]
    ws = [(refs.pop(0), refs.pop(0)) for _ in range(weights)]
    out, acc = refs
    k = pl.program_id(0)
    top = {0: 0, 1: 0}
    for x_parts, job in zip(xs, jobs):
        start = max(top.values()) if job.role is None else top[job.role]
        for role in top if job.role is None else (job.role,):
            top[role] = start + job.rows
        mine = slice(start, start + job.rows)
        role = True if job.role is None else meta[INNER] == job.role
        base = 0
        for x, (_, _, tiles, weight) in zip(x_parts, job.parts):

            def step(x=x, mine=mine, pair=ws[weight], first=base == 0):
                for h, w in enumerate(pair):
                    for n in range(0, WIDE // 2, 512):
                        at = slice(h * (WIDE // 2) + n, h * (WIDE // 2) + n + 512)
                        accumulate(acc, mine, at, dot(x[...], w[:, n : n + 512]), k, first)

            pl.when(role & (k >= base) & (k < base + tiles))(step)
            base += tiles

        def store(job=job, start=start):
            count = job.rows // 4
            for b in range(4):
                value = acc[start + b * count : start + (b + 1) * count, :]
                out[b, job.at : job.at + count, :] = value.astype(jnp.bfloat16)

        pl.when(role & (k == job.total - 1))(store)


def products(meta, jobs, weights, rows):
    steps = max(job.total for job in jobs)
    in_specs, args, uses = [], [], {}
    for job in jobs:
        base = 0
        for x, tile, tiles, weight in job.parts:

            def index(k, m, base=base, tile=tile, tiles=tiles, role=job.role):
                at = jnp.clip(k - base, 0, tiles - 1)
                if role is not None:
                    at = at * (m[INNER] if role == 1 else 1 - m[INNER])
                return (0, at + tile)

            in_specs.append(pl.BlockSpec((x.shape[0], TILE), index))
            args.append(x)
            for role in (0, 1) if job.role is None else (job.role,):
                uses[weight, role] = (base, tiles)
            base += tiles
    for i, (own, own_tile, other, other_tile) in enumerate(weights):
        for w, tile in ((own, own_tile), (other, other_tile)):

            def index(k, m, i=i, tile=tile):
                at = [jnp.clip(k - base, 0, tiles - 1) for base, tiles in (uses.get((i, r), (0, 1)) for r in (0, 1))]
                return (jnp.where(m[INNER] == 1, at[1], at[0]) + tile, 0)

            in_specs.append(pl.BlockSpec((TILE, w.shape[1]), index))
            args.append(w)
    both = sum(job.rows for job in jobs if job.role is None)
    height = both + max(sum(job.rows for job in jobs if job.role == r) for r in (0, 1))
    shape = (4, rows, WIDE)
    return pl.pallas_call(
        functools.partial(products_kernel, jobs, len(weights)),
        grid_spec=pltpu.PrefetchScalarGridSpec(
            num_scalar_prefetch=1,
            grid=(steps,),
            in_specs=in_specs,
            out_specs=pl.BlockSpec(shape, lambda k, m: (0, 0, 0)),
            scratch_shapes=[pltpu.VMEM((height, WIDE), jnp.float32)],
        ),
        out_shape=pltpu.HBM(shape, jnp.bfloat16),
        compiler_params=params(50),
        cost_estimate=CHEAP,
    )(meta, *args)


def shrink_kernel(tiles, slots, steps, meta, *refs):
    refs = list(refs)
    xs = [[refs.pop(0) for _ in part] for part in tiles]
    mine, other, held_mine, held_other, out, low = refs
    k = pl.program_id(0)
    inner = meta[INNER] == 1
    rows = BLOCK * 4
    for i, x_parts in enumerate(xs):
        base = 0
        for x, count in zip(x_parts, tiles[i]):

            @pl.when(inner & (k >= base) & (k < base + count))
            def _(i=i, x=x, first=base == 0):
                here = slice(i * rows, (i + 1) * rows)
                for h, a in enumerate((mine, other)):
                    accumulate(low, here, slice(h * 256, h * 256 + 256), times_transposed(x[...], a[...]), k, first)

            base += count

    @pl.when(inner & (k == steps - 1))
    def _():
        for i, slot in enumerate(slots):
            for b in range(4):
                at = 2 * SHARE + i * 64
                out[b, :, at : at + 64] = block_sums(meta, slot, low, i * rows, BLOCK, b)

    @pl.when(k == 0)
    def _():
        for b in range(4):
            for slot in range(4):
                name = meta[NAMES + 4 * slot + b]
                index = 2 * ((name >> 2) ^ meta[ZPOS]) + (name & 1)
                value = jnp.where(((name >> 1) & 1) == meta[CORE], held_mine[index], held_other[index])
                at = slot // 2 * SHARE
                out[b, slot % 2 * 64 : slot % 2 * 64 + 64, at : at + SHARE] = value


def shrink_sums(meta, xs, slots, mine, other, held):
    tiles = [[part.shape[1] // TILE for part in x] for x in xs]
    steps = sum(tiles[0])
    in_specs, args = [], []
    for x, counts in zip(xs, tiles):
        base = 0
        for part, count in zip(x, counts):

            def index(k, m, base=base, count=count):
                return (0, jnp.clip(k - base, 0, count - 1) * m[INNER])

            in_specs.append(pl.BlockSpec((part.shape[0], TILE), index))
            args.append(part)
            base += count
    for a in (mine, other):
        in_specs.append(pl.BlockSpec((a.shape[0], TILE), lambda k, m: (0, k * m[INNER])))
        args.append(a)
    for a in held:
        in_specs.append(pl.BlockSpec(a.shape, lambda k, m: (0, 0, 0)))
        args.append(a)
    shape = (4, BLOCK, 2 * SHARE + 256)
    return pl.pallas_call(
        functools.partial(shrink_kernel, tiles, slots, steps),
        grid_spec=pltpu.PrefetchScalarGridSpec(
            num_scalar_prefetch=1,
            grid=(steps,),
            in_specs=in_specs,
            out_specs=pl.BlockSpec(shape, lambda k, m: (0, 0, 0)),
            scratch_shapes=[pltpu.VMEM((4 * BLOCK * len(xs), 512), jnp.float32)],
        ),
        out_shape=pltpu.HBM(shape, jnp.bfloat16),
        compiler_params=params(40),
        cost_estimate=CHEAP,
    )(meta, *args)


def low_kernel(x, out, swapped):
    value = x[0].astype(jnp.float32)
    for b in range(1, 4):
        value = value + x[b].astype(jnp.float32)
    value = value.astype(jnp.bfloat16)
    out[...] = value
    swapped[...] = jnp.concatenate([value[:, i * 64 : i * 64 + 64] for i in (1, 0, 3, 2)], axis=1)


def low_sums(x):
    shape = jax.ShapeDtypeStruct((BLOCK, 256), jnp.bfloat16)
    whole = pl.BlockSpec((BLOCK, 256), lambda i: (0, 0))
    return pl.pallas_call(
        low_kernel,
        grid=(1,),
        in_specs=[pl.BlockSpec((4, BLOCK, 256), lambda i: (0, 0, 2 * SHARE // 256))],
        out_specs=(whole, whole),
        out_shape=(shape, shape),
        cost_estimate=CHEAP,
    )(x)


def add_kernel(x, y, out):
    out[...] = (x[...].astype(jnp.float32) + y[...].astype(jnp.float32)).astype(jnp.bfloat16)


def add(x, y):
    return pl.pallas_call(add_kernel, out_shape=jax.ShapeDtypeStruct(x.shape, x.dtype), cost_estimate=CHEAP)(x, y)


def finish_kernel(role, row, rows, lanes, has_more, meta, *refs):
    refs = list(refs)
    part = refs.pop(0)
    if lanes:
        low_in, low_out, expand = refs.pop(0), refs.pop(0), refs.pop(0)
    more = refs.pop(0) if has_more else None
    out = refs.pop(0)

    def run():
        total = part[0, row : row + rows, :].astype(jnp.float32)
        for b in range(1, 4):
            total = total + part[b, row : row + rows, :].astype(jnp.float32)
        if lanes:
            x = low_in[:rows, lanes[0] : lanes[0] + 64]
            y = low_out[:rows, lanes[1] : lanes[1] + 64]
            x = jnp.where(meta[INNER] == 1, x, y)
            delta = [dot(x, expand[i]) for i in range(expand.shape[0])]
            total = total + SCALE * jnp.concatenate(delta, axis=1)
        if has_more:
            total = total + more[...].astype(jnp.float32)
        out[...] = total.astype(jnp.bfloat16)

    if role is None:
        run()
    else:
        pl.when(meta[INNER] == role)(run)


def finish(meta, role, part, row, low=None, more=None, rows=BLOCK):
    span = WIDE // 2
    in_specs = [pl.BlockSpec((4, part.shape[1], span), lambda h, m: (0, 0, h))]
    args = [part]
    lanes = None
    if low is not None:
        *sums, expand, slots = low
        for x in sums:
            in_specs.append(pl.BlockSpec(x.shape, lambda h, m: (0, 0)))
            args.append(x)

        def index(h, m):
            slot = slots[1] + (slots[0] - slots[1]) * m[INNER]
            return (h ^ m[CORE], slot & 1, slot >> 1)

        in_specs.append(pl.BlockSpec((span // SHARE, 64, SHARE), index))
        args.append(expand)
        lanes = [64 * (0, 2, 1, 3)[slots[0]], 64 * (2, 0, 1, 3)[slots[1]]]
    if more is not None:
        in_specs.append(pl.BlockSpec((rows, span), lambda h, m: (0, h)))
        args.append(more)
    return pl.pallas_call(
        functools.partial(finish_kernel, role, row, rows, lanes, more is not None),
        grid_spec=pltpu.PrefetchScalarGridSpec(
            num_scalar_prefetch=1,
            grid=(2,),
            in_specs=in_specs,
            out_specs=pl.BlockSpec((rows, span), lambda h, m: (0, h)),
        ),
        out_shape=jax.ShapeDtypeStruct((rows, WIDE), jnp.bfloat16),
        compiler_params=params(32),
        cost_estimate=CHEAP,
    )(meta, *args)


def assemble_kernel(span, meta, count, own, one, two, inner_three, outer_three, out):
    z, c, inner = meta[ZPOS], meta[CORE], meta[INNER] == 1
    rows = own.shape[0]
    valid = lax.broadcasted_iota(jnp.int32, (rows, 1), 0) < count[0]

    def put(j, source):
        for h in range(2):
            at = pl.ds(pl.multiple_of((2 * j + h) * span, span), span)
            part = pl.ds(pl.multiple_of((h ^ c) * span, span), span)
            out[:, at] = jnp.where(valid, source[:, part], jnp.zeros((), jnp.bfloat16))

    put(z, own)
    put(z ^ 1, one)
    put(z ^ 2, two)

    @pl.when(inner)
    def _():
        put(z ^ 3, inner_three)

    @pl.when(jnp.logical_not(inner))
    def _():
        put(z ^ 3, outer_three)


def assemble(meta, count, *args):
    rows, wide = args[0].shape
    return pl.pallas_call(
        functools.partial(assemble_kernel, wide // 2),
        grid_spec=pltpu.PrefetchScalarGridSpec(
            num_scalar_prefetch=2,
            grid=(1,),
            in_specs=[pl.BlockSpec(a.shape, lambda n, m, k: (0, 0)) for a in args],
            out_specs=pl.BlockSpec((rows, 4 * wide), lambda n, m, k: (0, 0)),
        ),
        out_shape=jax.ShapeDtypeStruct((rows, 4 * wide), jnp.bfloat16),
        compiler_params=params(32),
        cost_estimate=CHEAP,
    )(meta, count, *args)


def line_of_four(hidden, down_weight, adapter_shrink, adapter_expand, block_adapter, block_rows):
    rows, feat = hidden.shape
    adp, _, rank = adapter_shrink.shape
    p = lax.axis_index("pool")
    t = lax.axis_index("tensor")
    tensors = lax.axis_size("tensor")
    z, c = p // 2, p % 2
    outer = (z == 0) | (z == 3)

    def exchange(x):
        return lax.all_to_all(x, "tensor", split_axis=0, concat_axis=0, tiled=True)

    place = jnp.stack([jnp.where(outer, 0, 1), c, z]).astype(jnp.int32)

    mid = send(hidden, MIDDLE)
    partner = send(hidden, XOR[1])
    cuts = [(lo, min(lo + 2 * TILE, feat)) for lo in range(0, feat, 2 * TILE)]
    pieces = [down_weight[lo:hi] for lo, hi in cuts]
    others = [send(w, SIBLING) for w in pieces]
    weights = [(down_weight, lo // TILE, w, 0) for (lo, _), w in zip(cuts, others)]

    def whole(x):
        return [(x, lo // TILE, (hi - lo) // TILE, i) for i, (lo, hi) in enumerate(cuts)]

    shares = exchange(
        adapter_expand.transpose(0, 2, 1).reshape(adp, rank, tensors, SHARE).transpose(2, 0, 1, 3)
    ).reshape(tensors, adp * rank, SHARE)
    label = jnp.zeros((16, SHARE), jnp.bfloat16).at[0, : block_adapter.shape[0]].set(block_adapter.astype(jnp.bfloat16))
    j_own = products(place, [Rows(whole(hidden), None, 0)], weights, BLOCK)
    shares = after([j_own], shares)

    def shares_of(s):
        return lax.dynamic_index_in_dim(shares, z ^ s, 0, keepdims=False)

    told = [send(jnp.concatenate([shares_of(s), label], axis=0), XOR[s]) for s in (1, 2, 3)]

    ready = [partner, mid, *told]
    far = send(after(ready, partner), MIDDLE)
    out_mid = send(after(ready, mid), OUTWARD)
    shrink_w = adapter_shrink.transpose(0, 2, 1).reshape(adp * rank, feat)
    shrink_o = send(after(ready, shrink_w), INWARD)
    v_own = [send(after([shrink_o], w), INWARD) for w in pieces[NEAR // (2 * TILE) :]]
    r_own = exchange(j_own)
    j_partner = products(place, [Rows(whole(partner), None, 0)], weights, BLOCK)
    r_partner = exchange(j_partner)
    j_mid = products(place, [Rows(whole(after([j_partner], mid)), 1, 0)], weights, BLOCK)
    r_mid = exchange(j_mid)
    far_near = far[:, :NEAR]
    out_far = send(after([out_mid, shrink_o, j_partner], far_near), OUTWARD)
    j_third = products(
        place,
        [Rows(whole(after([r_partner, far_near], far)), 1, 0), Rows(whole(out_mid), 0, 0)],
        weights,
        BLOCK,
    )
    r_third = exchange(j_third)
    v_other = [send(after([j_third], w), SIBLING) for w in v_own]

    held = jnp.concatenate([shares_of(0)] + [x[: adp * rank] for x in told]).reshape(4 * adp, rank, SHARE)
    held = (held, send(held, SIBLING))
    names = [block_adapter] + [x[adp * rank, : block_adapter.shape[0]].astype(jnp.int32) for x in told]
    name_m = jnp.where(outer, names[2], names[3])
    name_f = jnp.where(outer, names[3], names[2])
    meta = jnp.concatenate([place, names[0], names[1], name_m, name_f])
    shrink_mine = jnp.concatenate([shrink_w, after([j_third], shrink_o)], axis=0)
    shrink_other = send(shrink_mine, SIBLING)
    sums = shrink_sums(meta, [[hidden], [mid], [partner], [far]], [0, 2, 1, 3], shrink_mine, shrink_other, held)
    r_sums = exchange(sums)
    low, swapped = low_sums(r_sums)
    low = add(low, send(swapped, MIDDLE))
    low_out = send(low, OUTWARD)

    rest = [(a, 0, b, 0) for a, b in zip(v_own, v_other)] + weights[: NEAR // (2 * TILE)]
    j_fifth = products(
        place,
        [
            Rows([(after([sums], far), NEAR // TILE, 2, 0), (far, NEAR // TILE + 2, 1, 1)], 1, 0),
            Rows([(out_far, 0, 2, 2), (out_far, 2, 2, 3)], 0, 0),
        ],
        rest,
        BLOCK,
    )
    r_fifth = exchange(j_fifth)

    def term(inner_slot, outer_slot):
        return (low, low_out, r_sums, (inner_slot, outer_slot))

    x_partner = finish(meta, None, r_partner, 0, term(1, 1))
    home_partner = send(x_partner, XOR[1])
    x_two = finish(meta, None, r_third, 0, term(3, 2))
    home_two = send(x_two, XOR[2])
    x_mid = finish(meta, 1, r_mid, 0, term(2, 2))
    home_mid = send(x_mid, MIDDLE)
    x_own = finish(meta, None, r_own, 0, term(0, 0))
    r_fifth = after([x_partner, x_two, x_mid, x_own], r_fifth)
    x_far = finish(meta, 0, r_fifth, 0, term(3, 3))
    to_far = send(x_far, INWARD)
    to_far = after([home_partner, home_two, home_mid], to_far)
    home_far = send(finish(meta, 1, r_fifth, 0, more=to_far), ACROSS)
    count = lax.dynamic_slice_in_dim(block_rows, t, 1, 0)
    return assemble(meta, count, x_own, home_partner, home_two, home_mid, home_far)


def solution(mesh):
    in_specs = (
        P("pool", "tensor"),
        P("tensor", "pool"),
        P("pool", "tensor", None),
        P("pool", "tensor", None),
        P("pool"),
        P("pool"),
    )
    out_specs = P(("pool", "tensor"), None)
    body = line_of_four if dict(mesh.shape) == {"pool": 8, "tensor": 4} else general
    return jax.shard_map(body, mesh=mesh, in_specs=in_specs, out_specs=out_specs, check_vma=False)
```

```python
import functools

import jax
import jax.numpy as jnp
from jax import lax
from jax.experimental import pallas as pl
from jax.experimental.pallas import tpu as pltpu
from jax.sharding import PartitionSpec as P

BLOCK = 128
SCALE = 0.5


def general(hidden, down_weight, adapter_shrink, adapter_expand, block_adapter, block_rows):
    input_rows, feat = hidden.shape
    block_count = block_adapter.shape[0]
    column_span = adapter_expand.shape[1]
    tensor_pos = lax.axis_index("tensor")
    tensor_count = lax.axis_size("tensor")
    own_rows = input_rows // tensor_count
    blocks = hidden.reshape(block_count, BLOCK, feat)
    partial_value = jnp.dot(
        hidden,
        lax.all_gather(down_weight, "pool", axis=1, tiled=True),
        preferred_element_type=jnp.float32,
    )
    total = lax.psum_scatter(
        partial_value.astype(jnp.bfloat16), "tensor", scatter_dimension=0, tiled=True
    ).astype(jnp.float32)
    shrink_piece = lax.all_gather(adapter_shrink, "pool", axis=0, tiled=True)
    expand_piece = lax.all_gather(adapter_expand, "pool", axis=0, tiled=True)
    idents = jnp.arange(shrink_piece.shape[0], dtype=jnp.int32)
    pick = (block_adapter[:, None] == idents[None, :]).astype(jnp.bfloat16)
    first = jnp.einsum("bk,kfr->bfr", pick, shrink_piece, preferred_element_type=jnp.float32)
    second = jnp.einsum("bk,kcr->bcr", pick, expand_piece, preferred_element_type=jnp.float32)
    shrink = jnp.einsum(
        "bnf,bfr->bnr", blocks, first.astype(jnp.bfloat16), preferred_element_type=jnp.float32
    )
    summed_shrink = lax.psum(shrink.astype(jnp.bfloat16), "tensor")
    enlarged_rows = jnp.einsum(
        "bnr,bcr->bnc",
        summed_shrink,
        second.astype(jnp.bfloat16),
        preferred_element_type=jnp.float32,
    )
    adapter_delta_columns = (
        (SCALE * enlarged_rows).astype(jnp.bfloat16).reshape(input_rows, column_span)
    )
    delta_mine = lax.all_to_all(
        adapter_delta_columns, "tensor", split_axis=0, concat_axis=1, tiled=True
    )
    total = total + delta_mine.astype(jnp.float32)
    row_ids = tensor_pos * own_rows + jnp.arange(own_rows, dtype=jnp.int32)
    owning = (row_ids // BLOCK)[:, None] == jnp.arange(block_count, dtype=jnp.int32)[None, :]
    lengths = jnp.sum(jnp.where(owning, block_rows[None, :], 0), axis=1)
    valid = (row_ids % BLOCK < lengths).astype(jnp.float32)
    return (total * valid[:, None]).astype(jnp.bfloat16)


def dot(a, b):
    return jnp.dot(a, b, preferred_element_type=jnp.float32)


def on_line(pairs):
    return [(2 * a + c, 2 * b + c) for a, b in pairs for c in range(2)]


XOR = {s: on_line([(z, z ^ s) for z in range(4)]) for s in (1, 2, 3)}
MIDDLE = on_line([(1, 2), (2, 1)])
OUTWARD = on_line([(1, 0), (2, 3)])
INWARD = on_line([(0, 1), (3, 2)])
ACROSS = on_line([(1, 3), (2, 0)])
SIBLING = [(p, p ^ 1) for p in range(8)]

TILE = 512
NEAR = 4 * TILE
WIDE = 2048
SHARE = 512
INNER, CORE, ZPOS, NAMES = 0, 1, 2, 3
CHEAP = pl.CostEstimate(flops=1000, bytes_accessed=1000, transcendentals=0)


def send(x, pairs):
    return lax.ppermute(x, "pool", pairs)


def after(events, *xs):
    tied = lax.optimization_barrier((tuple(events), xs))
    return tied[1] if len(xs) > 1 else tied[1][0]


def params(limit):
    return pltpu.CompilerParams(vmem_limit_bytes=limit * 1024 * 1024)


class Rows:
    def __init__(self, parts, role, at):
        self.parts, self.role, self.at = parts, role, at
        self.rows = parts[0][0].shape[0]
        self.total = sum(part[2] for part in parts)


def block_sums(meta, slot, low, start, count, b):
    name = meta[NAMES + 4 * slot + b]
    chip = name >> 2
    place = ((((name >> 1) & 1) ^ meta[CORE]) << 2) + jnp.where(chip == meta[ZPOS], 0, 2) + (name & 1)
    place = jnp.where((chip == meta[ZPOS]) | (chip == (meta[ZPOS] ^ 1)), place, -1)
    value = jnp.zeros((count, 64), jnp.float32)
    for i in range(8):
        part = low[start + b * count : start + (b + 1) * count, i * 64 : i * 64 + 64]
        value = value + jnp.where(place == i, part, 0.0)
    return value.astype(jnp.bfloat16)


def accumulate(ref, rows, cols, value, k, first):
    if first:
        value = value + jnp.where(k == 0, 0.0, ref[rows, cols])
    else:
        value = value + ref[rows, cols]
    ref[rows, cols] = value


def times_transposed(x, a):
    return lax.dot_general(x, a, (((1,), (1,)), ((), ())), preferred_element_type=jnp.float32)


def products_kernel(jobs, weights, meta, *refs):
    refs = list(refs)
    xs = [[refs.pop(0) for _ in job.parts] for job in jobs]
    ws = [(refs.pop(0), refs.pop(0)) for _ in range(weights)]
    out, acc = refs
    k = pl.program_id(0)
    top = {0: 0, 1: 0}
    for x_parts, job in zip(xs, jobs):
        start = max(top.values()) if job.role is None else top[job.role]
        for role in top if job.role is None else (job.role,):
            top[role] = start + job.rows
        mine = slice(start, start + job.rows)
        role = True if job.role is None else meta[INNER] == job.role
        base = 0
        for x, (_, _, tiles, weight) in zip(x_parts, job.parts):

            def step(x=x, mine=mine, pair=ws[weight], first=base == 0):
                for h, w in enumerate(pair):
                    for n in range(0, WIDE // 2, 512):
                        at = slice(h * (WIDE // 2) + n, h * (WIDE // 2) + n + 512)
                        accumulate(acc, mine, at, dot(x[...], w[:, n : n + 512]), k, first)

            pl.when(role & (k >= base) & (k < base + tiles))(step)
            base += tiles

        def store(job=job, start=start):
            count = job.rows // 4
            for b in range(4):
                value = acc[start + b * count : start + (b + 1) * count, :]
                out[b, job.at : job.at + count, :] = value.astype(jnp.bfloat16)

        pl.when(role & (k == job.total - 1))(store)


def products(meta, jobs, weights, rows):
    steps = max(job.total for job in jobs)
    in_specs, args, uses = [], [], {}
    for job in jobs:
        base = 0
        for x, tile, tiles, weight in job.parts:

            def index(k, m, base=base, tile=tile, tiles=tiles, role=job.role):
                at = jnp.clip(k - base, 0, tiles - 1)
                if role is not None:
                    at = at * (m[INNER] if role == 1 else 1 - m[INNER])
                return (0, at + tile)

            in_specs.append(pl.BlockSpec((x.shape[0], TILE), index))
            args.append(x)
            for role in (0, 1) if job.role is None else (job.role,):
                uses[weight, role] = (base, tiles)
            base += tiles
    for i, (own, own_tile, other, other_tile) in enumerate(weights):
        for w, tile in ((own, own_tile), (other, other_tile)):

            def index(k, m, i=i, tile=tile):
                at = [jnp.clip(k - base, 0, tiles - 1) for base, tiles in (uses.get((i, r), (0, 1)) for r in (0, 1))]
                return (jnp.where(m[INNER] == 1, at[1], at[0]) + tile, 0)

            in_specs.append(pl.BlockSpec((TILE, w.shape[1]), index))
            args.append(w)
    both = sum(job.rows for job in jobs if job.role is None)
    height = both + max(sum(job.rows for job in jobs if job.role == r) for r in (0, 1))
    shape = (4, rows, WIDE)
    return pl.pallas_call(
        functools.partial(products_kernel, jobs, len(weights)),
        grid_spec=pltpu.PrefetchScalarGridSpec(
            num_scalar_prefetch=1,
            grid=(steps,),
            in_specs=in_specs,
            out_specs=pl.BlockSpec(shape, lambda k, m: (0, 0, 0)),
            scratch_shapes=[pltpu.VMEM((height, WIDE), jnp.float32)],
        ),
        out_shape=pltpu.HBM(shape, jnp.bfloat16),
        compiler_params=params(50),
        cost_estimate=CHEAP,
    )(meta, *args)


def shrink_kernel(tiles, slots, steps, meta, *refs):
    refs = list(refs)
    xs = [[refs.pop(0) for _ in part] for part in tiles]
    mine, other, held_mine, held_other, out, low = refs
    k = pl.program_id(0)
    inner = meta[INNER] == 1
    rows = BLOCK * 4
    for i, x_parts in enumerate(xs):
        base = 0
        for x, count in zip(x_parts, tiles[i]):

            @pl.when(inner & (k >= base) & (k < base + count))
            def _(i=i, x=x, first=base == 0):
                here = slice(i * rows, (i + 1) * rows)
                for h, a in enumerate((mine, other)):
                    accumulate(low, here, slice(h * 256, h * 256 + 256), times_transposed(x[...], a[...]), k, first)

            base += count

    @pl.when(inner & (k == steps - 1))
    def _():
        for i, slot in enumerate(slots):
            for b in range(4):
                at = 2 * SHARE + i * 64
                out[b, :, at : at + 64] = block_sums(meta, slot, low, i * rows, BLOCK, b)

    @pl.when(k == 0)
    def _():
        for b in range(4):
            for slot in range(4):
                name = meta[NAMES + 4 * slot + b]
                index = 2 * ((name >> 2) ^ meta[ZPOS]) + (name & 1)
                value = jnp.where(((name >> 1) & 1) == meta[CORE], held_mine[index], held_other[index])
                at = slot // 2 * SHARE
                out[b, slot % 2 * 64 : slot % 2 * 64 + 64, at : at + SHARE] = value


def shrink_sums(meta, xs, slots, mine, other, held):
    tiles = [[part.shape[1] // TILE for part in x] for x in xs]
    steps = sum(tiles[0])
    in_specs, args = [], []
    for x, counts in zip(xs, tiles):
        base = 0
        for part, count in zip(x, counts):

            def index(k, m, base=base, count=count):
                return (0, jnp.clip(k - base, 0, count - 1) * m[INNER])

            in_specs.append(pl.BlockSpec((part.shape[0], TILE), index))
            args.append(part)
            base += count
    for a in (mine, other):
        in_specs.append(pl.BlockSpec((a.shape[0], TILE), lambda k, m: (0, k * m[INNER])))
        args.append(a)
    for a in held:
        in_specs.append(pl.BlockSpec(a.shape, lambda k, m: (0, 0, 0)))
        args.append(a)
    shape = (4, BLOCK, 2 * SHARE + 256)
    return pl.pallas_call(
        functools.partial(shrink_kernel, tiles, slots, steps),
        grid_spec=pltpu.PrefetchScalarGridSpec(
            num_scalar_prefetch=1,
            grid=(steps,),
            in_specs=in_specs,
            out_specs=pl.BlockSpec(shape, lambda k, m: (0, 0, 0)),
            scratch_shapes=[pltpu.VMEM((4 * BLOCK * len(xs), 512), jnp.float32)],
        ),
        out_shape=pltpu.HBM(shape, jnp.bfloat16),
        compiler_params=params(40),
        cost_estimate=CHEAP,
    )(meta, *args)


def low_kernel(x, out, swapped):
    value = x[0].astype(jnp.float32)
    for b in range(1, 4):
        value = value + x[b].astype(jnp.float32)
    value = value.astype(jnp.bfloat16)
    out[...] = value
    swapped[...] = jnp.concatenate([value[:, i * 64 : i * 64 + 64] for i in (1, 0, 3, 2)], axis=1)


def low_sums(x):
    shape = jax.ShapeDtypeStruct((BLOCK, 256), jnp.bfloat16)
    whole = pl.BlockSpec((BLOCK, 256), lambda i: (0, 0))
    return pl.pallas_call(
        low_kernel,
        grid=(1,),
        in_specs=[pl.BlockSpec((4, BLOCK, 256), lambda i: (0, 0, 2 * SHARE // 256))],
        out_specs=(whole, whole),
        out_shape=(shape, shape),
        cost_estimate=CHEAP,
    )(x)


def add_kernel(x, y, out):
    out[...] = (x[...].astype(jnp.float32) + y[...].astype(jnp.float32)).astype(jnp.bfloat16)


def add(x, y):
    return pl.pallas_call(add_kernel, out_shape=jax.ShapeDtypeStruct(x.shape, x.dtype), cost_estimate=CHEAP)(x, y)


def finish_kernel(role, row, rows, lanes, has_more, meta, *refs):
    refs = list(refs)
    part = refs.pop(0)
    if lanes:
        low_in, low_out, expand = refs.pop(0), refs.pop(0), refs.pop(0)
    more = refs.pop(0) if has_more else None
    out = refs.pop(0)

    def run():
        total = part[0, row : row + rows, :].astype(jnp.float32)
        for b in range(1, 4):
            total = total + part[b, row : row + rows, :].astype(jnp.float32)
        if lanes:
            x = low_in[:rows, lanes[0] : lanes[0] + 64]
            y = low_out[:rows, lanes[1] : lanes[1] + 64]
            x = jnp.where(meta[INNER] == 1, x, y)
            delta = [dot(x, expand[i]) for i in range(expand.shape[0])]
            total = total + SCALE * jnp.concatenate(delta, axis=1)
        if has_more:
            total = total + more[...].astype(jnp.float32)
        out[...] = total.astype(jnp.bfloat16)

    if role is None:
        run()
    else:
        pl.when(meta[INNER] == role)(run)


def finish(meta, role, part, row, low=None, more=None, rows=BLOCK):
    span = WIDE // 2
    in_specs = [pl.BlockSpec((4, part.shape[1], span), lambda h, m: (0, 0, h))]
    args = [part]
    lanes = None
    if low is not None:
        *sums, expand, slots = low
        for x in sums:
            in_specs.append(pl.BlockSpec(x.shape, lambda h, m: (0, 0)))
            args.append(x)

        def index(h, m):
            slot = slots[1] + (slots[0] - slots[1]) * m[INNER]
            return (h ^ m[CORE], slot & 1, slot >> 1)

        in_specs.append(pl.BlockSpec((span // SHARE, 64, SHARE), index))
        args.append(expand)
        lanes = [64 * (0, 2, 1, 3)[slots[0]], 64 * (2, 0, 1, 3)[slots[1]]]
    if more is not None:
        in_specs.append(pl.BlockSpec((rows, span), lambda h, m: (0, h)))
        args.append(more)
    return pl.pallas_call(
        functools.partial(finish_kernel, role, row, rows, lanes, more is not None),
        grid_spec=pltpu.PrefetchScalarGridSpec(
            num_scalar_prefetch=1,
            grid=(2,),
            in_specs=in_specs,
            out_specs=pl.BlockSpec((rows, span), lambda h, m: (0, h)),
        ),
        out_shape=jax.ShapeDtypeStruct((rows, WIDE), jnp.bfloat16),
        compiler_params=params(32),
        cost_estimate=CHEAP,
    )(meta, *args)


def assemble_kernel(span, meta, count, own, one, two, inner_three, outer_three, out):
    z, c, inner = meta[ZPOS], meta[CORE], meta[INNER] == 1
    rows = own.shape[0]
    valid = lax.broadcasted_iota(jnp.int32, (rows, 1), 0) < count[0]

    def put(j, source):
        for h in range(2):
            at = pl.ds(pl.multiple_of((2 * j + h) * span, span), span)
            part = pl.ds(pl.multiple_of((h ^ c) * span, span), span)
            out[:, at] = jnp.where(valid, source[:, part], jnp.zeros((), jnp.bfloat16))

    put(z, own)
    put(z ^ 1, one)
    put(z ^ 2, two)

    @pl.when(inner)
    def _():
        put(z ^ 3, inner_three)

    @pl.when(jnp.logical_not(inner))
    def _():
        put(z ^ 3, outer_three)


def assemble(meta, count, *args):
    rows, wide = args[0].shape
    return pl.pallas_call(
        functools.partial(assemble_kernel, wide // 2),
        grid_spec=pltpu.PrefetchScalarGridSpec(
            num_scalar_prefetch=2,
            grid=(1,),
            in_specs=[pl.BlockSpec(a.shape, lambda n, m, k: (0, 0)) for a in args],
            out_specs=pl.BlockSpec((rows, 4 * wide), lambda n, m, k: (0, 0)),
        ),
        out_shape=jax.ShapeDtypeStruct((rows, 4 * wide), jnp.bfloat16),
        compiler_params=params(32),
        cost_estimate=CHEAP,
    )(meta, count, *args)


def line_of_four(hidden, down_weight, adapter_shrink, adapter_expand, block_adapter, block_rows):
    rows, feat = hidden.shape
    adp, _, rank = adapter_shrink.shape
    p = lax.axis_index("pool")
    t = lax.axis_index("tensor")
    tensors = lax.axis_size("tensor")
    z, c = p // 2, p % 2
    outer = (z == 0) | (z == 3)

    def exchange(x):
        return lax.all_to_all(x, "tensor", split_axis=0, concat_axis=0, tiled=True)

    place = jnp.stack([jnp.where(outer, 0, 1), c, z]).astype(jnp.int32)

    mid = send(hidden, MIDDLE)
    partner = send(hidden, XOR[1])
    cuts = [(lo, min(lo + 2 * TILE, feat)) for lo in range(0, feat, 2 * TILE)]
    pieces = [down_weight[lo:hi] for lo, hi in cuts]
    others = [send(w, SIBLING) for w in pieces]
    weights = [(down_weight, lo // TILE, w, 0) for (lo, _), w in zip(cuts, others)]

    def whole(x):
        return [(x, lo // TILE, (hi - lo) // TILE, i) for i, (lo, hi) in enumerate(cuts)]

    shares = exchange(
        adapter_expand.transpose(0, 2, 1).reshape(adp, rank, tensors, SHARE).transpose(2, 0, 1, 3)
    ).reshape(tensors, adp * rank, SHARE)
    label = jnp.zeros((16, SHARE), jnp.bfloat16).at[0, : block_adapter.shape[0]].set(block_adapter.astype(jnp.bfloat16))
    j_own = products(place, [Rows(whole(hidden), None, 0)], weights, BLOCK)
    shares = after([j_own], shares)

    def shares_of(s):
        return lax.dynamic_index_in_dim(shares, z ^ s, 0, keepdims=False)

    told = [send(jnp.concatenate([shares_of(s), label], axis=0), XOR[s]) for s in (1, 2, 3)]

    ready = [partner, mid, *told]
    far = send(after(ready, partner), MIDDLE)
    out_mid = send(after(ready, mid), OUTWARD)
    shrink_w = adapter_shrink.transpose(0, 2, 1).reshape(adp * rank, feat)
    shrink_o = send(after(ready, shrink_w), INWARD)
    v_own = [send(after([shrink_o], w), INWARD) for w in pieces[NEAR // (2 * TILE) :]]
    r_own = exchange(j_own)
    j_partner = products(place, [Rows(whole(partner), None, 0)], weights, BLOCK)
    r_partner = exchange(j_partner)
    j_mid = products(place, [Rows(whole(after([j_partner], mid)), 1, 0)], weights, BLOCK)
    r_mid = exchange(j_mid)
    far_near = far[:, :NEAR]
    out_far = send(after([out_mid, shrink_o, j_partner], far_near), OUTWARD)
    j_third = products(
        place,
        [Rows(whole(after([r_partner, far_near], far)), 1, 0), Rows(whole(out_mid), 0, 0)],
        weights,
        BLOCK,
    )
    r_third = exchange(j_third)
    v_other = [send(after([far_near], w), SIBLING) for w in v_own]

    held = jnp.concatenate([shares_of(0)] + [x[: adp * rank] for x in told]).reshape(4 * adp, rank, SHARE)
    held = (held, send(held, SIBLING))
    names = [block_adapter] + [x[adp * rank, : block_adapter.shape[0]].astype(jnp.int32) for x in told]
    name_m = jnp.where(outer, names[2], names[3])
    name_f = jnp.where(outer, names[3], names[2])
    meta = jnp.concatenate([place, names[0], names[1], name_m, name_f])
    shrink_mine = jnp.concatenate([shrink_w, after([j_partner], shrink_o)], axis=0)
    shrink_other = send(shrink_mine, SIBLING)
    sums = shrink_sums(meta, [[after([j_third], hidden)], [mid], [partner], [far]], [0, 2, 1, 3], shrink_mine, shrink_other, held)
    r_sums = exchange(sums)
    low, swapped = low_sums(r_sums)
    low = add(low, send(swapped, MIDDLE))
    low_out = send(low, OUTWARD)

    rest = [(a, 0, b, 0) for a, b in zip(v_own, v_other)] + weights[: NEAR // (2 * TILE)]
    j_fifth = products(
        place,
        [
            Rows([(after([sums], far), NEAR // TILE, 2, 0), (far, NEAR // TILE + 2, 1, 1)], 1, 0),
            Rows([(out_far, 0, 2, 2), (out_far, 2, 2, 3)], 0, 0),
        ],
        rest,
        BLOCK,
    )
    r_fifth = exchange(j_fifth)

    def term(inner_slot, outer_slot):
        return (low, low_out, r_sums, (inner_slot, outer_slot))

    x_partner = finish(meta, None, r_partner, 0, term(1, 1))
    home_partner = send(x_partner, XOR[1])
    x_two = finish(meta, None, r_third, 0, term(3, 2))
    home_two = send(x_two, XOR[2])
    x_mid = finish(meta, 1, r_mid, 0, term(2, 2))
    home_mid = send(x_mid, MIDDLE)
    x_own = finish(meta, None, r_own, 0, term(0, 0))
    r_fifth = after([x_partner, x_two, x_mid, x_own], r_fifth)
    x_far = finish(meta, 0, r_fifth, 0, term(3, 3))
    to_far = send(x_far, INWARD)
    to_far = after([home_partner, home_two, home_mid], to_far)
    home_far = send(finish(meta, 1, r_fifth, 0, more=to_far), ACROSS)
    count = lax.dynamic_slice_in_dim(block_rows, t, 1, 0)
    return assemble(meta, count, x_own, home_partner, home_two, home_mid, home_far)


def solution(mesh):
    in_specs = (
        P("pool", "tensor"),
        P("tensor", "pool"),
        P("pool", "tensor", None),
        P("pool", "tensor", None),
        P("pool"),
        P("pool"),
    )
    out_specs = P(("pool", "tensor"), None)
    body = line_of_four if dict(mesh.shape) == {"pool": 8, "tensor": 4} else general
    return jax.shard_map(body, mesh=mesh, in_specs=in_specs, out_specs=out_specs, check_vma=False)
```

```python
import functools

import jax
import jax.numpy as jnp
from jax import lax
from jax.experimental import pallas as pl
from jax.experimental.pallas import tpu as pltpu
from jax.sharding import PartitionSpec as P

BLOCK = 128
SCALE = 0.5


def general(hidden, down_weight, adapter_shrink, adapter_expand, block_adapter, block_rows):
    input_rows, feat = hidden.shape
    block_count = block_adapter.shape[0]
    column_span = adapter_expand.shape[1]
    tensor_pos = lax.axis_index("tensor")
    tensor_count = lax.axis_size("tensor")
    own_rows = input_rows // tensor_count
    blocks = hidden.reshape(block_count, BLOCK, feat)
    partial_value = jnp.dot(
        hidden,
        lax.all_gather(down_weight, "pool", axis=1, tiled=True),
        preferred_element_type=jnp.float32,
    )
    total = lax.psum_scatter(
        partial_value.astype(jnp.bfloat16), "tensor", scatter_dimension=0, tiled=True
    ).astype(jnp.float32)
    shrink_piece = lax.all_gather(adapter_shrink, "pool", axis=0, tiled=True)
    expand_piece = lax.all_gather(adapter_expand, "pool", axis=0, tiled=True)
    idents = jnp.arange(shrink_piece.shape[0], dtype=jnp.int32)
    pick = (block_adapter[:, None] == idents[None, :]).astype(jnp.bfloat16)
    first = jnp.einsum("bk,kfr->bfr", pick, shrink_piece, preferred_element_type=jnp.float32)
    second = jnp.einsum("bk,kcr->bcr", pick, expand_piece, preferred_element_type=jnp.float32)
    shrink = jnp.einsum(
        "bnf,bfr->bnr", blocks, first.astype(jnp.bfloat16), preferred_element_type=jnp.float32
    )
    summed_shrink = lax.psum(shrink.astype(jnp.bfloat16), "tensor")
    enlarged_rows = jnp.einsum(
        "bnr,bcr->bnc",
        summed_shrink,
        second.astype(jnp.bfloat16),
        preferred_element_type=jnp.float32,
    )
    adapter_delta_columns = (
        (SCALE * enlarged_rows).astype(jnp.bfloat16).reshape(input_rows, column_span)
    )
    delta_mine = lax.all_to_all(
        adapter_delta_columns, "tensor", split_axis=0, concat_axis=1, tiled=True
    )
    total = total + delta_mine.astype(jnp.float32)
    row_ids = tensor_pos * own_rows + jnp.arange(own_rows, dtype=jnp.int32)
    owning = (row_ids // BLOCK)[:, None] == jnp.arange(block_count, dtype=jnp.int32)[None, :]
    lengths = jnp.sum(jnp.where(owning, block_rows[None, :], 0), axis=1)
    valid = (row_ids % BLOCK < lengths).astype(jnp.float32)
    return (total * valid[:, None]).astype(jnp.bfloat16)


def dot(a, b):
    return jnp.dot(a, b, preferred_element_type=jnp.float32)


def on_line(pairs):
    return [(2 * a + c, 2 * b + c) for a, b in pairs for c in range(2)]


XOR = {s: on_line([(z, z ^ s) for z in range(4)]) for s in (1, 2, 3)}
MIDDLE = on_line([(1, 2), (2, 1)])
OUTWARD = on_line([(1, 0), (2, 3)])
INWARD = on_line([(0, 1), (3, 2)])
ACROSS = on_line([(1, 3), (2, 0)])
SIBLING = [(p, p ^ 1) for p in range(8)]

TILE = 512
NEAR = 4 * TILE
WIDE = 2048
SHARE = 512
INNER, CORE, ZPOS, NAMES = 0, 1, 2, 3
CHEAP = pl.CostEstimate(flops=1000, bytes_accessed=1000, transcendentals=0)


def send(x, pairs):
    return lax.ppermute(x, "pool", pairs)


def after(events, *xs):
    tied = lax.optimization_barrier((tuple(events), xs))
    return tied[1] if len(xs) > 1 else tied[1][0]


def params(limit):
    return pltpu.CompilerParams(vmem_limit_bytes=limit * 1024 * 1024)


class Rows:
    def __init__(self, parts, role, at):
        self.parts, self.role, self.at = parts, role, at
        self.rows = parts[0][0].shape[0]
        self.total = sum(part[2] for part in parts)


def block_sums(meta, slot, low, start, count, b):
    name = meta[NAMES + 4 * slot + b]
    chip = name >> 2
    place = ((((name >> 1) & 1) ^ meta[CORE]) << 2) + jnp.where(chip == meta[ZPOS], 0, 2) + (name & 1)
    place = jnp.where((chip == meta[ZPOS]) | (chip == (meta[ZPOS] ^ 1)), place, -1)
    value = jnp.zeros((count, 64), jnp.float32)
    for i in range(8):
        part = low[start + b * count : start + (b + 1) * count, i * 64 : i * 64 + 64]
        value = value + jnp.where(place == i, part, 0.0)
    return value.astype(jnp.bfloat16)


def accumulate(ref, rows, cols, value, k, first):
    if first:
        value = value + jnp.where(k == 0, 0.0, ref[rows, cols])
    else:
        value = value + ref[rows, cols]
    ref[rows, cols] = value


def times_transposed(x, a):
    return lax.dot_general(x, a, (((1,), (1,)), ((), ())), preferred_element_type=jnp.float32)


def products_kernel(jobs, weights, meta, *refs):
    refs = list(refs)
    xs = [[refs.pop(0) for _ in job.parts] for job in jobs]
    ws = [(refs.pop(0), refs.pop(0)) for _ in range(weights)]
    out, acc = refs
    k = pl.program_id(0)
    top = {0: 0, 1: 0}
    for x_parts, job in zip(xs, jobs):
        start = max(top.values()) if job.role is None else top[job.role]
        for role in top if job.role is None else (job.role,):
            top[role] = start + job.rows
        mine = slice(start, start + job.rows)
        role = True if job.role is None else meta[INNER] == job.role
        base = 0
        for x, (_, _, tiles, weight) in zip(x_parts, job.parts):

            def step(x=x, mine=mine, pair=ws[weight], first=base == 0):
                for h, w in enumerate(pair):
                    for n in range(0, WIDE // 2, 512):
                        at = slice(h * (WIDE // 2) + n, h * (WIDE // 2) + n + 512)
                        accumulate(acc, mine, at, dot(x[...], w[:, n : n + 512]), k, first)

            pl.when(role & (k >= base) & (k < base + tiles))(step)
            base += tiles

        def store(job=job, start=start):
            count = job.rows // 4
            for b in range(4):
                value = acc[start + b * count : start + (b + 1) * count, :]
                out[b, job.at : job.at + count, :] = value.astype(jnp.bfloat16)

        pl.when(role & (k == job.total - 1))(store)


def products(meta, jobs, weights, rows):
    steps = max(job.total for job in jobs)
    in_specs, args, uses = [], [], {}
    for job in jobs:
        base = 0
        for x, tile, tiles, weight in job.parts:

            def index(k, m, base=base, tile=tile, tiles=tiles, role=job.role):
                at = jnp.clip(k - base, 0, tiles - 1)
                if role is not None:
                    at = at * (m[INNER] if role == 1 else 1 - m[INNER])
                return (0, at + tile)

            in_specs.append(pl.BlockSpec((x.shape[0], TILE), index))
            args.append(x)
            for role in (0, 1) if job.role is None else (job.role,):
                uses[weight, role] = (base, tiles)
            base += tiles
    for i, (own, own_tile, other, other_tile) in enumerate(weights):
        for w, tile in ((own, own_tile), (other, other_tile)):

            def index(k, m, i=i, tile=tile):
                at = [jnp.clip(k - base, 0, tiles - 1) for base, tiles in (uses.get((i, r), (0, 1)) for r in (0, 1))]
                return (jnp.where(m[INNER] == 1, at[1], at[0]) + tile, 0)

            in_specs.append(pl.BlockSpec((TILE, w.shape[1]), index))
            args.append(w)
    both = sum(job.rows for job in jobs if job.role is None)
    height = both + max(sum(job.rows for job in jobs if job.role == r) for r in (0, 1))
    shape = (4, rows, WIDE)
    return pl.pallas_call(
        functools.partial(products_kernel, jobs, len(weights)),
        grid_spec=pltpu.PrefetchScalarGridSpec(
            num_scalar_prefetch=1,
            grid=(steps,),
            in_specs=in_specs,
            out_specs=pl.BlockSpec(shape, lambda k, m: (0, 0, 0)),
            scratch_shapes=[pltpu.VMEM((height, WIDE), jnp.float32)],
        ),
        out_shape=pltpu.HBM(shape, jnp.bfloat16),
        compiler_params=params(50),
        cost_estimate=CHEAP,
    )(meta, *args)


def shrink_kernel(tiles, slots, steps, meta, *refs):
    refs = list(refs)
    xs = [[refs.pop(0) for _ in part] for part in tiles]
    mine, other, held_mine, held_other, out, low = refs
    k = pl.program_id(0)
    inner = meta[INNER] == 1
    rows = BLOCK * 4
    for i, x_parts in enumerate(xs):
        base = 0
        for x, count in zip(x_parts, tiles[i]):

            @pl.when(inner & (k >= base) & (k < base + count))
            def _(i=i, x=x, first=base == 0):
                here = slice(i * rows, (i + 1) * rows)
                for h, a in enumerate((mine, other)):
                    accumulate(low, here, slice(h * 256, h * 256 + 256), times_transposed(x[...], a[...]), k, first)

            base += count

    @pl.when(inner & (k == steps - 1))
    def _():
        for i, slot in enumerate(slots):
            for b in range(4):
                at = 2 * SHARE + i * 64
                out[b, :, at : at + 64] = block_sums(meta, slot, low, i * rows, BLOCK, b)

    @pl.when(k == 0)
    def _():
        for b in range(4):
            for slot in range(4):
                name = meta[NAMES + 4 * slot + b]
                index = 2 * ((name >> 2) ^ meta[ZPOS]) + (name & 1)
                value = jnp.where(((name >> 1) & 1) == meta[CORE], held_mine[index], held_other[index])
                at = slot // 2 * SHARE
                out[b, slot % 2 * 64 : slot % 2 * 64 + 64, at : at + SHARE] = value


def shrink_sums(meta, xs, slots, mine, other, held):
    tiles = [[part.shape[1] // TILE for part in x] for x in xs]
    steps = sum(tiles[0])
    in_specs, args = [], []
    for x, counts in zip(xs, tiles):
        base = 0
        for part, count in zip(x, counts):

            def index(k, m, base=base, count=count):
                return (0, jnp.clip(k - base, 0, count - 1) * m[INNER])

            in_specs.append(pl.BlockSpec((part.shape[0], TILE), index))
            args.append(part)
            base += count
    for a in (mine, other):
        in_specs.append(pl.BlockSpec((a.shape[0], TILE), lambda k, m: (0, k * m[INNER])))
        args.append(a)
    for a in held:
        in_specs.append(pl.BlockSpec(a.shape, lambda k, m: (0, 0, 0)))
        args.append(a)
    shape = (4, BLOCK, 2 * SHARE + 256)
    return pl.pallas_call(
        functools.partial(shrink_kernel, tiles, slots, steps),
        grid_spec=pltpu.PrefetchScalarGridSpec(
            num_scalar_prefetch=1,
            grid=(steps,),
            in_specs=in_specs,
            out_specs=pl.BlockSpec(shape, lambda k, m: (0, 0, 0)),
            scratch_shapes=[pltpu.VMEM((4 * BLOCK * len(xs), 512), jnp.float32)],
        ),
        out_shape=pltpu.HBM(shape, jnp.bfloat16),
        compiler_params=params(40),
        cost_estimate=CHEAP,
    )(meta, *args)


def low_kernel(x, out, swapped):
    value = x[0].astype(jnp.float32)
    for b in range(1, 4):
        value = value + x[b].astype(jnp.float32)
    value = value.astype(jnp.bfloat16)
    out[...] = value
    swapped[...] = jnp.concatenate([value[:, i * 64 : i * 64 + 64] for i in (1, 0, 3, 2)], axis=1)


def low_sums(x):
    shape = jax.ShapeDtypeStruct((BLOCK, 256), jnp.bfloat16)
    whole = pl.BlockSpec((BLOCK, 256), lambda i: (0, 0))
    return pl.pallas_call(
        low_kernel,
        grid=(1,),
        in_specs=[pl.BlockSpec((4, BLOCK, 256), lambda i: (0, 0, 2 * SHARE // 256))],
        out_specs=(whole, whole),
        out_shape=(shape, shape),
        cost_estimate=CHEAP,
    )(x)


def add_kernel(x, y, out):
    out[...] = (x[...].astype(jnp.float32) + y[...].astype(jnp.float32)).astype(jnp.bfloat16)


def add(x, y):
    return pl.pallas_call(add_kernel, out_shape=jax.ShapeDtypeStruct(x.shape, x.dtype), cost_estimate=CHEAP)(x, y)


def finish_kernel(role, row, rows, lanes, has_more, meta, *refs):
    refs = list(refs)
    part = refs.pop(0)
    if lanes:
        low_in, low_out, expand = refs.pop(0), refs.pop(0), refs.pop(0)
    more = refs.pop(0) if has_more else None
    out = refs.pop(0)

    def run():
        total = part[0, row : row + rows, :].astype(jnp.float32)
        for b in range(1, 4):
            total = total + part[b, row : row + rows, :].astype(jnp.float32)
        if lanes:
            x = low_in[:rows, lanes[0] : lanes[0] + 64]
            y = low_out[:rows, lanes[1] : lanes[1] + 64]
            x = jnp.where(meta[INNER] == 1, x, y)
            delta = [dot(x, expand[i]) for i in range(expand.shape[0])]
            total = total + SCALE * jnp.concatenate(delta, axis=1)
        if has_more:
            total = total + more[...].astype(jnp.float32)
        out[...] = total.astype(jnp.bfloat16)

    if role is None:
        run()
    else:
        pl.when(meta[INNER] == role)(run)


def finish(meta, role, part, row, low=None, more=None, rows=BLOCK):
    span = WIDE // 2
    in_specs = [pl.BlockSpec((4, part.shape[1], span), lambda h, m: (0, 0, h))]
    args = [part]
    lanes = None
    if low is not None:
        *sums, expand, slots = low
        for x in sums:
            in_specs.append(pl.BlockSpec(x.shape, lambda h, m: (0, 0)))
            args.append(x)

        def index(h, m):
            slot = slots[1] + (slots[0] - slots[1]) * m[INNER]
            return (h ^ m[CORE], slot & 1, slot >> 1)

        in_specs.append(pl.BlockSpec((span // SHARE, 64, SHARE), index))
        args.append(expand)
        lanes = [64 * (0, 2, 1, 3)[slots[0]], 64 * (2, 0, 1, 3)[slots[1]]]
    if more is not None:
        in_specs.append(pl.BlockSpec((rows, span), lambda h, m: (0, h)))
        args.append(more)
    return pl.pallas_call(
        functools.partial(finish_kernel, role, row, rows, lanes, more is not None),
        grid_spec=pltpu.PrefetchScalarGridSpec(
            num_scalar_prefetch=1,
            grid=(2,),
            in_specs=in_specs,
            out_specs=pl.BlockSpec((rows, span), lambda h, m: (0, h)),
        ),
        out_shape=jax.ShapeDtypeStruct((rows, WIDE), jnp.bfloat16),
        compiler_params=params(32),
        cost_estimate=CHEAP,
    )(meta, *args)


def assemble_kernel(span, meta, count, own, one, two, inner_three, outer_three, out):
    z, c, inner = meta[ZPOS], meta[CORE], meta[INNER] == 1
    rows = own.shape[0]
    valid = lax.broadcasted_iota(jnp.int32, (rows, 1), 0) < count[0]

    def put(j, source):
        for h in range(2):
            at = pl.ds(pl.multiple_of((2 * j + h) * span, span), span)
            part = pl.ds(pl.multiple_of((h ^ c) * span, span), span)
            out[:, at] = jnp.where(valid, source[:, part], jnp.zeros((), jnp.bfloat16))

    put(z, own)
    put(z ^ 1, one)
    put(z ^ 2, two)

    @pl.when(inner)
    def _():
        put(z ^ 3, inner_three)

    @pl.when(jnp.logical_not(inner))
    def _():
        put(z ^ 3, outer_three)


def assemble(meta, count, *args):
    rows, wide = args[0].shape
    return pl.pallas_call(
        functools.partial(assemble_kernel, wide // 2),
        grid_spec=pltpu.PrefetchScalarGridSpec(
            num_scalar_prefetch=2,
            grid=(1,),
            in_specs=[pl.BlockSpec(a.shape, lambda n, m, k: (0, 0)) for a in args],
            out_specs=pl.BlockSpec((rows, 4 * wide), lambda n, m, k: (0, 0)),
        ),
        out_shape=jax.ShapeDtypeStruct((rows, 4 * wide), jnp.bfloat16),
        compiler_params=params(32),
        cost_estimate=CHEAP,
    )(meta, count, *args)


def line_of_four(hidden, down_weight, adapter_shrink, adapter_expand, block_adapter, block_rows):
    rows, feat = hidden.shape
    adp, _, rank = adapter_shrink.shape
    p = lax.axis_index("pool")
    t = lax.axis_index("tensor")
    tensors = lax.axis_size("tensor")
    z, c = p // 2, p % 2
    outer = (z == 0) | (z == 3)

    def exchange(x):
        return lax.all_to_all(x, "tensor", split_axis=0, concat_axis=0, tiled=True)

    place = jnp.stack([jnp.where(outer, 0, 1), c, z]).astype(jnp.int32)

    mid = send(hidden, MIDDLE)
    partner = send(hidden, XOR[1])
    cuts = [(lo, min(lo + 2 * TILE, feat)) for lo in range(0, feat, 2 * TILE)]
    pieces = [down_weight[lo:hi] for lo, hi in cuts]
    others = [send(w, SIBLING) for w in pieces]
    weights = [(down_weight, lo // TILE, w, 0) for (lo, _), w in zip(cuts, others)]

    def whole(x):
        return [(x, lo // TILE, (hi - lo) // TILE, i) for i, (lo, hi) in enumerate(cuts)]

    shares = exchange(
        adapter_expand.transpose(0, 2, 1).reshape(adp, rank, tensors, SHARE).transpose(2, 0, 1, 3)
    ).reshape(tensors, adp * rank, SHARE)
    label = jnp.zeros((16, SHARE), jnp.bfloat16).at[0, : block_adapter.shape[0]].set(block_adapter.astype(jnp.bfloat16))
    j_own = products(place, [Rows(whole(hidden), None, 0)], weights, BLOCK)
    shares = after([j_own], shares)

    def shares_of(s):
        return lax.dynamic_index_in_dim(shares, z ^ s, 0, keepdims=False)

    told = [send(jnp.concatenate([shares_of(s), label], axis=0), XOR[s]) for s in (1, 2, 3)]

    ready = [partner, mid, *told]
    far = send(after(ready, partner), MIDDLE)
    out_mid = send(after(ready, mid), OUTWARD)
    shrink_w = adapter_shrink.transpose(0, 2, 1).reshape(adp * rank, feat)
    shrink_o = send(after(ready, shrink_w), INWARD)
    v_own = [send(after([shrink_o], w), INWARD) for w in pieces[NEAR // (2 * TILE) :]]
    r_own = exchange(j_own)
    j_partner = products(place, [Rows(whole(partner), None, 0)], weights, BLOCK)
    r_partner = exchange(j_partner)
    j_mid = products(place, [Rows(whole(after([j_partner], mid)), 1, 0)], weights, BLOCK)
    r_mid = exchange(j_mid)
    far_near = far[:, :NEAR]
    out_far = send(after([out_mid, shrink_o, j_partner, j_mid], far_near), OUTWARD)
    j_third = products(
        place,
        [Rows(whole(after([r_partner, far_near], far)), 1, 0), Rows(whole(out_mid), 0, 0)],
        weights,
        BLOCK,
    )
    r_third = exchange(j_third)
    v_other = [send(after([out_far, j_third], v_own[0]), SIBLING)]
    v_other.append(send(after(v_other, v_own[1]), SIBLING))

    held = jnp.concatenate([shares_of(0)] + [x[: adp * rank] for x in told]).reshape(4 * adp, rank, SHARE)
    held = (held, send(held, SIBLING))
    names = [block_adapter] + [x[adp * rank, : block_adapter.shape[0]].astype(jnp.int32) for x in told]
    name_m = jnp.where(outer, names[2], names[3])
    name_f = jnp.where(outer, names[3], names[2])
    meta = jnp.concatenate([place, names[0], names[1], name_m, name_f])
    shrink_mine = jnp.concatenate([shrink_w, after([j_partner], shrink_o)], axis=0)
    shrink_other = send(shrink_mine, SIBLING)
    sums = shrink_sums(meta, [[after([j_third, v_own[1]], hidden)], [mid], [partner], [far]], [0, 2, 1, 3], shrink_mine, shrink_other, held)
    r_sums = exchange(sums)
    low, swapped = low_sums(r_sums)
    low = add(low, send(swapped, MIDDLE))
    low_out = send(low, OUTWARD)

    rest = [(a, 0, b, 0) for a, b in zip(v_own, v_other)] + weights[: NEAR // (2 * TILE)]
    j_fifth = products(
        place,
        [
            Rows([(after([sums], far), NEAR // TILE, 2, 0), (far, NEAR // TILE + 2, 1, 1)], 1, 0),
            Rows([(out_far, 0, 2, 2), (out_far, 2, 2, 3)], 0, 0),
        ],
        rest,
        BLOCK,
    )
    r_fifth = exchange(j_fifth)

    def term(inner_slot, outer_slot):
        return (low, low_out, r_sums, (inner_slot, outer_slot))

    x_partner = finish(meta, None, r_partner, 0, term(1, 1))
    home_partner = send(x_partner, XOR[1])
    x_two = finish(meta, None, r_third, 0, term(3, 2))
    home_two = send(x_two, XOR[2])
    x_mid = finish(meta, 1, r_mid, 0, term(2, 2))
    home_mid = send(x_mid, MIDDLE)
    x_own = finish(meta, None, r_own, 0, term(0, 0))
    r_fifth = after([x_partner, x_two, x_mid, x_own], r_fifth)
    x_far = finish(meta, 0, r_fifth, 0, term(3, 3))
    to_far = send(x_far, INWARD)
    to_far = after([home_partner, home_two, home_mid], to_far)
    home_far = send(finish(meta, 1, r_fifth, 0, more=to_far), ACROSS)
    count = lax.dynamic_slice_in_dim(block_rows, t, 1, 0)
    return assemble(meta, count, x_own, home_partner, home_two, home_mid, home_far)


def solution(mesh):
    in_specs = (
        P("pool", "tensor"),
        P("tensor", "pool"),
        P("pool", "tensor", None),
        P("pool", "tensor", None),
        P("pool"),
        P("pool"),
    )
    out_specs = P(("pool", "tensor"), None)
    body = line_of_four if dict(mesh.shape) == {"pool": 8, "tensor": 4} else general
    return jax.shard_map(body, mesh=mesh, in_specs=in_specs, out_specs=out_specs, check_vma=False)
```

```python
import functools

import jax
import jax.numpy as jnp
from jax import lax
from jax.experimental import pallas as pl
from jax.experimental.pallas import tpu as pltpu
from jax.sharding import PartitionSpec as P

BLOCK = 128
SCALE = 0.5


def general(hidden, down_weight, adapter_shrink, adapter_expand, block_adapter, block_rows):
    input_rows, feat = hidden.shape
    block_count = block_adapter.shape[0]
    column_span = adapter_expand.shape[1]
    tensor_pos = lax.axis_index("tensor")
    tensor_count = lax.axis_size("tensor")
    own_rows = input_rows // tensor_count
    blocks = hidden.reshape(block_count, BLOCK, feat)
    partial_value = jnp.dot(
        hidden,
        lax.all_gather(down_weight, "pool", axis=1, tiled=True),
        preferred_element_type=jnp.float32,
    )
    total = lax.psum_scatter(
        partial_value.astype(jnp.bfloat16), "tensor", scatter_dimension=0, tiled=True
    ).astype(jnp.float32)
    shrink_piece = lax.all_gather(adapter_shrink, "pool", axis=0, tiled=True)
    expand_piece = lax.all_gather(adapter_expand, "pool", axis=0, tiled=True)
    idents = jnp.arange(shrink_piece.shape[0], dtype=jnp.int32)
    pick = (block_adapter[:, None] == idents[None, :]).astype(jnp.bfloat16)
    first = jnp.einsum("bk,kfr->bfr", pick, shrink_piece, preferred_element_type=jnp.float32)
    second = jnp.einsum("bk,kcr->bcr", pick, expand_piece, preferred_element_type=jnp.float32)
    shrink = jnp.einsum(
        "bnf,bfr->bnr", blocks, first.astype(jnp.bfloat16), preferred_element_type=jnp.float32
    )
    summed_shrink = lax.psum(shrink.astype(jnp.bfloat16), "tensor")
    enlarged_rows = jnp.einsum(
        "bnr,bcr->bnc",
        summed_shrink,
        second.astype(jnp.bfloat16),
        preferred_element_type=jnp.float32,
    )
    adapter_delta_columns = (
        (SCALE * enlarged_rows).astype(jnp.bfloat16).reshape(input_rows, column_span)
    )
    delta_mine = lax.all_to_all(
        adapter_delta_columns, "tensor", split_axis=0, concat_axis=1, tiled=True
    )
    total = total + delta_mine.astype(jnp.float32)
    row_ids = tensor_pos * own_rows + jnp.arange(own_rows, dtype=jnp.int32)
    owning = (row_ids // BLOCK)[:, None] == jnp.arange(block_count, dtype=jnp.int32)[None, :]
    lengths = jnp.sum(jnp.where(owning, block_rows[None, :], 0), axis=1)
    valid = (row_ids % BLOCK < lengths).astype(jnp.float32)
    return (total * valid[:, None]).astype(jnp.bfloat16)


def dot(a, b):
    return jnp.dot(a, b, preferred_element_type=jnp.float32)


def on_line(pairs):
    return [(2 * a + c, 2 * b + c) for a, b in pairs for c in range(2)]


XOR = {s: on_line([(z, z ^ s) for z in range(4)]) for s in (1, 2, 3)}
MIDDLE = on_line([(1, 2), (2, 1)])
OUTWARD = on_line([(1, 0), (2, 3)])
INWARD = on_line([(0, 1), (3, 2)])
ACROSS = on_line([(1, 3), (2, 0)])
SIBLING = [(p, p ^ 1) for p in range(8)]

TILE = 512
NEAR = 4 * TILE
WIDE = 2048
SHARE = 512
INNER, CORE, ZPOS, NAMES = 0, 1, 2, 3
CHEAP = pl.CostEstimate(flops=1000, bytes_accessed=1000, transcendentals=0)


def send(x, pairs):
    return lax.ppermute(x, "pool", pairs)


def after(events, *xs):
    tied = lax.optimization_barrier((tuple(events), xs))
    return tied[1] if len(xs) > 1 else tied[1][0]


def params(limit):
    return pltpu.CompilerParams(vmem_limit_bytes=limit * 1024 * 1024)


class Rows:
    def __init__(self, parts, role, at):
        self.parts, self.role, self.at = parts, role, at
        self.rows = parts[0][0].shape[0]
        self.total = sum(part[2] for part in parts)


def block_sums(meta, slot, low, start, count, b):
    name = meta[NAMES + 4 * slot + b]
    chip = name >> 2
    place = ((((name >> 1) & 1) ^ meta[CORE]) << 2) + jnp.where(chip == meta[ZPOS], 0, 2) + (name & 1)
    place = jnp.where((chip == meta[ZPOS]) | (chip == (meta[ZPOS] ^ 1)), place, -1)
    value = jnp.zeros((count, 64), jnp.float32)
    for i in range(8):
        part = low[start + b * count : start + (b + 1) * count, i * 64 : i * 64 + 64]
        value = value + jnp.where(place == i, part, 0.0)
    return value.astype(jnp.bfloat16)


def accumulate(ref, rows, cols, value, k, first):
    if first:
        value = value + jnp.where(k == 0, 0.0, ref[rows, cols])
    else:
        value = value + ref[rows, cols]
    ref[rows, cols] = value


def times_transposed(x, a):
    return lax.dot_general(x, a, (((1,), (1,)), ((), ())), preferred_element_type=jnp.float32)


def products_kernel(jobs, weights, meta, *refs):
    refs = list(refs)
    xs = [[refs.pop(0) for _ in job.parts] for job in jobs]
    ws = [(refs.pop(0), refs.pop(0)) for _ in range(weights)]
    out, acc = refs
    k = pl.program_id(0)
    top = {0: 0, 1: 0}
    for x_parts, job in zip(xs, jobs):
        start = max(top.values()) if job.role is None else top[job.role]
        for role in top if job.role is None else (job.role,):
            top[role] = start + job.rows
        mine = slice(start, start + job.rows)
        role = True if job.role is None else meta[INNER] == job.role
        base = 0
        for x, (_, _, tiles, weight) in zip(x_parts, job.parts):

            def step(x=x, mine=mine, pair=ws[weight], first=base == 0):
                for h, w in enumerate(pair):
                    for n in range(0, WIDE // 2, 512):
                        at = slice(h * (WIDE // 2) + n, h * (WIDE // 2) + n + 512)
                        accumulate(acc, mine, at, dot(x[...], w[:, n : n + 512]), k, first)

            pl.when(role & (k >= base) & (k < base + tiles))(step)
            base += tiles

        def store(job=job, start=start):
            count = job.rows // 4
            for b in range(4):
                value = acc[start + b * count : start + (b + 1) * count, :]
                out[b, job.at : job.at + count, :] = value.astype(jnp.bfloat16)

        pl.when(role & (k == job.total - 1))(store)


def products(meta, jobs, weights, rows):
    steps = max(job.total for job in jobs)
    in_specs, args, uses = [], [], {}
    for job in jobs:
        base = 0
        for x, tile, tiles, weight in job.parts:

            def index(k, m, base=base, tile=tile, tiles=tiles, role=job.role):
                at = jnp.clip(k - base, 0, tiles - 1)
                if role is not None:
                    at = at * (m[INNER] if role == 1 else 1 - m[INNER])
                return (0, at + tile)

            in_specs.append(pl.BlockSpec((x.shape[0], TILE), index))
            args.append(x)
            for role in (0, 1) if job.role is None else (job.role,):
                uses[weight, role] = (base, tiles)
            base += tiles
    for i, (own, own_tile, other, other_tile) in enumerate(weights):
        for w, tile in ((own, own_tile), (other, other_tile)):

            def index(k, m, i=i, tile=tile):
                at = [jnp.clip(k - base, 0, tiles - 1) for base, tiles in (uses.get((i, r), (0, 1)) for r in (0, 1))]
                return (jnp.where(m[INNER] == 1, at[1], at[0]) + tile, 0)

            in_specs.append(pl.BlockSpec((TILE, w.shape[1]), index))
            args.append(w)
    both = sum(job.rows for job in jobs if job.role is None)
    height = both + max(sum(job.rows for job in jobs if job.role == r) for r in (0, 1))
    shape = (4, rows, WIDE)
    return pl.pallas_call(
        functools.partial(products_kernel, jobs, len(weights)),
        grid_spec=pltpu.PrefetchScalarGridSpec(
            num_scalar_prefetch=1,
            grid=(steps,),
            in_specs=in_specs,
            out_specs=pl.BlockSpec(shape, lambda k, m: (0, 0, 0)),
            scratch_shapes=[pltpu.VMEM((height, WIDE), jnp.float32)],
        ),
        out_shape=pltpu.HBM(shape, jnp.bfloat16),
        compiler_params=params(50),
        cost_estimate=CHEAP,
    )(meta, *args)


def shrink_kernel(tiles, slots, steps, meta, *refs):
    refs = list(refs)
    xs = [[refs.pop(0) for _ in part] for part in tiles]
    mine, other, held_mine, held_other, out, low = refs
    k = pl.program_id(0)
    inner = meta[INNER] == 1
    rows = BLOCK * 4
    for i, x_parts in enumerate(xs):
        base = 0
        for x, count in zip(x_parts, tiles[i]):

            @pl.when(inner & (k >= base) & (k < base + count))
            def _(i=i, x=x, first=base == 0):
                here = slice(i * rows, (i + 1) * rows)
                for h, a in enumerate((mine, other)):
                    accumulate(low, here, slice(h * 256, h * 256 + 256), times_transposed(x[...], a[...]), k, first)

            base += count

    @pl.when(inner & (k == steps - 1))
    def _():
        for i, slot in enumerate(slots):
            for b in range(4):
                at = 2 * SHARE + i * 64
                out[b, :, at : at + 64] = block_sums(meta, slot, low, i * rows, BLOCK, b)

    @pl.when(k == 0)
    def _():
        for b in range(4):
            for slot in range(4):
                name = meta[NAMES + 4 * slot + b]
                index = 2 * ((name >> 2) ^ meta[ZPOS]) + (name & 1)
                value = jnp.where(((name >> 1) & 1) == meta[CORE], held_mine[index], held_other[index])
                at = slot // 2 * SHARE
                out[b, slot % 2 * 64 : slot % 2 * 64 + 64, at : at + SHARE] = value


def shrink_sums(meta, xs, slots, mine, other, held):
    tiles = [[part.shape[1] // TILE for part in x] for x in xs]
    steps = sum(tiles[0])
    in_specs, args = [], []
    for x, counts in zip(xs, tiles):
        base = 0
        for part, count in zip(x, counts):

            def index(k, m, base=base, count=count):
                return (0, jnp.clip(k - base, 0, count - 1) * m[INNER])

            in_specs.append(pl.BlockSpec((part.shape[0], TILE), index))
            args.append(part)
            base += count
    for a in (mine, other):
        in_specs.append(pl.BlockSpec((a.shape[0], TILE), lambda k, m: (0, k * m[INNER])))
        args.append(a)
    for a in held:
        in_specs.append(pl.BlockSpec(a.shape, lambda k, m: (0, 0, 0)))
        args.append(a)
    shape = (4, BLOCK, 2 * SHARE + 256)
    return pl.pallas_call(
        functools.partial(shrink_kernel, tiles, slots, steps),
        grid_spec=pltpu.PrefetchScalarGridSpec(
            num_scalar_prefetch=1,
            grid=(steps,),
            in_specs=in_specs,
            out_specs=pl.BlockSpec(shape, lambda k, m: (0, 0, 0)),
            scratch_shapes=[pltpu.VMEM((4 * BLOCK * len(xs), 512), jnp.float32)],
        ),
        out_shape=pltpu.HBM(shape, jnp.bfloat16),
        compiler_params=params(40),
        cost_estimate=CHEAP,
    )(meta, *args)


def low_kernel(x, out, swapped):
    value = x[0].astype(jnp.float32)
    for b in range(1, 4):
        value = value + x[b].astype(jnp.float32)
    value = value.astype(jnp.bfloat16)
    out[...] = value
    swapped[...] = jnp.concatenate([value[:, i * 64 : i * 64 + 64] for i in (1, 0, 3, 2)], axis=1)


def low_sums(x):
    shape = jax.ShapeDtypeStruct((BLOCK, 256), jnp.bfloat16)
    whole = pl.BlockSpec((BLOCK, 256), lambda i: (0, 0))
    return pl.pallas_call(
        low_kernel,
        grid=(1,),
        in_specs=[pl.BlockSpec((4, BLOCK, 256), lambda i: (0, 0, 2 * SHARE // 256))],
        out_specs=(whole, whole),
        out_shape=(shape, shape),
        cost_estimate=CHEAP,
    )(x)


def add_kernel(x, y, out):
    out[...] = (x[...].astype(jnp.float32) + y[...].astype(jnp.float32)).astype(jnp.bfloat16)


def add(x, y):
    return pl.pallas_call(add_kernel, out_shape=jax.ShapeDtypeStruct(x.shape, x.dtype), cost_estimate=CHEAP)(x, y)


def finish_kernel(role, row, rows, lanes, has_more, meta, *refs):
    refs = list(refs)
    part = refs.pop(0)
    if lanes:
        low_in, low_out, expand = refs.pop(0), refs.pop(0), refs.pop(0)
    more = refs.pop(0) if has_more else None
    out = refs.pop(0)

    def run():
        total = part[0, row : row + rows, :].astype(jnp.float32)
        for b in range(1, 4):
            total = total + part[b, row : row + rows, :].astype(jnp.float32)
        if lanes:
            x = low_in[:rows, lanes[0] : lanes[0] + 64]
            y = low_out[:rows, lanes[1] : lanes[1] + 64]
            x = jnp.where(meta[INNER] == 1, x, y)
            delta = [dot(x, expand[i]) for i in range(expand.shape[0])]
            total = total + SCALE * jnp.concatenate(delta, axis=1)
        if has_more:
            total = total + more[...].astype(jnp.float32)
        out[...] = total.astype(jnp.bfloat16)

    if role is None:
        run()
    else:
        pl.when(meta[INNER] == role)(run)


def finish(meta, role, part, row, low=None, more=None, rows=BLOCK):
    span = WIDE // 2
    in_specs = [pl.BlockSpec((4, part.shape[1], span), lambda h, m: (0, 0, h))]
    args = [part]
    lanes = None
    if low is not None:
        *sums, expand, slots = low
        for x in sums:
            in_specs.append(pl.BlockSpec(x.shape, lambda h, m: (0, 0)))
            args.append(x)

        def index(h, m):
            slot = slots[1] + (slots[0] - slots[1]) * m[INNER]
            return (h ^ m[CORE], slot & 1, slot >> 1)

        in_specs.append(pl.BlockSpec((span // SHARE, 64, SHARE), index))
        args.append(expand)
        lanes = [64 * (0, 2, 1, 3)[slots[0]], 64 * (2, 0, 1, 3)[slots[1]]]
    if more is not None:
        in_specs.append(pl.BlockSpec((rows, span), lambda h, m: (0, h)))
        args.append(more)
    return pl.pallas_call(
        functools.partial(finish_kernel, role, row, rows, lanes, more is not None),
        grid_spec=pltpu.PrefetchScalarGridSpec(
            num_scalar_prefetch=1,
            grid=(2,),
            in_specs=in_specs,
            out_specs=pl.BlockSpec((rows, span), lambda h, m: (0, h)),
        ),
        out_shape=jax.ShapeDtypeStruct((rows, WIDE), jnp.bfloat16),
        compiler_params=params(32),
        cost_estimate=CHEAP,
    )(meta, *args)


def assemble_kernel(span, meta, count, own, one, two, inner_three, outer_three, out):
    z, c, inner = meta[ZPOS], meta[CORE], meta[INNER] == 1
    rows = own.shape[0]
    valid = lax.broadcasted_iota(jnp.int32, (rows, 1), 0) < count[0]

    def put(j, source):
        for h in range(2):
            at = pl.ds(pl.multiple_of((2 * j + h) * span, span), span)
            part = pl.ds(pl.multiple_of((h ^ c) * span, span), span)
            out[:, at] = jnp.where(valid, source[:, part], jnp.zeros((), jnp.bfloat16))

    put(z, own)
    put(z ^ 1, one)
    put(z ^ 2, two)

    @pl.when(inner)
    def _():
        put(z ^ 3, inner_three)

    @pl.when(jnp.logical_not(inner))
    def _():
        put(z ^ 3, outer_three)


def assemble(meta, count, *args):
    rows, wide = args[0].shape
    return pl.pallas_call(
        functools.partial(assemble_kernel, wide // 2),
        grid_spec=pltpu.PrefetchScalarGridSpec(
            num_scalar_prefetch=2,
            grid=(1,),
            in_specs=[pl.BlockSpec(a.shape, lambda n, m, k: (0, 0)) for a in args],
            out_specs=pl.BlockSpec((rows, 4 * wide), lambda n, m, k: (0, 0)),
        ),
        out_shape=jax.ShapeDtypeStruct((rows, 4 * wide), jnp.bfloat16),
        compiler_params=params(32),
        cost_estimate=CHEAP,
    )(meta, count, *args)


def line_of_four(hidden, down_weight, adapter_shrink, adapter_expand, block_adapter, block_rows):
    rows, feat = hidden.shape
    adp, _, rank = adapter_shrink.shape
    p = lax.axis_index("pool")
    t = lax.axis_index("tensor")
    tensors = lax.axis_size("tensor")
    z, c = p // 2, p % 2
    outer = (z == 0) | (z == 3)

    def exchange(x):
        return lax.all_to_all(x, "tensor", split_axis=0, concat_axis=0, tiled=True)

    place = jnp.stack([jnp.where(outer, 0, 1), c, z]).astype(jnp.int32)

    mid = send(hidden, MIDDLE)
    partner = send(hidden, XOR[1])
    cuts = [(lo, min(lo + 2 * TILE, feat)) for lo in range(0, feat, 2 * TILE)]
    pieces = [down_weight[lo:hi] for lo, hi in cuts]
    others = [send(w, SIBLING) for w in pieces]
    weights = [(down_weight, lo // TILE, w, 0) for (lo, _), w in zip(cuts, others)]

    def whole(x):
        return [(x, lo // TILE, (hi - lo) // TILE, i) for i, (lo, hi) in enumerate(cuts)]

    shares = exchange(
        adapter_expand.transpose(0, 2, 1).reshape(adp, rank, tensors, SHARE).transpose(2, 0, 1, 3)
    ).reshape(tensors, adp * rank, SHARE)
    label = jnp.zeros((16, SHARE), jnp.bfloat16).at[0, : block_adapter.shape[0]].set(block_adapter.astype(jnp.bfloat16))
    j_own = products(place, [Rows(whole(hidden), None, 0)], weights, BLOCK)
    shares = after([j_own], shares)

    def shares_of(s):
        return lax.dynamic_index_in_dim(shares, z ^ s, 0, keepdims=False)

    told = [send(jnp.concatenate([shares_of(s), label], axis=0), XOR[s]) for s in (1, 2, 3)]

    ready = [partner, mid, *told]
    far = send(after(ready, partner), MIDDLE)
    out_mid = send(after(ready, mid), OUTWARD)
    shrink_w = adapter_shrink.transpose(0, 2, 1).reshape(adp * rank, feat)
    shrink_o = send(after(ready, shrink_w), INWARD)
    v_own = [send(after([shrink_o], w), INWARD) for w in pieces[NEAR // (2 * TILE) :]]
    j_partner = products(place, [Rows(whole(partner), None, 0)], weights, BLOCK)
    r_partner = exchange(j_partner)
    held = jnp.concatenate([shares_of(0)] + [x[: adp * rank] for x in told]).reshape(4 * adp, rank, SHARE)
    held = (held, send(held, SIBLING))
    j_mid = products(place, [Rows(whole(after([j_partner, held[1]], mid)), 1, 0)], weights, BLOCK)
    r_mid = exchange(j_mid)
    shrink_mine = jnp.concatenate([shrink_w, after([j_partner], shrink_o)], axis=0)
    shrink_other = send(shrink_mine, SIBLING)

    far_near = far[:, :NEAR]
    out_far = send(after([out_mid, shrink_o, j_partner, j_mid], far_near), OUTWARD)
    j_third = products(
        place,
        [Rows(whole(after([r_partner, far_near, shrink_other], far)), 1, 0), Rows(whole(out_mid), 0, 0)],
        weights,
        BLOCK,
    )
    r_third = exchange(j_third)
    v_other = [send(after([out_far, j_third], w), SIBLING) for w in v_own]

    names = [block_adapter] + [x[adp * rank, : block_adapter.shape[0]].astype(jnp.int32) for x in told]
    name_m = jnp.where(outer, names[2], names[3])
    name_f = jnp.where(outer, names[3], names[2])
    meta = jnp.concatenate([place, names[0], names[1], name_m, name_f])
    sums = shrink_sums(meta, [[after([j_third, v_own[1]], hidden)], [mid], [partner], [far]], [0, 2, 1, 3], shrink_mine, shrink_other, held)
    r_sums = exchange(sums)
    low, swapped = low_sums(r_sums)
    low = add(low, send(swapped, MIDDLE))
    low_out = send(low, OUTWARD)

    rest = [(a, 0, b, 0) for a, b in zip(v_own, v_other)] + weights[: NEAR // (2 * TILE)]
    j_fifth = products(
        place,
        [
            Rows([(after([sums], far), NEAR // TILE, 2, 0), (far, NEAR // TILE + 2, 1, 1)], 1, 0),
            Rows([(out_far, 0, 2, 2), (out_far, 2, 2, 3)], 0, 0),
        ],
        rest,
        BLOCK,
    )
    r_fifth = exchange(j_fifth)

    def term(inner_slot, outer_slot):
        return (low, low_out, r_sums, (inner_slot, outer_slot))

    x_partner = finish(meta, None, r_partner, 0, term(1, 1))
    home_partner = send(x_partner, XOR[1])
    x_two = finish(meta, None, r_third, 0, term(3, 2))
    home_two = send(x_two, XOR[2])
    x_mid = finish(meta, 1, r_mid, 0, term(2, 2))
    home_mid = send(x_mid, MIDDLE)
    r_fifth = after([x_partner, x_two, x_mid], r_fifth)
    x_far = finish(meta, 0, r_fifth, 0, term(3, 3))
    to_far = send(x_far, INWARD)
    x_own = finish(meta, None, exchange(after([x_far], j_own)), 0, term(0, 0))
    to_far = after([home_partner, home_two, home_mid], to_far)
    home_far = send(finish(meta, 1, r_fifth, 0, more=to_far), ACROSS)
    count = lax.dynamic_slice_in_dim(block_rows, t, 1, 0)
    return assemble(meta, count, x_own, home_partner, home_two, home_mid, home_far)


def solution(mesh):
    in_specs = (
        P("pool", "tensor"),
        P("tensor", "pool"),
        P("pool", "tensor", None),
        P("pool", "tensor", None),
        P("pool"),
        P("pool"),
    )
    out_specs = P(("pool", "tensor"), None)
    body = line_of_four if dict(mesh.shape) == {"pool": 8, "tensor": 4} else general
    return jax.shard_map(body, mesh=mesh, in_specs=in_specs, out_specs=out_specs, check_vma=False)
```

```python
import functools

import jax
import jax.numpy as jnp
from jax import lax
from jax.experimental import pallas as pl
from jax.experimental.pallas import tpu as pltpu
from jax.sharding import PartitionSpec as P

BLOCK = 128
SCALE = 0.5


def general(hidden, down_weight, adapter_shrink, adapter_expand, block_adapter, block_rows):
    input_rows, feat = hidden.shape
    block_count = block_adapter.shape[0]
    column_span = adapter_expand.shape[1]
    tensor_pos = lax.axis_index("tensor")
    tensor_count = lax.axis_size("tensor")
    own_rows = input_rows // tensor_count
    blocks = hidden.reshape(block_count, BLOCK, feat)
    partial_value = jnp.dot(
        hidden,
        lax.all_gather(down_weight, "pool", axis=1, tiled=True),
        preferred_element_type=jnp.float32,
    )
    total = lax.psum_scatter(
        partial_value.astype(jnp.bfloat16), "tensor", scatter_dimension=0, tiled=True
    ).astype(jnp.float32)
    shrink_piece = lax.all_gather(adapter_shrink, "pool", axis=0, tiled=True)
    expand_piece = lax.all_gather(adapter_expand, "pool", axis=0, tiled=True)
    idents = jnp.arange(shrink_piece.shape[0], dtype=jnp.int32)
    pick = (block_adapter[:, None] == idents[None, :]).astype(jnp.bfloat16)
    first = jnp.einsum("bk,kfr->bfr", pick, shrink_piece, preferred_element_type=jnp.float32)
    second = jnp.einsum("bk,kcr->bcr", pick, expand_piece, preferred_element_type=jnp.float32)
    shrink = jnp.einsum(
        "bnf,bfr->bnr", blocks, first.astype(jnp.bfloat16), preferred_element_type=jnp.float32
    )
    summed_shrink = lax.psum(shrink.astype(jnp.bfloat16), "tensor")
    enlarged_rows = jnp.einsum(
        "bnr,bcr->bnc",
        summed_shrink,
        second.astype(jnp.bfloat16),
        preferred_element_type=jnp.float32,
    )
    adapter_delta_columns = (
        (SCALE * enlarged_rows).astype(jnp.bfloat16).reshape(input_rows, column_span)
    )
    delta_mine = lax.all_to_all(
        adapter_delta_columns, "tensor", split_axis=0, concat_axis=1, tiled=True
    )
    total = total + delta_mine.astype(jnp.float32)
    row_ids = tensor_pos * own_rows + jnp.arange(own_rows, dtype=jnp.int32)
    owning = (row_ids // BLOCK)[:, None] == jnp.arange(block_count, dtype=jnp.int32)[None, :]
    lengths = jnp.sum(jnp.where(owning, block_rows[None, :], 0), axis=1)
    valid = (row_ids % BLOCK < lengths).astype(jnp.float32)
    return (total * valid[:, None]).astype(jnp.bfloat16)


def dot(a, b):
    return jnp.dot(a, b, preferred_element_type=jnp.float32)


def on_line(pairs):
    return [(2 * a + c, 2 * b + c) for a, b in pairs for c in range(2)]


XOR = {s: on_line([(z, z ^ s) for z in range(4)]) for s in (1, 2, 3)}
MIDDLE = on_line([(1, 2), (2, 1)])
OUTWARD = on_line([(1, 0), (2, 3)])
INWARD = on_line([(0, 1), (3, 2)])
ACROSS = on_line([(1, 3), (2, 0)])
SIBLING = [(p, p ^ 1) for p in range(8)]

TILE = 512
NEAR = 5 * TILE
WIDE = 2048
SHARE = 512
INNER, CORE, ZPOS, NAMES = 0, 1, 2, 3
CHEAP = pl.CostEstimate(flops=1000, bytes_accessed=1000, transcendentals=0)


def send(x, pairs):
    return lax.ppermute(x, "pool", pairs)


def after(events, *xs):
    tied = lax.optimization_barrier((tuple(events), xs))
    return tied[1] if len(xs) > 1 else tied[1][0]


def params(limit):
    return pltpu.CompilerParams(vmem_limit_bytes=limit * 1024 * 1024)


class Rows:
    def __init__(self, parts, role, at):
        self.parts, self.role, self.at = parts, role, at
        self.rows = parts[0][0].shape[0]
        self.total = sum(part[2] for part in parts)


def block_sums(meta, slot, low, start, count, b):
    name = meta[NAMES + 4 * slot + b]
    chip = name >> 2
    place = ((((name >> 1) & 1) ^ meta[CORE]) << 2) + jnp.where(chip == meta[ZPOS], 0, 2) + (name & 1)
    place = jnp.where((chip == meta[ZPOS]) | (chip == (meta[ZPOS] ^ 1)), place, -1)
    value = jnp.zeros((count, 64), jnp.float32)
    for i in range(8):
        part = low[start + b * count : start + (b + 1) * count, i * 64 : i * 64 + 64]
        value = value + jnp.where(place == i, part, 0.0)
    return value.astype(jnp.bfloat16)


def accumulate(ref, rows, cols, value, k, first):
    if first:
        value = value + jnp.where(k == 0, 0.0, ref[rows, cols])
    else:
        value = value + ref[rows, cols]
    ref[rows, cols] = value


def times_transposed(x, a):
    return lax.dot_general(x, a, (((1,), (1,)), ((), ())), preferred_element_type=jnp.float32)


def products_kernel(jobs, weights, meta, *refs):
    refs = list(refs)
    xs = [[refs.pop(0) for _ in job.parts] for job in jobs]
    ws = [(refs.pop(0), refs.pop(0)) for _ in range(weights)]
    out, acc = refs
    k = pl.program_id(0)
    top = {0: 0, 1: 0}
    for x_parts, job in zip(xs, jobs):
        start = max(top.values()) if job.role is None else top[job.role]
        for role in top if job.role is None else (job.role,):
            top[role] = start + job.rows
        mine = slice(start, start + job.rows)
        role = True if job.role is None else meta[INNER] == job.role
        base = 0
        for x, (_, _, tiles, weight) in zip(x_parts, job.parts):

            def step(x=x, mine=mine, pair=ws[weight], first=base == 0):
                for h, w in enumerate(pair):
                    for n in range(0, WIDE // 2, 512):
                        at = slice(h * (WIDE // 2) + n, h * (WIDE // 2) + n + 512)
                        accumulate(acc, mine, at, dot(x[...], w[:, n : n + 512]), k, first)

            pl.when(role & (k >= base) & (k < base + tiles))(step)
            base += tiles

        def store(job=job, start=start):
            count = job.rows // 4
            for b in range(4):
                value = acc[start + b * count : start + (b + 1) * count, :]
                out[b, job.at : job.at + count, :] = value.astype(jnp.bfloat16)

        pl.when(role & (k == job.total - 1))(store)


def products(meta, jobs, weights, rows):
    steps = max(job.total for job in jobs)
    in_specs, args, uses = [], [], {}
    for job in jobs:
        base = 0
        for x, tile, tiles, weight in job.parts:

            def index(k, m, base=base, tile=tile, tiles=tiles, role=job.role):
                at = jnp.clip(k - base, 0, tiles - 1)
                if role is not None:
                    at = at * (m[INNER] if role == 1 else 1 - m[INNER])
                return (0, at + tile)

            in_specs.append(pl.BlockSpec((x.shape[0], TILE), index))
            args.append(x)
            for role in (0, 1) if job.role is None else (job.role,):
                uses[weight, role] = (base, tiles)
            base += tiles
    for i, (own, own_tile, other, other_tile) in enumerate(weights):
        for w, tile in ((own, own_tile), (other, other_tile)):

            def index(k, m, i=i, tile=tile):
                at = [jnp.clip(k - base, 0, tiles - 1) for base, tiles in (uses.get((i, r), (0, 1)) for r in (0, 1))]
                return (jnp.where(m[INNER] == 1, at[1], at[0]) + tile, 0)

            in_specs.append(pl.BlockSpec((TILE, w.shape[1]), index))
            args.append(w)
    both = sum(job.rows for job in jobs if job.role is None)
    height = both + max(sum(job.rows for job in jobs if job.role == r) for r in (0, 1))
    shape = (4, rows, WIDE)
    return pl.pallas_call(
        functools.partial(products_kernel, jobs, len(weights)),
        grid_spec=pltpu.PrefetchScalarGridSpec(
            num_scalar_prefetch=1,
            grid=(steps,),
            in_specs=in_specs,
            out_specs=pl.BlockSpec(shape, lambda k, m: (0, 0, 0)),
            scratch_shapes=[pltpu.VMEM((height, WIDE), jnp.float32)],
        ),
        out_shape=pltpu.HBM(shape, jnp.bfloat16),
        compiler_params=params(50),
        cost_estimate=CHEAP,
    )(meta, *args)


def shrink_kernel(tiles, slots, steps, meta, *refs):
    refs = list(refs)
    xs = [[refs.pop(0) for _ in part] for part in tiles]
    mine, other, held_mine, held_other, out, low = refs
    k = pl.program_id(0)
    inner = meta[INNER] == 1
    rows = BLOCK * 4
    for i, x_parts in enumerate(xs):
        base = 0
        for x, count in zip(x_parts, tiles[i]):

            @pl.when(inner & (k >= base) & (k < base + count))
            def _(i=i, x=x, first=base == 0):
                here = slice(i * rows, (i + 1) * rows)
                for h, a in enumerate((mine, other)):
                    accumulate(low, here, slice(h * 256, h * 256 + 256), times_transposed(x[...], a[...]), k, first)

            base += count

    @pl.when(inner & (k == steps - 1))
    def _():
        for i, slot in enumerate(slots):
            for b in range(4):
                at = 2 * SHARE + i * 64
                out[b, :, at : at + 64] = block_sums(meta, slot, low, i * rows, BLOCK, b)

    @pl.when(k == 0)
    def _():
        for b in range(4):
            for slot in range(4):
                name = meta[NAMES + 4 * slot + b]
                index = 2 * ((name >> 2) ^ meta[ZPOS]) + (name & 1)
                value = jnp.where(((name >> 1) & 1) == meta[CORE], held_mine[index], held_other[index])
                at = slot // 2 * SHARE
                out[b, slot % 2 * 64 : slot % 2 * 64 + 64, at : at + SHARE] = value


def shrink_sums(meta, xs, slots, mine, other, held):
    tiles = [[part.shape[1] // TILE for part in x] for x in xs]
    steps = sum(tiles[0])
    in_specs, args = [], []
    for x, counts in zip(xs, tiles):
        base = 0
        for part, count in zip(x, counts):

            def index(k, m, base=base, count=count):
                return (0, jnp.clip(k - base, 0, count - 1) * m[INNER])

            in_specs.append(pl.BlockSpec((part.shape[0], TILE), index))
            args.append(part)
            base += count
    for a in (mine, other):
        in_specs.append(pl.BlockSpec((a.shape[0], TILE), lambda k, m: (0, k * m[INNER])))
        args.append(a)
    for a in held:
        in_specs.append(pl.BlockSpec(a.shape, lambda k, m: (0, 0, 0)))
        args.append(a)
    shape = (4, BLOCK, 2 * SHARE + 256)
    return pl.pallas_call(
        functools.partial(shrink_kernel, tiles, slots, steps),
        grid_spec=pltpu.PrefetchScalarGridSpec(
            num_scalar_prefetch=1,
            grid=(steps,),
            in_specs=in_specs,
            out_specs=pl.BlockSpec(shape, lambda k, m: (0, 0, 0)),
            scratch_shapes=[pltpu.VMEM((4 * BLOCK * len(xs), 512), jnp.float32)],
        ),
        out_shape=pltpu.HBM(shape, jnp.bfloat16),
        compiler_params=params(40),
        cost_estimate=CHEAP,
    )(meta, *args)


def low_kernel(x, out, swapped):
    value = x[0].astype(jnp.float32)
    for b in range(1, 4):
        value = value + x[b].astype(jnp.float32)
    value = value.astype(jnp.bfloat16)
    out[...] = value
    swapped[...] = jnp.concatenate([value[:, i * 64 : i * 64 + 64] for i in (1, 0, 3, 2)], axis=1)


def low_sums(x):
    shape = jax.ShapeDtypeStruct((BLOCK, 256), jnp.bfloat16)
    whole = pl.BlockSpec((BLOCK, 256), lambda i: (0, 0))
    return pl.pallas_call(
        low_kernel,
        grid=(1,),
        in_specs=[pl.BlockSpec((4, BLOCK, 256), lambda i: (0, 0, 2 * SHARE // 256))],
        out_specs=(whole, whole),
        out_shape=(shape, shape),
        cost_estimate=CHEAP,
    )(x)


def add_kernel(x, y, out):
    out[...] = (x[...].astype(jnp.float32) + y[...].astype(jnp.float32)).astype(jnp.bfloat16)


def add(x, y):
    return pl.pallas_call(add_kernel, out_shape=jax.ShapeDtypeStruct(x.shape, x.dtype), cost_estimate=CHEAP)(x, y)


def finish_kernel(role, row, rows, lanes, has_more, meta, *refs):
    refs = list(refs)
    part = refs.pop(0)
    if lanes:
        low_in, low_out, expand = refs.pop(0), refs.pop(0), refs.pop(0)
    more = refs.pop(0) if has_more else None
    out = refs.pop(0)

    def run():
        total = part[0, row : row + rows, :].astype(jnp.float32)
        for b in range(1, 4):
            total = total + part[b, row : row + rows, :].astype(jnp.float32)
        if lanes:
            x = low_in[:rows, lanes[0] : lanes[0] + 64]
            y = low_out[:rows, lanes[1] : lanes[1] + 64]
            x = jnp.where(meta[INNER] == 1, x, y)
            delta = [dot(x, expand[i]) for i in range(expand.shape[0])]
            total = total + SCALE * jnp.concatenate(delta, axis=1)
        if has_more:
            total = total + more[...].astype(jnp.float32)
        out[...] = total.astype(jnp.bfloat16)

    if role is None:
        run()
    else:
        pl.when(meta[INNER] == role)(run)


def finish(meta, role, part, row, low=None, more=None, rows=BLOCK):
    span = WIDE // 2
    in_specs = [pl.BlockSpec((4, part.shape[1], span), lambda h, m: (0, 0, h))]
    args = [part]
    lanes = None
    if low is not None:
        *sums, expand, slots = low
        for x in sums:
            in_specs.append(pl.BlockSpec(x.shape, lambda h, m: (0, 0)))
            args.append(x)

        def index(h, m):
            slot = slots[1] + (slots[0] - slots[1]) * m[INNER]
            return (h ^ m[CORE], slot & 1, slot >> 1)

        in_specs.append(pl.BlockSpec((span // SHARE, 64, SHARE), index))
        args.append(expand)
        lanes = [64 * (0, 2, 1, 3)[slots[0]], 64 * (2, 0, 1, 3)[slots[1]]]
    if more is not None:
        in_specs.append(pl.BlockSpec((rows, span), lambda h, m: (0, h)))
        args.append(more)
    return pl.pallas_call(
        functools.partial(finish_kernel, role, row, rows, lanes, more is not None),
        grid_spec=pltpu.PrefetchScalarGridSpec(
            num_scalar_prefetch=1,
            grid=(2,),
            in_specs=in_specs,
            out_specs=pl.BlockSpec((rows, span), lambda h, m: (0, h)),
        ),
        out_shape=jax.ShapeDtypeStruct((rows, WIDE), jnp.bfloat16),
        compiler_params=params(32),
        cost_estimate=CHEAP,
    )(meta, *args)


def assemble_kernel(span, meta, count, own, one, two, inner_three, outer_three, out):
    z, c, inner = meta[ZPOS], meta[CORE], meta[INNER] == 1
    rows = own.shape[0]
    valid = lax.broadcasted_iota(jnp.int32, (rows, 1), 0) < count[0]

    def put(j, source):
        for h in range(2):
            at = pl.ds(pl.multiple_of((2 * j + h) * span, span), span)
            part = pl.ds(pl.multiple_of((h ^ c) * span, span), span)
            out[:, at] = jnp.where(valid, source[:, part], jnp.zeros((), jnp.bfloat16))

    put(z, own)
    put(z ^ 1, one)
    put(z ^ 2, two)

    @pl.when(inner)
    def _():
        put(z ^ 3, inner_three)

    @pl.when(jnp.logical_not(inner))
    def _():
        put(z ^ 3, outer_three)


def assemble(meta, count, *args):
    rows, wide = args[0].shape
    return pl.pallas_call(
        functools.partial(assemble_kernel, wide // 2),
        grid_spec=pltpu.PrefetchScalarGridSpec(
            num_scalar_prefetch=2,
            grid=(1,),
            in_specs=[pl.BlockSpec(a.shape, lambda n, m, k: (0, 0)) for a in args],
            out_specs=pl.BlockSpec((rows, 4 * wide), lambda n, m, k: (0, 0)),
        ),
        out_shape=jax.ShapeDtypeStruct((rows, 4 * wide), jnp.bfloat16),
        compiler_params=params(32),
        cost_estimate=CHEAP,
    )(meta, count, *args)


def line_of_four(hidden, down_weight, adapter_shrink, adapter_expand, block_adapter, block_rows):
    rows, feat = hidden.shape
    adp, _, rank = adapter_shrink.shape
    p = lax.axis_index("pool")
    t = lax.axis_index("tensor")
    tensors = lax.axis_size("tensor")
    z, c = p // 2, p % 2
    outer = (z == 0) | (z == 3)

    def exchange(x):
        return lax.all_to_all(x, "tensor", split_axis=0, concat_axis=0, tiled=True)

    place = jnp.stack([jnp.where(outer, 0, 1), c, z]).astype(jnp.int32)

    mid = send(hidden, MIDDLE)
    partner = send(hidden, XOR[1])
    cuts = [(0, 2 * TILE), (2 * TILE, 4 * TILE), (4 * TILE, NEAR), (NEAR, feat)]
    pieces = [down_weight[lo:hi] for lo, hi in cuts]
    others = [send(w, SIBLING) for w in pieces]
    weights = [(down_weight, lo // TILE, w, 0) for (lo, _), w in zip(cuts, others)]

    def whole(x):
        return [(x, lo // TILE, (hi - lo) // TILE, i) for i, (lo, hi) in enumerate(cuts)]

    shares = exchange(
        adapter_expand.transpose(0, 2, 1).reshape(adp, rank, tensors, SHARE).transpose(2, 0, 1, 3)
    ).reshape(tensors, adp * rank, SHARE)
    label = jnp.zeros((16, SHARE), jnp.bfloat16).at[0, : block_adapter.shape[0]].set(block_adapter.astype(jnp.bfloat16))
    j_own = products(place, [Rows(whole(hidden), None, 0)], weights, BLOCK)

    ready = [partner, mid, j_own]
    far = send(after(ready, partner), MIDDLE)
    out_mid = send(after(ready, mid), OUTWARD)
    v_own = [send(after(ready, w), INWARD) for w in pieces[3:]]
    r_own = exchange(j_own)
    j_partner = products(place, [Rows(whole(partner), None, 0)], weights, BLOCK)
    r_partner = exchange(j_partner)
    j_mid = products(place, [Rows(whole(after([j_partner], mid)), 1, 0)], weights, BLOCK)
    r_mid = exchange(j_mid)
    shrink_w = adapter_shrink.transpose(0, 2, 1).reshape(adp * rank, feat)
    shrink_o = send(after([partner, mid], shrink_w), INWARD)
    shares = after([j_mid, *v_own, shrink_o], shares)

    def shares_of(s):
        return lax.dynamic_index_in_dim(shares, z ^ s, 0, keepdims=False)

    told = [send(jnp.concatenate([shares_of(s), label], axis=0), XOR[s]) for s in (1, 2, 3)]

    far_near = far[:, :NEAR]
    out_far = send(after([out_mid, *told], far_near), OUTWARD)
    j_third = products(
        place,
        [Rows(whole(after([r_partner, far_near, *told], far)), 1, 0), Rows(whole(out_mid), 0, 0)],
        weights,
        BLOCK,
    )
    r_third = exchange(j_third)
    v_other = [send(after([out_far, j_third], w), SIBLING) for w in v_own]

    held = jnp.concatenate([shares_of(0)] + [x[: adp * rank] for x in told]).reshape(4 * adp, rank, SHARE)
    held = (held, send(held, SIBLING))
    names = [block_adapter] + [x[adp * rank, : block_adapter.shape[0]].astype(jnp.int32) for x in told]
    name_m = jnp.where(outer, names[2], names[3])
    name_f = jnp.where(outer, names[3], names[2])
    meta = jnp.concatenate([place, names[0], names[1], name_m, name_f])
    shrink_mine = jnp.concatenate([shrink_w, after([j_third], shrink_o)], axis=0)
    shrink_other = send(shrink_mine, SIBLING)
    sums = shrink_sums(meta, [[hidden], [mid], [partner], [far]], [0, 2, 1, 3], shrink_mine, shrink_other, held)
    r_sums = exchange(sums)
    low, swapped = low_sums(r_sums)
    low = add(low, send(swapped, MIDDLE))
    low_out = send(low, OUTWARD)

    rest = [(a, 0, b, 0) for a, b in zip(v_own, v_other)] + weights[:3]
    j_fifth = products(
        place,
        [
            Rows([(after([sums], far), NEAR // TILE, 2, 0)], 1, 0),
            Rows([(out_far, 0, 2, 1), (out_far, 2, 2, 2), (out_far, 4, 1, 3)], 0, 0),
        ],
        rest,
        BLOCK,
    )
    r_fifth = exchange(j_fifth)

    def term(inner_slot, outer_slot):
        return (low, low_out, r_sums, (inner_slot, outer_slot))

    x_partner = finish(meta, None, r_partner, 0, term(1, 1))
    home_partner = send(x_partner, XOR[1])
    x_two = finish(meta, None, r_third, 0, term(3, 2))
    home_two = send(x_two, XOR[2])
    x_mid = finish(meta, 1, r_mid, 0, term(2, 2))
    home_mid = send(x_mid, MIDDLE)
    x_own = finish(meta, None, r_own, 0, term(0, 0))
    r_fifth = after([x_partner, x_two, x_mid, x_own], r_fifth)
    x_far = finish(meta, 0, r_fifth, 0, term(3, 3))
    to_far = send(x_far, INWARD)
    to_far = after([home_partner, home_two, home_mid], to_far)
    home_far = send(finish(meta, 1, r_fifth, 0, more=to_far), ACROSS)
    count = lax.dynamic_slice_in_dim(block_rows, t, 1, 0)
    return assemble(meta, count, x_own, home_partner, home_two, home_mid, home_far)


def solution(mesh):
    in_specs = (
        P("pool", "tensor"),
        P("tensor", "pool"),
        P("pool", "tensor", None),
        P("pool", "tensor", None),
        P("pool"),
        P("pool"),
    )
    out_specs = P(("pool", "tensor"), None)
    body = line_of_four if dict(mesh.shape) == {"pool": 8, "tensor": 4} else general
    return jax.shard_map(body, mesh=mesh, in_specs=in_specs, out_specs=out_specs, check_vma=False)
```

```python
import functools

import jax
import jax.numpy as jnp
from jax import lax
from jax.experimental import pallas as pl
from jax.experimental.pallas import tpu as pltpu
from jax.sharding import PartitionSpec as P

BLOCK = 128
SCALE = 0.5


def general(hidden, down_weight, adapter_shrink, adapter_expand, block_adapter, block_rows):
    input_rows, feat = hidden.shape
    block_count = block_adapter.shape[0]
    column_span = adapter_expand.shape[1]
    tensor_pos = lax.axis_index("tensor")
    tensor_count = lax.axis_size("tensor")
    own_rows = input_rows // tensor_count
    blocks = hidden.reshape(block_count, BLOCK, feat)
    partial_value = jnp.dot(
        hidden,
        lax.all_gather(down_weight, "pool", axis=1, tiled=True),
        preferred_element_type=jnp.float32,
    )
    total = lax.psum_scatter(
        partial_value.astype(jnp.bfloat16), "tensor", scatter_dimension=0, tiled=True
    ).astype(jnp.float32)
    shrink_piece = lax.all_gather(adapter_shrink, "pool", axis=0, tiled=True)
    expand_piece = lax.all_gather(adapter_expand, "pool", axis=0, tiled=True)
    idents = jnp.arange(shrink_piece.shape[0], dtype=jnp.int32)
    pick = (block_adapter[:, None] == idents[None, :]).astype(jnp.bfloat16)
    first = jnp.einsum("bk,kfr->bfr", pick, shrink_piece, preferred_element_type=jnp.float32)
    second = jnp.einsum("bk,kcr->bcr", pick, expand_piece, preferred_element_type=jnp.float32)
    shrink = jnp.einsum(
        "bnf,bfr->bnr", blocks, first.astype(jnp.bfloat16), preferred_element_type=jnp.float32
    )
    summed_shrink = lax.psum(shrink.astype(jnp.bfloat16), "tensor")
    enlarged_rows = jnp.einsum(
        "bnr,bcr->bnc",
        summed_shrink,
        second.astype(jnp.bfloat16),
        preferred_element_type=jnp.float32,
    )
    adapter_delta_columns = (
        (SCALE * enlarged_rows).astype(jnp.bfloat16).reshape(input_rows, column_span)
    )
    delta_mine = lax.all_to_all(
        adapter_delta_columns, "tensor", split_axis=0, concat_axis=1, tiled=True
    )
    total = total + delta_mine.astype(jnp.float32)
    row_ids = tensor_pos * own_rows + jnp.arange(own_rows, dtype=jnp.int32)
    owning = (row_ids // BLOCK)[:, None] == jnp.arange(block_count, dtype=jnp.int32)[None, :]
    lengths = jnp.sum(jnp.where(owning, block_rows[None, :], 0), axis=1)
    valid = (row_ids % BLOCK < lengths).astype(jnp.float32)
    return (total * valid[:, None]).astype(jnp.bfloat16)


def dot(a, b):
    return jnp.dot(a, b, preferred_element_type=jnp.float32)


def on_line(pairs):
    return [(2 * a + c, 2 * b + c) for a, b in pairs for c in range(2)]


XOR = {s: on_line([(z, z ^ s) for z in range(4)]) for s in (1, 2, 3)}
MIDDLE = on_line([(1, 2), (2, 1)])
OUTWARD = on_line([(1, 0), (2, 3)])
INWARD = on_line([(0, 1), (3, 2)])
ACROSS = on_line([(1, 3), (2, 0)])
SIBLING = [(p, p ^ 1) for p in range(8)]

TILE = 512
NEAR = 5 * TILE
WIDE = 2048
SHARE = 512
INNER, CORE, ZPOS, NAMES = 0, 1, 2, 3
CHEAP = pl.CostEstimate(flops=1000, bytes_accessed=1000, transcendentals=0)


def send(x, pairs):
    return lax.ppermute(x, "pool", pairs)


def after(events, *xs):
    tied = lax.optimization_barrier((tuple(events), xs))
    return tied[1] if len(xs) > 1 else tied[1][0]


def params(limit):
    return pltpu.CompilerParams(vmem_limit_bytes=limit * 1024 * 1024)


class Rows:
    def __init__(self, parts, role, at):
        self.parts, self.role, self.at = parts, role, at
        self.rows = parts[0][0].shape[0]
        self.total = sum(part[2] for part in parts)


def block_sums(meta, slot, low, start, count, b):
    name = meta[NAMES + 4 * slot + b]
    chip = name >> 2
    place = ((((name >> 1) & 1) ^ meta[CORE]) << 2) + jnp.where(chip == meta[ZPOS], 0, 2) + (name & 1)
    place = jnp.where((chip == meta[ZPOS]) | (chip == (meta[ZPOS] ^ 1)), place, -1)
    value = jnp.zeros((count, 64), jnp.float32)
    for i in range(8):
        part = low[start + b * count : start + (b + 1) * count, i * 64 : i * 64 + 64]
        value = value + jnp.where(place == i, part, 0.0)
    return value.astype(jnp.bfloat16)


def accumulate(ref, rows, cols, value, k, first):
    if first:
        value = value + jnp.where(k == 0, 0.0, ref[rows, cols])
    else:
        value = value + ref[rows, cols]
    ref[rows, cols] = value


def times_transposed(x, a):
    return lax.dot_general(x, a, (((1,), (1,)), ((), ())), preferred_element_type=jnp.float32)


def products_kernel(jobs, weights, meta, *refs):
    refs = list(refs)
    xs = [[refs.pop(0) for _ in job.parts] for job in jobs]
    ws = [(refs.pop(0), refs.pop(0)) for _ in range(weights)]
    out, acc = refs
    k = pl.program_id(0)
    top = {0: 0, 1: 0}
    for x_parts, job in zip(xs, jobs):
        start = max(top.values()) if job.role is None else top[job.role]
        for role in top if job.role is None else (job.role,):
            top[role] = start + job.rows
        mine = slice(start, start + job.rows)
        role = True if job.role is None else meta[INNER] == job.role
        base = 0
        for x, (_, _, tiles, weight) in zip(x_parts, job.parts):

            def step(x=x, mine=mine, pair=ws[weight], first=base == 0):
                for h, w in enumerate(pair):
                    for n in range(0, WIDE // 2, 512):
                        at = slice(h * (WIDE // 2) + n, h * (WIDE // 2) + n + 512)
                        accumulate(acc, mine, at, dot(x[...], w[:, n : n + 512]), k, first)

            pl.when(role & (k >= base) & (k < base + tiles))(step)
            base += tiles

        def store(job=job, start=start):
            count = job.rows // 4
            for b in range(4):
                value = acc[start + b * count : start + (b + 1) * count, :]
                out[b, job.at : job.at + count, :] = value.astype(jnp.bfloat16)

        pl.when(role & (k == job.total - 1))(store)


def products(meta, jobs, weights, rows):
    steps = max(job.total for job in jobs)
    in_specs, args, uses = [], [], {}
    for job in jobs:
        base = 0
        for x, tile, tiles, weight in job.parts:

            def index(k, m, base=base, tile=tile, tiles=tiles, role=job.role):
                at = jnp.clip(k - base, 0, tiles - 1)
                if role is not None:
                    at = at * (m[INNER] if role == 1 else 1 - m[INNER])
                return (0, at + tile)

            in_specs.append(pl.BlockSpec((x.shape[0], TILE), index))
            args.append(x)
            for role in (0, 1) if job.role is None else (job.role,):
                uses[weight, role] = (base, tiles)
            base += tiles
    for i, (own, own_tile, other, other_tile) in enumerate(weights):
        for w, tile in ((own, own_tile), (other, other_tile)):

            def index(k, m, i=i, tile=tile):
                at = [jnp.clip(k - base, 0, tiles - 1) for base, tiles in (uses.get((i, r), (0, 1)) for r in (0, 1))]
                return (jnp.where(m[INNER] == 1, at[1], at[0]) + tile, 0)

            in_specs.append(pl.BlockSpec((TILE, w.shape[1]), index))
            args.append(w)
    both = sum(job.rows for job in jobs if job.role is None)
    height = both + max(sum(job.rows for job in jobs if job.role == r) for r in (0, 1))
    shape = (4, rows, WIDE)
    return pl.pallas_call(
        functools.partial(products_kernel, jobs, len(weights)),
        grid_spec=pltpu.PrefetchScalarGridSpec(
            num_scalar_prefetch=1,
            grid=(steps,),
            in_specs=in_specs,
            out_specs=pl.BlockSpec(shape, lambda k, m: (0, 0, 0)),
            scratch_shapes=[pltpu.VMEM((height, WIDE), jnp.float32)],
        ),
        out_shape=pltpu.HBM(shape, jnp.bfloat16),
        compiler_params=params(50),
        cost_estimate=CHEAP,
    )(meta, *args)


def shrink_kernel(tiles, slots, steps, meta, *refs):
    refs = list(refs)
    xs = [[refs.pop(0) for _ in part] for part in tiles]
    mine, other, held_mine, held_other, out, low = refs
    k = pl.program_id(0)
    inner = meta[INNER] == 1
    rows = BLOCK * 4
    for i, x_parts in enumerate(xs):
        base = 0
        for x, count in zip(x_parts, tiles[i]):

            @pl.when(inner & (k >= base) & (k < base + count))
            def _(i=i, x=x, first=base == 0):
                here = slice(i * rows, (i + 1) * rows)
                for h, a in enumerate((mine, other)):
                    accumulate(low, here, slice(h * 256, h * 256 + 256), times_transposed(x[...], a[...]), k, first)

            base += count

    @pl.when(inner & (k == steps - 1))
    def _():
        for i, slot in enumerate(slots):
            for b in range(4):
                at = 2 * SHARE + i * 64
                out[b, :, at : at + 64] = block_sums(meta, slot, low, i * rows, BLOCK, b)

    @pl.when(k == 0)
    def _():
        for b in range(4):
            for slot in range(4):
                name = meta[NAMES + 4 * slot + b]
                index = 2 * ((name >> 2) ^ meta[ZPOS]) + (name & 1)
                value = jnp.where(((name >> 1) & 1) == meta[CORE], held_mine[index], held_other[index])
                at = slot // 2 * SHARE
                out[b, slot % 2 * 64 : slot % 2 * 64 + 64, at : at + SHARE] = value


def shrink_sums(meta, xs, slots, mine, other, held):
    tiles = [[part.shape[1] // TILE for part in x] for x in xs]
    steps = sum(tiles[0])
    in_specs, args = [], []
    for x, counts in zip(xs, tiles):
        base = 0
        for part, count in zip(x, counts):

            def index(k, m, base=base, count=count):
                return (0, jnp.clip(k - base, 0, count - 1) * m[INNER])

            in_specs.append(pl.BlockSpec((part.shape[0], TILE), index))
            args.append(part)
            base += count
    for a in (mine, other):
        in_specs.append(pl.BlockSpec((a.shape[0], TILE), lambda k, m: (0, k * m[INNER])))
        args.append(a)
    for a in held:
        in_specs.append(pl.BlockSpec(a.shape, lambda k, m: (0, 0, 0)))
        args.append(a)
    shape = (4, BLOCK, 2 * SHARE + 256)
    return pl.pallas_call(
        functools.partial(shrink_kernel, tiles, slots, steps),
        grid_spec=pltpu.PrefetchScalarGridSpec(
            num_scalar_prefetch=1,
            grid=(steps,),
            in_specs=in_specs,
            out_specs=pl.BlockSpec(shape, lambda k, m: (0, 0, 0)),
            scratch_shapes=[pltpu.VMEM((4 * BLOCK * len(xs), 512), jnp.float32)],
        ),
        out_shape=pltpu.HBM(shape, jnp.bfloat16),
        compiler_params=params(40),
        cost_estimate=CHEAP,
    )(meta, *args)


def low_kernel(x, out, swapped):
    value = x[0].astype(jnp.float32)
    for b in range(1, 4):
        value = value + x[b].astype(jnp.float32)
    value = value.astype(jnp.bfloat16)
    out[...] = value
    swapped[...] = jnp.concatenate([value[:, i * 64 : i * 64 + 64] for i in (1, 0, 3, 2)], axis=1)


def low_sums(x):
    shape = jax.ShapeDtypeStruct((BLOCK, 256), jnp.bfloat16)
    whole = pl.BlockSpec((BLOCK, 256), lambda i: (0, 0))
    return pl.pallas_call(
        low_kernel,
        grid=(1,),
        in_specs=[pl.BlockSpec((4, BLOCK, 256), lambda i: (0, 0, 2 * SHARE // 256))],
        out_specs=(whole, whole),
        out_shape=(shape, shape),
        cost_estimate=CHEAP,
    )(x)


def add_kernel(x, y, out):
    out[...] = (x[...].astype(jnp.float32) + y[...].astype(jnp.float32)).astype(jnp.bfloat16)


def add(x, y):
    return pl.pallas_call(add_kernel, out_shape=jax.ShapeDtypeStruct(x.shape, x.dtype), cost_estimate=CHEAP)(x, y)


def finish_kernel(role, row, rows, lanes, has_more, meta, *refs):
    refs = list(refs)
    part = refs.pop(0)
    if lanes:
        low_in, low_out, expand = refs.pop(0), refs.pop(0), refs.pop(0)
    more = refs.pop(0) if has_more else None
    out = refs.pop(0)

    def run():
        total = part[0, row : row + rows, :].astype(jnp.float32)
        for b in range(1, 4):
            total = total + part[b, row : row + rows, :].astype(jnp.float32)
        if lanes:
            x = low_in[:rows, lanes[0] : lanes[0] + 64]
            y = low_out[:rows, lanes[1] : lanes[1] + 64]
            x = jnp.where(meta[INNER] == 1, x, y)
            delta = [dot(x, expand[i]) for i in range(expand.shape[0])]
            total = total + SCALE * jnp.concatenate(delta, axis=1)
        if has_more:
            total = total + more[...].astype(jnp.float32)
        out[...] = total.astype(jnp.bfloat16)

    if role is None:
        run()
    else:
        pl.when(meta[INNER] == role)(run)


def finish(meta, role, part, row, low=None, more=None, rows=BLOCK):
    span = WIDE // 2
    in_specs = [pl.BlockSpec((4, part.shape[1], span), lambda h, m: (0, 0, h))]
    args = [part]
    lanes = None
    if low is not None:
        *sums, expand, slots = low
        for x in sums:
            in_specs.append(pl.BlockSpec(x.shape, lambda h, m: (0, 0)))
            args.append(x)

        def index(h, m):
            slot = slots[1] + (slots[0] - slots[1]) * m[INNER]
            return (h ^ m[CORE], slot & 1, slot >> 1)

        in_specs.append(pl.BlockSpec((span // SHARE, 64, SHARE), index))
        args.append(expand)
        lanes = [64 * (0, 2, 1, 3)[slots[0]], 64 * (2, 0, 1, 3)[slots[1]]]
    if more is not None:
        in_specs.append(pl.BlockSpec((rows, span), lambda h, m: (0, h)))
        args.append(more)
    return pl.pallas_call(
        functools.partial(finish_kernel, role, row, rows, lanes, more is not None),
        grid_spec=pltpu.PrefetchScalarGridSpec(
            num_scalar_prefetch=1,
            grid=(2,),
            in_specs=in_specs,
            out_specs=pl.BlockSpec((rows, span), lambda h, m: (0, h)),
        ),
        out_shape=jax.ShapeDtypeStruct((rows, WIDE), jnp.bfloat16),
        compiler_params=params(32),
        cost_estimate=CHEAP,
    )(meta, *args)


def assemble_kernel(span, meta, count, own, one, two, inner_three, outer_three, out):
    z, c, inner = meta[ZPOS], meta[CORE], meta[INNER] == 1
    rows = own.shape[0]
    valid = lax.broadcasted_iota(jnp.int32, (rows, 1), 0) < count[0]

    def put(j, source):
        for h in range(2):
            at = pl.ds(pl.multiple_of((2 * j + h) * span, span), span)
            part = pl.ds(pl.multiple_of((h ^ c) * span, span), span)
            out[:, at] = jnp.where(valid, source[:, part], jnp.zeros((), jnp.bfloat16))

    put(z, own)
    put(z ^ 1, one)
    put(z ^ 2, two)

    @pl.when(inner)
    def _():
        put(z ^ 3, inner_three)

    @pl.when(jnp.logical_not(inner))
    def _():
        put(z ^ 3, outer_three)


def assemble(meta, count, *args):
    rows, wide = args[0].shape
    return pl.pallas_call(
        functools.partial(assemble_kernel, wide // 2),
        grid_spec=pltpu.PrefetchScalarGridSpec(
            num_scalar_prefetch=2,
            grid=(1,),
            in_specs=[pl.BlockSpec(a.shape, lambda n, m, k: (0, 0)) for a in args],
            out_specs=pl.BlockSpec((rows, 4 * wide), lambda n, m, k: (0, 0)),
        ),
        out_shape=jax.ShapeDtypeStruct((rows, 4 * wide), jnp.bfloat16),
        compiler_params=params(32),
        cost_estimate=CHEAP,
    )(meta, count, *args)


def line_of_four(hidden, down_weight, adapter_shrink, adapter_expand, block_adapter, block_rows):
    rows, feat = hidden.shape
    adp, _, rank = adapter_shrink.shape
    p = lax.axis_index("pool")
    t = lax.axis_index("tensor")
    tensors = lax.axis_size("tensor")
    z, c = p // 2, p % 2
    outer = (z == 0) | (z == 3)

    def exchange(x):
        return lax.all_to_all(x, "tensor", split_axis=0, concat_axis=0, tiled=True)

    place = jnp.stack([jnp.where(outer, 0, 1), c, z]).astype(jnp.int32)

    mid = send(hidden, MIDDLE)
    partner = send(hidden, XOR[1])
    cuts = [(0, 2 * TILE), (2 * TILE, 4 * TILE), (4 * TILE, NEAR), (NEAR, feat)]
    pieces = [down_weight[lo:hi] for lo, hi in cuts]
    others = [send(w, SIBLING) for w in pieces]
    weights = [(down_weight, lo // TILE, w, 0) for (lo, _), w in zip(cuts, others)]

    def whole(x):
        return [(x, lo // TILE, (hi - lo) // TILE, i) for i, (lo, hi) in enumerate(cuts)]

    shares = exchange(
        adapter_expand.transpose(0, 2, 1).reshape(adp, rank, tensors, SHARE).transpose(2, 0, 1, 3)
    ).reshape(tensors, adp * rank, SHARE)
    label = jnp.zeros((16, SHARE), jnp.bfloat16).at[0, : block_adapter.shape[0]].set(block_adapter.astype(jnp.bfloat16))
    j_own = products(place, [Rows(whole(hidden), None, 0)], weights, BLOCK)

    ready = [partner, mid, j_own]
    far = send(after(ready, partner), MIDDLE)
    out_mid = send(after(ready, mid), OUTWARD)
    v_own = [send(after(ready, w), INWARD) for w in pieces[3:]]
    r_own = exchange(j_own)
    j_partner = products(place, [Rows(whole(partner), None, 0)], weights, BLOCK)
    r_partner = exchange(j_partner)
    j_mid = products(place, [Rows(whole(after([j_partner], mid)), 1, 0)], weights, BLOCK)
    r_mid = exchange(j_mid)
    shrink_w = adapter_shrink.transpose(0, 2, 1).reshape(adp * rank, feat)
    shrink_o = send(after([partner, mid], shrink_w), INWARD)
    shares = after([j_mid, *v_own, shrink_o], shares)

    def shares_of(s):
        return lax.dynamic_index_in_dim(shares, z ^ s, 0, keepdims=False)

    told = [send(jnp.concatenate([shares_of(s), label], axis=0), XOR[s]) for s in (1, 2, 3)]

    held = jnp.concatenate([shares_of(0)] + [x[: adp * rank] for x in told]).reshape(4 * adp, rank, SHARE)
    held = (held, send(held, SIBLING))
    shrink_mine = jnp.concatenate([shrink_w, after([j_mid], shrink_o)], axis=0)
    shrink_other = send(shrink_mine, SIBLING)

    far_near = far[:, :NEAR]
    out_far = send(after([out_mid, *told], far_near), OUTWARD)
    j_third = products(
        place,
        [Rows(whole(after([r_partner, far_near, held[1], shrink_other], far)), 1, 0), Rows(whole(out_mid), 0, 0)],
        weights,
        BLOCK,
    )
    r_third = exchange(j_third)
    v_other = [send(after([out_far, j_third], w), SIBLING) for w in v_own]

    names = [block_adapter] + [x[adp * rank, : block_adapter.shape[0]].astype(jnp.int32) for x in told]
    name_m = jnp.where(outer, names[2], names[3])
    name_f = jnp.where(outer, names[3], names[2])
    meta = jnp.concatenate([place, names[0], names[1], name_m, name_f])
    sums = shrink_sums(meta, [[after([j_third], hidden)], [mid], [partner], [far]], [0, 2, 1, 3], shrink_mine, shrink_other, held)
    r_sums = exchange(sums)
    low, swapped = low_sums(r_sums)
    low = add(low, send(swapped, MIDDLE))
    low_out = send(low, OUTWARD)

    rest = [(a, 0, b, 0) for a, b in zip(v_own, v_other)] + weights[:3]
    j_fifth = products(
        place,
        [
            Rows([(after([sums], far), NEAR // TILE, 2, 0)], 1, 0),
            Rows([(out_far, 0, 2, 1), (out_far, 2, 2, 2), (out_far, 4, 1, 3)], 0, 0),
        ],
        rest,
        BLOCK,
    )
    r_fifth = exchange(j_fifth)

    def term(inner_slot, outer_slot):
        return (low, low_out, r_sums, (inner_slot, outer_slot))

    x_partner = finish(meta, None, r_partner, 0, term(1, 1))
    home_partner = send(x_partner, XOR[1])
    x_two = finish(meta, None, r_third, 0, term(3, 2))
    home_two = send(x_two, XOR[2])
    x_mid = finish(meta, 1, r_mid, 0, term(2, 2))
    home_mid = send(x_mid, MIDDLE)
    x_own = finish(meta, None, r_own, 0, term(0, 0))
    r_fifth = after([x_partner, x_two, x_mid, x_own], r_fifth)
    x_far = finish(meta, 0, r_fifth, 0, term(3, 3))
    to_far = send(x_far, INWARD)
    to_far = after([home_partner, home_two, home_mid], to_far)
    home_far = send(finish(meta, 1, r_fifth, 0, more=to_far), ACROSS)
    count = lax.dynamic_slice_in_dim(block_rows, t, 1, 0)
    return assemble(meta, count, x_own, home_partner, home_two, home_mid, home_far)


def solution(mesh):
    in_specs = (
        P("pool", "tensor"),
        P("tensor", "pool"),
        P("pool", "tensor", None),
        P("pool", "tensor", None),
        P("pool"),
        P("pool"),
    )
    out_specs = P(("pool", "tensor"), None)
    body = line_of_four if dict(mesh.shape) == {"pool": 8, "tensor": 4} else general
    return jax.shard_map(body, mesh=mesh, in_specs=in_specs, out_specs=out_specs, check_vma=False)
```
